32 devices in a mesh: row: 8 (over z, x), col: 4 (over y, core).
Axes of the slice: x: 2, y: 2, z: 4, core: 2. Of those that a mesh axis runs over, the one named last changes fastest.
Arguments:
- ensemble: float32 [4096, 1024], P(('row', 'col')), may hold values from -6 to 6
- obs_blocks: int32 [2, 256], replicated, may hold values from 0 to 1023
- obs_weights: float32 [2, 256, 4], replicated, may hold values from 0.1 to 1
- comp_tags: int32 [2, 256], replicated, may hold values from 0 to 1
- obs_values: float32 [2, 256], replicated, may hold values from -6 to 6
- obs_noise: bfloat16 [2, 256, 1024], replicated, may hold values from -6 to 6
Outputs:
- analysis: float32 [4096, 1024], P(('row', 'col'))
The draws below stay inside these ranges and needn't reach their ends.
Inputs may be any that keep to these rules, and one draw needn't show every extreme that they name: Observation o reads state rows 4 * obs_blocks[b, o] to 4 * obs_blocks[b, o] + 3. `comp_tags`: 0 marks an atmosphere observation, 1 an ocean one.
All inputs are finite; a program needn't handle non-finite values.
Results may differ from the reference program's by a relative error of at most 0.0035.
Values may be sent and summed in bfloat16 or wider, within the bound.
No kernel may reach another device: no remote copies, remote signals or barrier semaphores. Data moves between devices by JAX's collectives and lax.ppermute only.
A program may use at most 64 MiB of HBM per device.

```python
import jax
import jax.numpy as jnp
from jax import lax

M = 1024
B = 256
K = 4
NB = 2
NROWS = 4096
NBLK = 1024


def set_ends(values, rng, smallest, top_value):
    longest = values.shape.index(max(values.shape))
    spots = []
    for shift in (0, 1):
        where = [jax.random.randint(jax.random.fold_in(rng, axis), (), 0, length) for axis, length in enumerate(values.shape)]
        where[longest] = (where[longest] + shift) % values.shape[longest]
        spots.append(tuple(where))
    return values.at[spots[0]].set(smallest).at[spots[1]].set(top_value)


def block_scale(rng, shape, split, low, high):
    factor_of, own = 1.0, jax.random.fold_in(rng, 6)
    for position, blocks in split:
        draws = jnp.exp(jax.random.uniform(jax.random.fold_in(own, position), (blocks,), jnp.float32, low / len(split), high / len(split)))
        factor_of = factor_of * jnp.repeat(draws, shape[position] // blocks).reshape([-1 if axis == position else 1 for axis in range(len(shape))])
    return factor_of


def gaussian(own_key, extent, deviation, most, pieces=(), kind=jnp.bfloat16):
    values = deviation * jax.random.normal(own_key, extent, jnp.float32)
    if pieces:
        values = values * block_scale(own_key, extent, pieces, -0.22, 0.18)
    return jnp.clip(values, -most, most).astype(kind)


def setup_inputs(seed: int = 0) -> dict:
    arg_keys = jax.random.split(jax.random.key(seed), 7)
    ensemble = gaussian(arg_keys[0], (NROWS, M), 1.0, 6.0, ((0, 32),), jnp.float32)
    obs_blocks = set_ends(jax.random.randint(arg_keys[1], (NB, B), 0, NBLK), jax.random.fold_in(arg_keys[1], 1), 0, NBLK - 1).astype(jnp.int32)
    obs_weights = jnp.clip(jax.random.uniform(arg_keys[2], (NB, B, K), jnp.float32, 0.1, 1.0), 0.1, 1.0)
    comp_tags = set_ends(jax.random.randint(arg_keys[3], (NB, B), 0, 2), jax.random.fold_in(arg_keys[3], 1), 0, 1).astype(jnp.int32)
    obs_values = gaussian(arg_keys[4], (NB, B), 1.0, 6.0, (), jnp.float32)
    obs_noise = gaussian(arg_keys[5], (NB, B, M), 1.0, 6.0)
    return dict(ensemble=ensemble, obs_blocks=obs_blocks, obs_weights=obs_weights, comp_tags=comp_tags, obs_values=obs_values, obs_noise=obs_noise)


def reference(ensemble, obs_blocks, obs_weights, comp_tags, obs_values, obs_noise):
    ensemble_state = ensemble
    highest = lax.Precision.HIGHEST
    for batch_index in range(NB):
        row_ids = obs_blocks[batch_index][:, None] * K + jnp.arange(K, dtype=jnp.int32)[None, :]
        picked = ensemble_state[row_ids.reshape(-1)].reshape(B, K, M)
        observed = lax.optimization_barrier(jnp.sum(obs_weights[batch_index][:, :, None] * picked, axis=1))
        observed = lax.optimization_barrier(observed.astype(jnp.bfloat16)).astype(jnp.float32)
        anomalies = observed - lax.optimization_barrier(jnp.mean(observed, axis=1, keepdims=True))
        variance = jnp.where(comp_tags[batch_index] == 0, jnp.float32(0.5), jnp.float32(2.0))
        covariance = jnp.dot(anomalies, anomalies.T, precision=highest) / (M - 1) + jnp.diag(variance)
        factor_lower = jnp.linalg.cholesky(covariance)
        innovation = obs_values[batch_index][:, None] + jnp.sqrt(variance)[:, None] * obs_noise[batch_index].astype(jnp.float32) - observed
        whitened = jax.scipy.linalg.solve_triangular(factor_lower, anomalies, lower=True).astype(jnp.bfloat16)
        white_innov = jax.scipy.linalg.solve_triangular(factor_lower, innovation, lower=True).astype(jnp.bfloat16)
        state_anom = ensemble_state - lax.optimization_barrier(jnp.mean(ensemble_state, axis=1, keepdims=True))
        projected = jnp.dot(state_anom, whitened.astype(jnp.float32).T, precision=highest)
        ensemble_state = ensemble_state + jnp.dot(projected, white_innov.astype(jnp.float32), precision=highest) / (M - 1)
    return ensemble_state
```

```python
import functools

import jax
import jax.numpy as jnp
from jax import lax
from jax.experimental import pallas as pl
from jax.experimental.pallas import tpu as pltpu
from jax.sharding import PartitionSpec as P

SLOTS = 32
SCALE = 0.5
TOLERANCE = 2e-3
BF16 = jnp.bfloat16
F32 = jnp.float32
VMEM = pl.BlockSpec(memory_space=pltpu.VMEM)
SMEM = pl.BlockSpec(memory_space=pltpu.SMEM)
PARAMS = pltpu.CompilerParams(vmem_limit_bytes=40 * 1024 * 1024)


def nt(a, b):
    return lax.dot_general(a, b, (((1,), (1,)), ((), ())), preferred_element_type=F32)


def nn(a, b):
    return lax.dot_general(a, b, (((1,), (0,)), ((), ())), preferred_element_type=F32)


def split(a):
    high = a.astype(BF16)
    return high, (a - high.astype(F32)).astype(BF16)


def dot3(dot, a, b):
    (ah, al), (bh, bl) = a, b
    return dot(ah, bh) + (dot(ah, bl) + dot(al, bh))


def row_mean(a):
    return jnp.sum(a, axis=1, keepdims=True) * (1.0 / a.shape[1])


def column(row):
    size = row.shape[1]
    lane = lax.broadcasted_iota(jnp.int32, (size, size), 1)
    sub = lax.broadcasted_iota(jnp.int32, (size, size), 0)
    return jnp.sum(jnp.where(lane == sub, row, jnp.zeros_like(row)), axis=1, keepdims=True)


def both_ways(row):
    as_float = row.astype(F32)
    return as_float, column(as_float)


def split_rows(first, second):
    high = second.astype(BF16)
    return first.astype(BF16), high, (second - high.astype(F32)).astype(BF16)


def pick_kernel(place, blocks, weights, state, keep0, send0, keep1, send1):
    device = place[0]
    batches, points, size = weights.shape
    width, members = state.shape
    held = width // points
    lane = lax.broadcasted_iota(jnp.int32, (size, size), 1)
    sub = lax.broadcasted_iota(jnp.int32, (size, size), 0)
    slots = lax.broadcasted_iota(jnp.int32, (SLOTS, size), 0)
    lanes = lax.broadcasted_iota(jnp.int32, (SLOTS, width), 1)
    selectors = []
    for batch in range(batches):
        row = blocks[batch : batch + 1, :]
        pair_row, pair_column = both_ways(row // (2 * held))
        before = jnp.where((pair_row == pair_column) & (sub < lane), 1.0, 0.0)
        rank = jnp.sum(before, axis=0, keepdims=True).astype(jnp.int32)
        slot = jnp.where(row // held == device, rank, -1)
        chosen = jnp.where(slots == slot, 1.0, 0.0)
        local = jnp.sum(chosen * (row - device * held).astype(F32), axis=1, keepdims=True)
        weight = lax.dot_general(
            chosen,
            weights[batch],
            (((1,), (1,)), ((), ())),
            precision=lax.Precision.HIGHEST,
            preferred_element_type=F32,
        )
        value = jnp.zeros((SLOTS, width), F32)
        for point in range(points):
            value = jnp.where(lanes % points == point, weight[:, point : point + 1], value)
        selectors.append(jnp.where((lanes // points).astype(F32) == local, value, 0.0))
    rows = jnp.dot(
        jnp.concatenate(selectors, axis=0),
        state[...],
        precision=lax.Precision.HIGHEST,
        preferred_element_type=F32,
    )
    left, right = rows[:, : members // 2], rows[:, members // 2 :]
    first = device % 2 == 0
    for half, out0, out1 in (
        (jnp.where(first, left, right), keep0, keep1),
        (jnp.where(first, right, left), send0, send1),
    ):
        out0[...], out1[:SLOTS, :], out1[SLOTS:, :] = split_rows(half[:SLOTS], half[SLOTS:])


def pick(place, blocks, weights, state):
    half = state.shape[1] // 2
    outs = [jax.ShapeDtypeStruct((rows, half), BF16) for rows in (SLOTS, SLOTS, 2 * SLOTS, 2 * SLOTS)]
    return pl.pallas_call(
        pick_kernel,
        out_shape=outs,
        in_specs=[SMEM, VMEM, VMEM, VMEM],
        out_specs=[VMEM] * 4,
        compiler_params=PARAMS,
        name="pick",
    )(place, blocks, weights, state)


def pick_all_kernel(place, blocks, weights, state, out):
    device = place[0]
    batches, points, size = weights.shape
    width = state.shape[0]
    lanes = lax.broadcasted_iota(jnp.int32, (size, width), 1)
    rows = []
    for batch in range(batches):
        value = jnp.zeros((size, width), F32)
        for point in range(points):
            weight = column(weights[batch, point : point + 1, :])
            value = jnp.where(lanes % points == point, weight, value)
        row = blocks[batch : batch + 1, :]
        local = column((row - device * (width // points)).astype(F32))
        selector = jnp.where((lanes // points).astype(F32) == local, value, 0.0)
        rows.append(
            jnp.dot(
                selector, state[...], precision=lax.Precision.HIGHEST, preferred_element_type=F32
            )
        )
    out[:size, :], out[size : 2 * size, :], out[2 * size :, :] = split_rows(*rows)


def pick_all(place, blocks, weights, state):
    return pl.pallas_call(
        pick_all_kernel,
        out_shape=jax.ShapeDtypeStruct((3 * blocks.shape[1], state.shape[1]), BF16),
        in_specs=[SMEM, VMEM, VMEM, VMEM],
        out_specs=VMEM,
        compiler_params=PARAMS,
        name="pick_all",
    )(place, blocks, weights, state)


def in_order(device, row, held, parts, refs):
    size = row.shape[1]
    pair_row, pair_column = both_ways(row // (2 * held))
    lane = lax.broadcasted_iota(jnp.int32, (size, size), 1)
    sub = lax.broadcasted_iota(jnp.int32, (size, size), 0)
    before = jnp.where((pair_row == pair_column) & (lane < sub), 1.0, 0.0)
    rank = jnp.sum(before, axis=1, keepdims=True).astype(jnp.int32)
    away = (2 * pair_column.astype(jnp.int32)) ^ device
    far, near = (away >> 4) & 1, (away >> 3) & 1
    x, y = (away >> 2) & 1, (away >> 1) & 1
    block = jnp.where(near == 0, 4 * x + 2 * y + far, 4 * y + 2 * x + far)
    halves = []
    for group in (refs[:2], refs[2:]):
        total = jnp.zeros((size, group[0].shape[-1]), F32)
        for index, ref in enumerate(group):
            values = ref[...].reshape(-1, ref.shape[-1])
            slots = lax.broadcasted_iota(jnp.int32, (size, values.shape[0]), 1)
            chosen = jnp.zeros((size, values.shape[0]), F32)
            for part in range(parts):
                slot = (block * parts + part) * SLOTS + rank
                chosen = chosen + jnp.where((slots == slot) & (near == index), 1.0, 0.0)
            total = total + nn(chosen.astype(BF16), values)
        halves.append(total)
    first = device % 2 == 0
    return jnp.concatenate(
        [jnp.where(first, halves[0], halves[1]), jnp.where(first, halves[1], halves[0])], axis=1
    )


def eliminate(covariance, work, inverse):
    size = covariance.shape[0]
    lane = lax.broadcasted_iota(jnp.int32, (size, size), 1)
    sub = lax.broadcasted_iota(jnp.int32, (size, size), 0)
    work[...] = covariance
    inverse[...] = jnp.where(lane == sub, 1.0, 0.0)

    def step(k, carry):
        row = work[pl.ds(k, 1), :]
        current = work[...]
        pivot = jnp.sum(jnp.where(lane[:1] == k, row, 0.0), axis=1, keepdims=True)
        column = jnp.sum(jnp.where(lane == k, current, 0.0), axis=1, keepdims=True)
        factor = jnp.where(sub[:, :1] > k, column / pivot, 0.0)
        inverse_row = inverse[pl.ds(k, 1), :]
        work[...] = current - factor * row
        inverse[...] = inverse[...] - factor * inverse_row
        return carry

    lax.fori_loop(0, size, step, 0)
    pivots = jnp.sum(jnp.where(lane == sub, work[...], 0.0), axis=1, keepdims=True)
    inverse[...] = inverse[...] * (1.0 / jnp.sqrt(pivots))


def inverse_factor(covariance, work, inverse):
    size = covariance.shape[0]
    lane = lax.broadcasted_iota(jnp.int32, (size, size), 1)
    sub = lax.broadcasted_iota(jnp.int32, (size, size), 0)
    diagonal = lane == sub
    eye = jnp.where(diagonal, 1.0, 0.0)
    half = jnp.where(lane < sub, 1.0, jnp.where(diagonal, 0.5, 0.0))
    on_diagonal = jnp.where(diagonal, covariance, 0.0)
    scale_row = lax.rsqrt(jnp.sum(on_diagonal, axis=0, keepdims=True) * (1.0 / SCALE))
    scale_column = lax.rsqrt(jnp.sum(on_diagonal, axis=1, keepdims=True) * (1.0 / SCALE))
    scaled = covariance * scale_row * scale_column

    def third_order(m):
        low = (m - eye) * half
        lowb = low.astype(BF16)
        return (nn(lowb, lowb) + half * nt(lowb, lowb)) - low

    m = scaled
    t = None
    for step in range(3):
        u = third_order(m) + eye
        ub = u.astype(BF16)
        t = u if t is None else nn(ub, t.astype(BF16))
        if step < 2:
            m = nt(nn(ub, m.astype(BF16)).astype(BF16), ub)
    parts = split(scaled)
    ts = split(t)
    m = dot3(nt, split(dot3(nn, ts, parts)), ts)
    t = t + nn(third_order(m).astype(BF16), ts[0])
    ts = split(t)
    m = dot3(nt, split(dot3(nn, ts, parts)), ts)
    error = m - eye
    t = t - nn((error * half).astype(BF16), ts[0])
    inverse[...] = t * scale_row
    good = jnp.min(jnp.where(jnp.abs(error) <= TOLERANCE, 1.0, 0.0))

    @pl.when(good < 0.5)
    def _():
        eliminate(covariance, work, inverse)


def whiten(observed, tags, values, noise, work, inverse):
    members = observed.shape[1]
    size = observed.shape[0]
    anomalies = observed - row_mean(observed)
    ah, al = split(anomalies)
    lane = lax.broadcasted_iota(jnp.int32, (size, size), 1)
    sub = lax.broadcasted_iota(jnp.int32, (size, size), 0)
    variance = column(jnp.where(tags == 0, 0.5, 2.0))
    values = column(values)
    covariance = dot3(nt, (ah, al), (ah, al)) * (1.0 / (members - 1))
    covariance = covariance + jnp.where(lane == sub, variance, 0.0)
    inverse_factor(covariance, work, inverse)
    ts = split(inverse[...])
    innovation = values + jnp.sqrt(variance) * noise.astype(F32) - observed
    whitened = dot3(nn, ts, (ah, al)).astype(BF16)
    white_innov = dot3(nn, ts, split(innovation)).astype(BF16)
    return whitened, white_innov


def update(state, whitened, white_innov):
    members = state.shape[1]
    sh, sl = split(state - row_mean(state))
    ph, plow = split(nt(sh, whitened) + nt(sl, whitened))
    return state + (nn(ph, white_innov) + nn(plow, white_innov)) * (1.0 / (members - 1))


def first_kernel(direct, place, blocks, tags, values, noise, *rest):
    arrived, (whitened, white_innov, work, inverse) = rest[:-4], rest[-4:]
    if direct:
        held = place[1]
        observed = in_order(place[0], blocks[:1, :], held, 1, arrived)
    else:
        observed = arrived[0][...].astype(F32)
    w, v = whiten(observed, tags[:1, :], values[:1, :], noise[0], work, inverse)
    whitened[...] = w
    white_innov[...] = v


def second_kernel(direct, place, blocks, tags, values, noise, state, whitened, white_innov, *rest):
    arrived, (analysis, work, inverse) = rest[:-3], rest[-3:]
    if direct:
        held = place[1]
        prior = in_order(place[0], blocks[1:2, :], held, 2, arrived)
    else:
        prior = arrived[0][...].astype(F32) + arrived[1][...].astype(F32)
    w, v = whitened[...], white_innov[...]
    observed = update(prior, w, v).astype(BF16).astype(F32)
    first = update(state[...], w, v)
    w, v = whiten(observed, tags[1:2, :], values[1:2, :], noise[0], work, inverse)
    analysis[...] = update(first, w, v)


def whole(array):
    return pl.BlockSpec(array.shape, lambda i, n=len(array.shape): (0,) * n)


def batch_call(kernel, name, batch, outs, place, blocks, tags, values, noise, *arrays):
    rows, members = noise.shape[1:]
    return pl.pallas_call(
        kernel,
        grid=(1,),
        out_shape=outs,
        in_specs=[SMEM, whole(blocks), whole(tags), whole(values)]
        + [pl.BlockSpec((1, rows, members), lambda i: (batch, 0, 0))]
        + [whole(array) for array in arrays],
        out_specs=[whole(out) for out in outs],
        scratch_shapes=[pltpu.VMEM((rows, rows), F32), pltpu.VMEM((rows, rows), F32)],
        compiler_params=PARAMS,
        name=name,
    )(place, blocks, tags, values, noise, *arrays)


def batches(direct, place, blocks, tags, values, noise, state, arrived0, arrived1):
    shape = jax.ShapeDtypeStruct(noise.shape[1:], BF16)
    whitened, white_innov = batch_call(
        functools.partial(first_kernel, direct),
        "first_batch",
        0,
        [shape, shape],
        place,
        blocks,
        tags,
        values,
        noise,
        *arrived0,
    )
    return batch_call(
        functools.partial(second_kernel, direct),
        "second_batch",
        1,
        [jax.ShapeDtypeStruct(state.shape, F32)],
        place,
        blocks,
        tags,
        values,
        noise,
        state,
        whitened,
        white_innov,
        *arrived1,
    )[0]


AXES = ("row", "col")
CORE, Y, X, NEAR_Z, FAR_Z = 1, 2, 4, 8, 16


def swap(value, mask):
    return lax.ppermute(value, AXES, [(i, i ^ mask) for i in range(32)])


def joined(value, mask):
    return jnp.concatenate([value, swap(value, mask)], axis=0)


def gather(keep, send):
    block = (keep + swap(send, CORE))[None]
    along_z = joined(joined(block, FAR_Z), NEAR_Z)
    first = joined(joined(along_z[:2], Y), X)
    second = joined(joined(along_z[2:], X), Y)
    return first, second, swap(first, CORE), swap(second, CORE)


def by_slots(place, ensemble, blocks, weights, tags, values, noise):
    keep0, send0, keep1, send1 = pick(place, blocks, weights, ensemble)
    arrived0, arrived1 = gather(keep0, send0), gather(keep1, send1)
    return batches(True, place, blocks, tags, values, noise, ensemble, arrived0, arrived1)


def by_sum(add_up, place, ensemble, blocks, weights, tags, values, noise):
    rows = blocks.shape[1]
    picked = add_up(pick_all(place, blocks, weights, ensemble))
    arrived0, arrived1 = picked[:rows], (picked[rows : 2 * rows], picked[2 * rows :])
    return batches(False, place, blocks, tags, values, noise, ensemble, (arrived0,), arrived1)


def add_by_swaps(value):
    for mask in (CORE, Y, X, NEAR_Z, FAR_Z):
        value = value + swap(value, mask)
    return value


def add_by_psum(value):
    return lax.psum(value, AXES)


def body(staged, ensemble, obs_blocks, obs_weights, comp_tags, obs_values, obs_noise):
    held = ensemble.shape[0] // obs_weights.shape[2]
    place = jnp.stack([lax.axis_index(AXES), held]).astype(jnp.int32)
    by_point = jnp.swapaxes(obs_weights, 1, 2)
    operands = (place, ensemble, obs_blocks, by_point, comp_tags, obs_values, obs_noise)
    if not staged:
        return by_sum(add_by_psum, *operands)
    pair = obs_blocks // (2 * held)
    counts = jnp.sum(
        (pair[:, :, None] == jnp.arange(16, dtype=jnp.int32)).astype(jnp.int32), axis=1
    )
    fits = jnp.max(counts) <= SLOTS
    return lax.cond(fits, by_slots, functools.partial(by_sum, add_by_swaps), *operands)


def solution(mesh):
    staged = (mesh.shape["row"], mesh.shape["col"]) == (8, 4)
    in_specs = (P(AXES, None), P(), P(), P(), P(), P())
    out_specs = P(AXES, None)
    return jax.shard_map(
        functools.partial(body, staged),
        mesh=mesh,
        in_specs=in_specs,
        out_specs=out_specs,
        check_vma=False,
    )
```

```python
import functools

import jax
import jax.numpy as jnp
from jax import lax
from jax.experimental import pallas as pl
from jax.experimental.pallas import tpu as pltpu
from jax.sharding import PartitionSpec as P

SLOTS = 64
UNIT = 1.0 / 1024
SCALE = 0.5
TOLERANCE = 2e-3
BF16 = jnp.bfloat16
F32 = jnp.float32
VMEM = pl.BlockSpec(memory_space=pltpu.VMEM)
SMEM = pl.BlockSpec(memory_space=pltpu.SMEM)
PARAMS = pltpu.CompilerParams(vmem_limit_bytes=40 * 1024 * 1024)


def nt(a, b):
    return lax.dot_general(a, b, (((1,), (1,)), ((), ())), preferred_element_type=F32)


def nn(a, b):
    return lax.dot_general(a, b, (((1,), (0,)), ((), ())), preferred_element_type=F32)


def split(a):
    high = a.astype(BF16)
    return high, (a - high.astype(F32)).astype(BF16)


def dot3(dot, a, b):
    (ah, al), (bh, bl) = a, b
    return dot(ah, bh) + (dot(ah, bl) + dot(al, bh))


def row_mean(a):
    return jnp.sum(a, axis=1, keepdims=True) * (1.0 / a.shape[1])


def column(row):
    size = row.shape[1]
    lane = lax.broadcasted_iota(jnp.int32, (size, size), 1)
    sub = lax.broadcasted_iota(jnp.int32, (size, size), 0)
    return jnp.sum(jnp.where(lane == sub, row, jnp.zeros_like(row)), axis=1, keepdims=True)


def both_ways(row):
    as_float = row.astype(F32)
    return as_float, column(as_float)


def select(lanes, points, local, weight):
    value = jnp.zeros(lanes.shape, F32)
    for point in range(points):
        value = jnp.where(lanes % points == point, weight[point], value)
    return jnp.where((lanes // points).astype(F32) == local, value, 0.0)


def rounded(value):
    return value.astype(BF16).astype(F32)


def pick_kernel(place, blocks, weights, state, keep, send):
    device = place[0]
    batches, points, size = weights.shape
    width, members = state.shape
    held = width // points
    lane = lax.broadcasted_iota(jnp.int32, (size, size), 1)
    sub = lax.broadcasted_iota(jnp.int32, (size, size), 0)
    slots = lax.broadcasted_iota(jnp.int32, (SLOTS, size), 0)
    lanes = lax.broadcasted_iota(jnp.int32, (SLOTS, width), 1)
    selectors, taken = [], []
    for batch in range(batches):
        row = blocks[batch : batch + 1, :]
        pair_row, pair_column = both_ways(row // (2 * held))
        before = jnp.where((pair_row == pair_column) & (sub < lane), 1.0, 0.0)
        rank = jnp.sum(before, axis=0, keepdims=True).astype(jnp.int32)
        slot = jnp.where(row // held == device, rank if batch == 0 else SLOTS - 1 - rank, -1)
        chosen = jnp.where(slots == slot, 1.0, 0.0)
        local = jnp.sum(chosen * (row - device * held).astype(F32), axis=1, keepdims=True)
        weight = lax.dot_general(
            chosen,
            weights[batch],
            (((1,), (1,)), ((), ())),
            precision=lax.Precision.HIGHEST,
            preferred_element_type=F32,
        )
        columns = [weight[:, point : point + 1] for point in range(points)]
        selectors.append(select(lanes, points, local, columns))
        taken.append(jnp.sum(chosen, axis=1, keepdims=True))
    rows = jnp.dot(
        selectors[0] + selectors[1],
        state[...],
        precision=lax.Precision.HIGHEST,
        preferred_element_type=F32,
    )
    rows = jnp.where(taken[0] > 0.5, rounded(rows), rows)
    code = jnp.round(rows * (1.0 / UNIT)).astype(jnp.int32)
    left, right = code[:, : members // 2], code[:, members // 2 :]
    first = device % 2 == 0
    keep[...] = jnp.where(first, left, right).astype(jnp.int16)
    send[...] = jnp.where(first, right, left).astype(jnp.int16)


def pick(place, blocks, weights, state):
    return pl.pallas_call(
        pick_kernel,
        out_shape=[jax.ShapeDtypeStruct((SLOTS, state.shape[1] // 2), jnp.int16)] * 2,
        in_specs=[SMEM, VMEM, VMEM, VMEM],
        out_specs=[VMEM] * 2,
        compiler_params=PARAMS,
        name="pick",
    )(place, blocks, weights, state)


def pick_all_kernel(place, blocks, weights, state, out):
    device = place[0]
    batches, points, size = weights.shape
    width = state.shape[0]
    lanes = lax.broadcasted_iota(jnp.int32, (size, width), 1)
    for batch in range(batches):
        columns = [column(weights[batch, point : point + 1, :]) for point in range(points)]
        local = column((blocks[batch : batch + 1, :] - device * (width // points)).astype(F32))
        rows = jnp.dot(
            select(lanes, points, local, columns),
            state[...],
            precision=lax.Precision.HIGHEST,
            preferred_element_type=F32,
        )
        rows = rounded(rows) if batch == 0 else rows
        out[batch * size : (batch + 1) * size, :] = jnp.round(rows * (1.0 / UNIT))


def pick_all(place, blocks, weights, state):
    return pl.pallas_call(
        pick_all_kernel,
        out_shape=jax.ShapeDtypeStruct((blocks.size, state.shape[1]), F32),
        in_specs=[SMEM, VMEM, VMEM, VMEM],
        out_specs=VMEM,
        compiler_params=PARAMS,
        name="pick_all",
    )(place, blocks, weights, state)


def put_in_order(place, blocks, members, pieces):
    device, held = place[0], place[1]
    size = blocks.shape[1]
    lane = lax.broadcasted_iota(jnp.int32, (size, size), 1)
    sub = lax.broadcasted_iota(jnp.int32, (size, size), 0)
    values = jnp.concatenate([ref[...].reshape(2 * SLOTS, -1) for _, ref in pieces], axis=0)
    values = values.astype(jnp.int32)
    high, low = values >> 8, values & 255
    high, low = high.astype(F32).astype(BF16), low.astype(F32).astype(BF16)
    slots = lax.broadcasted_iota(jnp.int32, (size, values.shape[0]), 1)
    results = []
    for batch in range(blocks.shape[0]):
        pair_row, pair_column = both_ways(blocks[batch : batch + 1, :] // (2 * held))
        before = jnp.where((pair_row == pair_column) & (lane < sub), 1.0, 0.0)
        rank = jnp.sum(before, axis=1, keepdims=True).astype(jnp.int32)
        away = (2 * pair_column.astype(jnp.int32)) ^ device
        near_x_y = (away >> 1) & 7
        where = jnp.full(rank.shape, -2 * SLOTS, jnp.int32)
        for index, (distance, _) in enumerate(pieces):
            where = jnp.where(near_x_y == distance, 2 * SLOTS * index, where)
        slot = where + SLOTS * ((away >> 4) & 1) + (rank if batch == 0 else SLOTS - 1 - rank)
        chosen = jnp.where(slots == slot, 1.0, 0.0).astype(BF16)
        results.append(256.0 * nn(chosen, high) + nn(chosen, low))
    return results


def early_kernel(distances, place, blocks, *refs):
    results = put_in_order(place, blocks, refs[0].shape[-1], list(zip(distances, refs[:-1])))
    size = blocks.shape[1]
    for batch, result in enumerate(results):
        refs[-1][batch * size : (batch + 1) * size, :] = result


def late_kernel(distances, place, blocks, early, *refs):
    results = put_in_order(place, blocks, refs[0].shape[-1], list(zip(distances, refs[:-2])))
    size = blocks.shape[1]
    refs[-2][...] = ((results[0] + early[:size, :]) * UNIT).astype(BF16)
    refs[-1][...] = (results[1] + early[size:, :]).astype(jnp.int32).astype(jnp.int16)


def early_rows(place, blocks, pieces):
    distances = [distance for distance, _ in pieces]
    half = pieces[0][1].shape[-1]
    return pl.pallas_call(
        functools.partial(early_kernel, distances),
        out_shape=jax.ShapeDtypeStruct((blocks.size, half), F32),
        in_specs=[SMEM] + [VMEM] * (1 + len(pieces)),
        out_specs=VMEM,
        compiler_params=PARAMS,
        cost_estimate=pl.CostEstimate(flops=10**9, bytes_accessed=4 * 10**6, transcendentals=0),
        name="early_rows",
    )(place, blocks, *[piece for _, piece in pieces])


def late_rows(place, blocks, early, pieces):
    distances = [distance for distance, _ in pieces]
    rows, half = blocks.shape[1], early.shape[1]
    return pl.pallas_call(
        functools.partial(late_kernel, distances),
        out_shape=[
            jax.ShapeDtypeStruct((rows, half), BF16),
            jax.ShapeDtypeStruct((rows, half), jnp.int16),
        ],
        in_specs=[SMEM] + [VMEM] * (2 + len(pieces)),
        out_specs=[VMEM] * 2,
        compiler_params=PARAMS,
        name="late_rows",
    )(place, blocks, early, *[piece for _, piece in pieces])


def eliminate(covariance, work, inverse):
    size = covariance.shape[0]
    lane = lax.broadcasted_iota(jnp.int32, (size, size), 1)
    sub = lax.broadcasted_iota(jnp.int32, (size, size), 0)
    work[...] = covariance
    inverse[...] = jnp.where(lane == sub, 1.0, 0.0)

    def step(k, carry):
        row = work[pl.ds(k, 1), :]
        current = work[...]
        pivot = jnp.sum(jnp.where(lane[:1] == k, row, 0.0), axis=1, keepdims=True)
        column = jnp.sum(jnp.where(lane == k, current, 0.0), axis=1, keepdims=True)
        factor = jnp.where(sub[:, :1] > k, column / pivot, 0.0)
        inverse_row = inverse[pl.ds(k, 1), :]
        work[...] = current - factor * row
        inverse[...] = inverse[...] - factor * inverse_row
        return carry

    lax.fori_loop(0, size, step, 0)
    pivots = jnp.sum(jnp.where(lane == sub, work[...], 0.0), axis=1, keepdims=True)
    inverse[...] = inverse[...] * (1.0 / jnp.sqrt(pivots))


def inverse_factor(covariance, work, inverse):
    size = covariance.shape[0]
    lane = lax.broadcasted_iota(jnp.int32, (size, size), 1)
    sub = lax.broadcasted_iota(jnp.int32, (size, size), 0)
    diagonal = lane == sub
    eye = jnp.where(diagonal, 1.0, 0.0)
    half = jnp.where(lane < sub, 1.0, jnp.where(diagonal, 0.5, 0.0))
    on_diagonal = jnp.where(diagonal, covariance, 0.0)
    scale_row = lax.rsqrt(jnp.sum(on_diagonal, axis=0, keepdims=True) * (1.0 / SCALE))
    scale_column = lax.rsqrt(jnp.sum(on_diagonal, axis=1, keepdims=True) * (1.0 / SCALE))
    scaled = covariance * scale_row * scale_column

    def third_order(m):
        low = (m - eye) * half
        lowb = low.astype(BF16)
        return (nn(lowb, lowb) + half * nt(lowb, lowb)) - low

    m = scaled
    t = None
    for step in range(3):
        u = third_order(m) + eye
        ub = u.astype(BF16)
        t = u if t is None else nn(ub, t.astype(BF16))
        if step < 2:
            m = nt(nn(ub, m.astype(BF16)).astype(BF16), ub)
    parts = split(scaled)
    ts = split(t)
    m = dot3(nt, split(dot3(nn, ts, parts)), ts)
    t = t + nn(third_order(m).astype(BF16), ts[0])
    ts = split(t)
    m = dot3(nt, split(dot3(nn, ts, parts)), ts)
    error = m - eye
    t = t - nn((error * half).astype(BF16), ts[0])
    inverse[...] = t * scale_row
    good = jnp.min(jnp.where(jnp.abs(error) <= TOLERANCE, 1.0, 0.0))

    @pl.when(good < 0.5)
    def _():
        eliminate(covariance, work, inverse)


def whiten(observed, tags, values, noise, work, inverse):
    members = observed.shape[1]
    size = observed.shape[0]
    anomalies = observed - row_mean(observed)
    ah, al = split(anomalies)
    lane = lax.broadcasted_iota(jnp.int32, (size, size), 1)
    sub = lax.broadcasted_iota(jnp.int32, (size, size), 0)
    variance = column(jnp.where(tags == 0, 0.5, 2.0))
    values = column(values)
    covariance = dot3(nt, (ah, al), (ah, al)) * (1.0 / (members - 1))
    covariance = covariance + jnp.where(lane == sub, variance, 0.0)
    inverse_factor(covariance, work, inverse)
    ts = split(inverse[...])
    innovation = values + jnp.sqrt(variance) * noise.astype(F32) - observed
    whitened = dot3(nn, ts, (ah, al)).astype(BF16)
    white_innov = dot3(nn, ts, split(innovation)).astype(BF16)
    return whitened, white_innov


def update(state, whitened, white_innov):
    members = state.shape[1]
    sh, sl = split(state - row_mean(state))
    ph, plow = split(nt(sh, whitened) + nt(sl, whitened))
    return state + (nn(ph, white_innov) + nn(plow, white_innov)) * (1.0 / (members - 1))


def both_halves(place, own, other):
    own, other = own[...].astype(F32), other[...].astype(F32)
    first = place[0] % 2 == 0
    return jnp.concatenate(
        [jnp.where(first, own, other), jnp.where(first, other, own)], axis=1
    )


def first_kernel(place, tags, values, noise, own, other, whitened, white_innov, work, inverse):
    observed = both_halves(place, own, other)
    w, v = whiten(observed, tags[:1, :], values[:1, :], noise[0], work, inverse)
    whitened[...] = w
    white_innov[...] = v


def second_kernel(
    place, tags, values, noise, own, other, state, whitened, white_innov, analysis, work, inverse
):
    prior = both_halves(place, own, other) * UNIT
    w, v = whitened[...], white_innov[...]
    observed = rounded(update(prior, w, v))
    first = update(state[...], w, v)
    w, v = whiten(observed, tags[1:2, :], values[1:2, :], noise[0], work, inverse)
    analysis[...] = update(first, w, v)


def whole(array):
    return pl.BlockSpec(array.shape, lambda i, n=len(array.shape): (0,) * n)


def batch_call(kernel, name, batch, outs, place, tags, values, noise, *arrays):
    rows, members = noise.shape[1:]
    return pl.pallas_call(
        kernel,
        grid=(1,),
        out_shape=outs,
        in_specs=[SMEM, whole(tags), whole(values)]
        + [pl.BlockSpec((1, rows, members), lambda i: (batch, 0, 0))]
        + [whole(array) for array in arrays],
        out_specs=[whole(out) for out in outs],
        scratch_shapes=[pltpu.VMEM((rows, rows), F32), pltpu.VMEM((rows, rows), F32)],
        compiler_params=PARAMS,
        name=name,
    )(place, tags, values, noise, *arrays)


def batches(place, tags, values, noise, state, observed, prior):
    shape = jax.ShapeDtypeStruct(noise.shape[1:], BF16)
    shared = (place, tags, values, noise)
    whitened, white_innov = batch_call(
        first_kernel, "first_batch", 0, [shape, shape], *shared, *observed
    )
    analysis = jax.ShapeDtypeStruct(state.shape, F32)
    return batch_call(
        second_kernel, "second_batch", 1, [analysis], *shared, *prior, state, whitened, white_innov
    )[0]


AXES = ("row", "col")
CORE, Y, X, NEAR_Z, FAR_Z = 1, 2, 4, 8, 16


def swap(value, mask):
    return lax.ppermute(value, AXES, [(i, i ^ mask) for i in range(32)])


def by_slots(place, ensemble, blocks, weights):
    keep, send = pick(place, blocks, weights, ensemble)
    block = (keep + swap(send, CORE))[None]
    here = jnp.concatenate([block, swap(block, FAR_Z)], axis=0)
    near = swap(here, NEAR_Z)
    early = [(0, here), (NEAR_Z // 2, near)]
    early += [(mask // 2, swap(here, mask)) for mask in (Y, X, X | Y)]
    late = [((NEAR_Z | mask) // 2, swap(near, mask)) for mask in (Y, X, X | Y)]
    return late_rows(place, blocks, early_rows(place, blocks, early), late)


def add_by_swaps(value):
    for mask in (CORE, Y, X, NEAR_Z, FAR_Z):
        value = value + swap(value, mask)
    return value


def half_of(value, core):
    rows, members = value.shape
    return lax.dynamic_slice(value, (0, core * (members // 2)), (rows, members // 2))


def by_sum(add_up, other, place, ensemble, blocks, weights):
    rows = blocks.shape[1]
    codes = add_up(pick_all(place, blocks, weights, ensemble))
    codes = half_of(codes, (place[0] + other) % 2)
    return (codes[:rows] * UNIT).astype(BF16), codes[rows:].astype(jnp.int16)


def body(staged, ensemble, obs_blocks, obs_weights, comp_tags, obs_values, obs_noise):
    held = ensemble.shape[0] // obs_weights.shape[2]
    place = jnp.stack([lax.axis_index(AXES), held]).astype(jnp.int32)
    by_point = jnp.swapaxes(obs_weights, 1, 2)
    operands = (place, ensemble, obs_blocks, by_point)
    if staged:
        pair = obs_blocks // (2 * held)
        counts = jnp.sum(
            (pair[:, :, None] == jnp.arange(16, dtype=jnp.int32)).astype(jnp.int32), axis=(0, 1)
        )
        slotted = by_slots(*operands)
        own = lax.cond(
            jnp.max(counts) <= SLOTS,
            lambda slotted, *operands: tuple(slotted),
            lambda slotted, *operands: by_sum(add_by_swaps, 0, *operands),
            slotted,
            *operands,
        )
        pairs = [(half, swap(half, CORE)) for half in own]
    else:
        add_up = lambda value: lax.psum(value, AXES)
        pairs = list(zip(by_sum(add_up, 0, *operands), by_sum(add_up, 1, *operands)))
    return batches(place, comp_tags, obs_values, obs_noise, ensemble, *pairs)


def solution(mesh):
    staged = (mesh.shape["row"], mesh.shape["col"]) == (8, 4)
    in_specs = (P(AXES, None), P(), P(), P(), P(), P())
    out_specs = P(AXES, None)
    return jax.shard_map(
        functools.partial(body, staged),
        mesh=mesh,
        in_specs=in_specs,
        out_specs=out_specs,
        check_vma=False,
    )
```

```python
import functools

import jax
import jax.numpy as jnp
from jax import lax
from jax.experimental import pallas as pl
from jax.experimental.pallas import tpu as pltpu
from jax.sharding import PartitionSpec as P

SLOTS = 64
UNIT = 1.0 / 1024
SCALE = 0.55
TOLERANCE = 0.03
BF16 = jnp.bfloat16
F32 = jnp.float32
VMEM = pl.BlockSpec(memory_space=pltpu.VMEM)
SMEM = pl.BlockSpec(memory_space=pltpu.SMEM)
PARAMS = pltpu.CompilerParams(vmem_limit_bytes=40 * 1024 * 1024)


def nt(a, b):
    return lax.dot_general(a, b, (((1,), (1,)), ((), ())), preferred_element_type=F32)


def nn(a, b):
    return lax.dot_general(a, b, (((1,), (0,)), ((), ())), preferred_element_type=F32)


def split(a):
    high = a.astype(BF16)
    return high, (a - high.astype(F32)).astype(BF16)


def dot3(dot, a, b):
    (ah, al), (bh, bl) = a, b
    return dot(ah, bh) + (dot(ah, bl) + dot(al, bh))


def row_mean(a):
    return jnp.sum(a, axis=1, keepdims=True) * (1.0 / a.shape[1])


def column(row):
    size = row.shape[1]
    lane = lax.broadcasted_iota(jnp.int32, (size, size), 1)
    sub = lax.broadcasted_iota(jnp.int32, (size, size), 0)
    return jnp.sum(jnp.where(lane == sub, row, jnp.zeros_like(row)), axis=1, keepdims=True)


def both_ways(row):
    as_float = row.astype(F32)
    return as_float, column(as_float)


def select(lanes, points, local, weight):
    value = jnp.zeros(lanes.shape, F32)
    for point in range(points):
        value = jnp.where(lanes % points == point, weight[point], value)
    return jnp.where((lanes // points).astype(F32) == local, value, 0.0)


def rounded(value):
    return value.astype(BF16).astype(F32)


def pick_kernel(place, blocks, weights, state_ref, keep, send, state, arrived):
    load = pltpu.make_async_copy(state_ref, state, arrived)
    load.start()
    device = place[0]
    batches, points, size = weights.shape
    width, members = state.shape
    held = width // points
    lane = lax.broadcasted_iota(jnp.int32, (size, size), 1)
    sub = lax.broadcasted_iota(jnp.int32, (size, size), 0)
    slots = lax.broadcasted_iota(jnp.int32, (SLOTS, size), 0)
    lanes = lax.broadcasted_iota(jnp.int32, (SLOTS, width), 1)
    selectors, taken = [], []
    for batch in range(batches):
        row = blocks[batch : batch + 1, :]
        pair_row, pair_column = both_ways(row // (2 * held))
        before = jnp.where((pair_row == pair_column) & (sub < lane), 1.0, 0.0)
        rank = jnp.sum(before, axis=0, keepdims=True).astype(jnp.int32)
        slot = jnp.where(row // held == device, rank if batch == 0 else SLOTS - 1 - rank, -1)
        chosen = jnp.where(slots == slot, 1.0, 0.0)
        local = jnp.sum(chosen * (row - device * held).astype(F32), axis=1, keepdims=True)
        weight = lax.dot_general(
            chosen,
            weights[batch],
            (((1,), (1,)), ((), ())),
            precision=lax.Precision.HIGHEST,
            preferred_element_type=F32,
        )
        columns = [weight[:, point : point + 1] for point in range(points)]
        selectors.append(select(lanes, points, local, columns))
        taken.append(jnp.sum(chosen, axis=1, keepdims=True))
    load.wait()
    rows = jnp.dot(
        selectors[0] + selectors[1],
        state[...],
        precision=lax.Precision.HIGHEST,
        preferred_element_type=F32,
    )
    rows = jnp.where(taken[0] > 0.5, rounded(rows), rows)
    code = jnp.round(rows * (1.0 / UNIT)).astype(jnp.int32)
    left, right = code[:, : members // 2], code[:, members // 2 :]
    first = device % 2 == 0
    keep[...] = jnp.where(first, left, right).astype(jnp.int16)
    send[...] = jnp.where(first, right, left).astype(jnp.int16)


def pick(place, blocks, weights, state):
    return pl.pallas_call(
        pick_kernel,
        out_shape=[jax.ShapeDtypeStruct((SLOTS, state.shape[1] // 2), jnp.int16)] * 2,
        in_specs=[SMEM, VMEM, VMEM, pl.BlockSpec(memory_space=pl.ANY)],
        out_specs=[VMEM] * 2,
        scratch_shapes=[pltpu.VMEM(state.shape, F32), pltpu.SemaphoreType.DMA],
        compiler_params=PARAMS,
        name="pick",
    )(place, blocks, weights, state)


def pick_all_kernel(place, blocks, weights, state, out):
    device = place[0]
    batches, points, size = weights.shape
    width = state.shape[0]
    lanes = lax.broadcasted_iota(jnp.int32, (size, width), 1)
    for batch in range(batches):
        columns = [column(weights[batch, point : point + 1, :]) for point in range(points)]
        local = column((blocks[batch : batch + 1, :] - device * (width // points)).astype(F32))
        rows = jnp.dot(
            select(lanes, points, local, columns),
            state[...],
            precision=lax.Precision.HIGHEST,
            preferred_element_type=F32,
        )
        rows = rounded(rows) if batch == 0 else rows
        out[batch * size : (batch + 1) * size, :] = jnp.round(rows * (1.0 / UNIT))


def pick_all(place, blocks, weights, state):
    return pl.pallas_call(
        pick_all_kernel,
        out_shape=jax.ShapeDtypeStruct((blocks.size, state.shape[1]), F32),
        in_specs=[SMEM, VMEM, VMEM, VMEM],
        out_specs=VMEM,
        compiler_params=PARAMS,
        name="pick_all",
    )(place, blocks, weights, state)


def order_kernel(groups, place, blocks, *outs):
    device, held = place[0], place[1]
    size = blocks.shape[1]
    lane = lax.broadcasted_iota(jnp.int32, (size, size), 1)
    sub = lax.broadcasted_iota(jnp.int32, (size, size), 0)
    for batch in range(blocks.shape[0]):
        pair_row, pair_column = both_ways(blocks[batch : batch + 1, :] // (2 * held))
        before = jnp.where((pair_row == pair_column) & (lane < sub), 1.0, 0.0)
        rank = jnp.sum(before, axis=1, keepdims=True).astype(jnp.int32)
        away = (2 * pair_column.astype(jnp.int32)) ^ device
        slot = SLOTS * ((away >> 4) & 1) + (rank if batch == 0 else SLOTS - 1 - rank)
        for distances, out in zip(groups, outs):
            where = jnp.full(rank.shape, -2 * SLOTS, jnp.int32)
            for index, distance in enumerate(distances):
                where = jnp.where((away >> 1) & 7 == distance, 2 * SLOTS * index, where)
            slots = lax.broadcasted_iota(jnp.int32, (size, out.shape[1]), 1)
            chosen = jnp.where(slots == where + slot, 1.0, 0.0)
            out[batch * size : (batch + 1) * size, :] = chosen.astype(BF16)


def order(place, blocks, groups):
    return pl.pallas_call(
        functools.partial(order_kernel, groups),
        out_shape=[
            jax.ShapeDtypeStruct((blocks.size, 2 * SLOTS * len(group)), BF16) for group in groups
        ],
        in_specs=[SMEM, VMEM],
        out_specs=[VMEM] * len(groups),
        compiler_params=PARAMS,
        cost_estimate=pl.CostEstimate(flops=10**6, bytes_accessed=10**6, transcendentals=0),
        name="order",
    )(place, blocks)


def put_in_order(chosen, pieces):
    size = chosen.shape[0] // 2
    values = jnp.concatenate([ref[...].reshape(2 * SLOTS, -1) for ref in pieces], axis=0)
    high, low = split(values.astype(jnp.int32).astype(F32))
    second = chosen[size:, :]
    return nn(chosen[:size, :], high), nn(second, high) + nn(second, low)


def early_kernel(chosen, *refs):
    size = chosen.shape[0] // 2
    refs[-1][:size, :], refs[-1][size:, :] = put_in_order(chosen, refs[:-1])


def late_kernel(chosen, early, *refs):
    size = chosen.shape[0] // 2
    first, second = put_in_order(chosen, refs[:-2])
    refs[-2][...] = ((first + early[:size, :]) * UNIT).astype(BF16)
    refs[-1][...] = (second + early[size:, :]).astype(jnp.int32).astype(jnp.int16)


def early_rows(chosen, pieces):
    return pl.pallas_call(
        early_kernel,
        out_shape=jax.ShapeDtypeStruct((chosen.shape[0], pieces[0].shape[-1]), F32),
        in_specs=[VMEM] * (1 + len(pieces)),
        out_specs=VMEM,
        compiler_params=PARAMS,
        cost_estimate=pl.CostEstimate(flops=10**9, bytes_accessed=4 * 10**6, transcendentals=0),
        name="early_rows",
    )(chosen, *pieces)


def late_rows(chosen, early, pieces):
    shape = (early.shape[0] // 2, early.shape[1])
    return pl.pallas_call(
        late_kernel,
        out_shape=[jax.ShapeDtypeStruct(shape, BF16), jax.ShapeDtypeStruct(shape, jnp.int16)],
        in_specs=[VMEM] * (2 + len(pieces)),
        out_specs=[VMEM] * 2,
        compiler_params=PARAMS,
        name="late_rows",
    )(chosen, early, *pieces)


def eliminate(covariance, work, inverse):
    size = covariance.shape[0]
    lane = lax.broadcasted_iota(jnp.int32, (size, size), 1)
    sub = lax.broadcasted_iota(jnp.int32, (size, size), 0)
    work[...] = covariance
    inverse[...] = jnp.where(lane == sub, 1.0, 0.0)

    def step(k, carry):
        row = work[pl.ds(k, 1), :]
        current = work[...]
        pivot = jnp.sum(jnp.where(lane[:1] == k, row, 0.0), axis=1, keepdims=True)
        column = jnp.sum(jnp.where(lane == k, current, 0.0), axis=1, keepdims=True)
        factor = jnp.where(sub[:, :1] > k, column / pivot, 0.0)
        inverse_row = inverse[pl.ds(k, 1), :]
        work[...] = current - factor * row
        inverse[...] = inverse[...] - factor * inverse_row
        return carry

    lax.fori_loop(0, size, step, 0)
    pivots = jnp.sum(jnp.where(lane == sub, work[...], 0.0), axis=1, keepdims=True)
    inverse[...] = inverse[...] * (1.0 / jnp.sqrt(pivots))


def inverse_factor(covariance, work, inverse):
    size = covariance.shape[0]
    lane = lax.broadcasted_iota(jnp.int32, (size, size), 1)
    sub = lax.broadcasted_iota(jnp.int32, (size, size), 0)
    diagonal = lane == sub
    eye = jnp.where(diagonal, 1.0, 0.0)
    half = jnp.where(lane < sub, 1.0, jnp.where(diagonal, 0.5, 0.0))
    on_diagonal = jnp.where(diagonal, covariance, 0.0)
    scale_row = lax.rsqrt(jnp.sum(on_diagonal, axis=0, keepdims=True) * (1.0 / SCALE))
    scale_column = lax.rsqrt(jnp.sum(on_diagonal, axis=1, keepdims=True) * (1.0 / SCALE))
    scaled = covariance * scale_row * scale_column

    def third_order(m):
        low = (m - eye) * half
        lowb = low.astype(BF16)
        return (nn(lowb, lowb) + half * nt(lowb, lowb)) - low

    m = scaled
    t = None
    for step in range(2):
        u = third_order(m) + eye
        ub = u.astype(BF16)
        t = u if t is None else nn(ub, t.astype(BF16))
        if step < 1:
            m = nt(nn(ub, m.astype(BF16)).astype(BF16), ub)
    parts = split(scaled)
    ts = split(t)
    m = dot3(nt, split(dot3(nn, ts, parts)), ts)
    t = t + nn(third_order(m).astype(BF16), ts[0])
    ts = split(t)
    m = dot3(nt, split(dot3(nn, ts, parts)), ts)
    error = m - eye
    t = t - nn((error * half).astype(BF16), ts[0])
    inverse[...] = t * scale_row
    good = jnp.sum(error * error) <= TOLERANCE * TOLERANCE

    @pl.when(jnp.logical_not(good))
    def _():
        eliminate(covariance, work, inverse)


def whiten(observed, tags, values, noise, work, inverse):
    members = observed.shape[1]
    size = observed.shape[0]
    mean = row_mean(observed)
    ah, al = split(observed - mean)
    lane = lax.broadcasted_iota(jnp.int32, (size, size), 1)
    sub = lax.broadcasted_iota(jnp.int32, (size, size), 0)
    variance_row = jnp.where(tags == 0, 0.5, 2.0)
    variance = column(variance_row)
    mean_row = jnp.sum(jnp.where(lane == sub, mean, 0.0), axis=0, keepdims=True)
    covariance = dot3(nt, (ah, al), (ah, al)) * (1.0 / (members - 1))
    covariance = covariance + jnp.where(lane == sub, variance, 0.0)
    inverse_factor(covariance, work, inverse)
    t = inverse[...]
    th, tl = split(t)
    nh, nl = split(t * jnp.sqrt(variance_row))
    exact = observed.astype(BF16)
    applied = nn(th, exact) + nn(tl, exact)
    noise = nn(nh, noise) + nn(nl, noise)
    mean_part = jnp.sum(t * mean_row, axis=1, keepdims=True)
    value_part = jnp.sum(t * values, axis=1, keepdims=True)
    whitened = (applied - mean_part).astype(BF16)
    white_innov = (noise + value_part - applied).astype(BF16)
    return whitened, white_innov


def update(state, whitened, white_innov):
    members = state.shape[1]
    sh, sl = split(state - row_mean(state))
    ph, plow = split(nt(sh, whitened) + nt(sl, whitened))
    return state + (nn(ph, white_innov) + nn(plow, white_innov)) * (1.0 / (members - 1))


def both_halves(place, own, other):
    own, other = own[...].astype(F32), other[...].astype(F32)
    first = place[0] % 2 == 0
    return jnp.concatenate(
        [jnp.where(first, own, other), jnp.where(first, other, own)], axis=1
    )


def first_kernel(place, tags, values, noise, own, other, whitened, white_innov, work, inverse):
    observed = both_halves(place, own, other)
    w, v = whiten(observed, tags[:1, :], values[:1, :], noise[0], work, inverse)
    whitened[...] = w
    white_innov[...] = v


def second_kernel(
    place, tags, values, noise, own, other, state, whitened, white_innov, analysis, work, inverse
):
    prior = both_halves(place, own, other) * UNIT
    w, v = whitened[...], white_innov[...]
    observed = rounded(update(prior, w, v))
    first = update(state[...], w, v)
    w, v = whiten(observed, tags[1:2, :], values[1:2, :], noise[0], work, inverse)
    analysis[...] = update(first, w, v)


def whole(array):
    return pl.BlockSpec(array.shape, lambda i, n=len(array.shape): (0,) * n)


def batch_call(kernel, name, batch, outs, place, tags, values, noise, *arrays):
    rows, members = noise.shape[1:]
    return pl.pallas_call(
        kernel,
        grid=(1,),
        out_shape=outs,
        in_specs=[SMEM, whole(tags), whole(values)]
        + [pl.BlockSpec((1, rows, members), lambda i: (batch, 0, 0))]
        + [whole(array) for array in arrays],
        out_specs=[whole(out) for out in outs],
        scratch_shapes=[pltpu.VMEM((rows, rows), F32), pltpu.VMEM((rows, rows), F32)],
        compiler_params=PARAMS,
        name=name,
    )(place, tags, values, noise, *arrays)


def batches(place, tags, values, noise, state, observed, prior):
    shape = jax.ShapeDtypeStruct(noise.shape[1:], BF16)
    shared = (place, tags, values, noise)
    whitened, white_innov = batch_call(
        first_kernel, "first_batch", 0, [shape, shape], *shared, *observed
    )
    analysis = jax.ShapeDtypeStruct(state.shape, F32)
    return batch_call(
        second_kernel, "second_batch", 1, [analysis], *shared, *prior, state, whitened, white_innov
    )[0]


AXES = ("row", "col")
CORE, Y, X, NEAR_Z, FAR_Z = 1, 2, 4, 8, 16


def swap(value, mask):
    return lax.ppermute(value, AXES, [(i, i ^ mask) for i in range(32)])


def by_slots(place, ensemble, blocks, weights):
    sides = (X | Y, X, Y)
    groups = [[0] + [mask // 2 for mask in sides + (NEAR_Z,)]]
    groups += [[(NEAR_Z | mask) // 2 for mask in sides]]
    early_places, late_places = order(place, blocks, groups)
    keep, send = pick(place, blocks, weights, ensemble)
    block = (keep + swap(send, CORE))[None]
    here = jnp.concatenate([block, swap(block, FAR_Z)], axis=0)
    early = [here] + [swap(here, mask) for mask in sides + (NEAR_Z,)]
    late = [swap(early[-1], mask) for mask in sides]
    return late_rows(late_places, early_rows(early_places, early), late)


def add_by_swaps(value):
    for mask in (CORE, Y, X, NEAR_Z, FAR_Z):
        value = value + swap(value, mask)
    return value


def half_of(value, core):
    rows, members = value.shape
    return lax.dynamic_slice(value, (0, core * (members // 2)), (rows, members // 2))


def by_sum(add_up, other, place, ensemble, blocks, weights):
    rows = blocks.shape[1]
    codes = add_up(pick_all(place, blocks, weights, ensemble))
    codes = half_of(codes, (place[0] + other) % 2)
    return (codes[:rows] * UNIT).astype(BF16), codes[rows:].astype(jnp.int16)


def body(staged, ensemble, obs_blocks, obs_weights, comp_tags, obs_values, obs_noise):
    held = ensemble.shape[0] // obs_weights.shape[2]
    place = jnp.stack([lax.axis_index(AXES), held]).astype(jnp.int32)
    by_point = jnp.swapaxes(obs_weights, 1, 2)
    operands = (place, ensemble, obs_blocks, by_point)
    if staged:
        pair = obs_blocks // (2 * held)
        counts = jnp.sum(
            (pair[:, :, None] == jnp.arange(16, dtype=jnp.int32)).astype(jnp.int32), axis=(0, 1)
        )
        slotted = by_slots(*operands)
        own = lax.cond(
            jnp.max(counts) <= SLOTS,
            lambda slotted, *operands: tuple(slotted),
            lambda slotted, *operands: by_sum(add_by_swaps, 0, *operands),
            slotted,
            *operands,
        )
        pairs = [(half, swap(half, CORE)) for half in own]
    else:
        add_up = lambda value: lax.psum(value, AXES)
        pairs = list(zip(by_sum(add_up, 0, *operands), by_sum(add_up, 1, *operands)))
    return batches(place, comp_tags, obs_values, obs_noise, ensemble, *pairs)


def solution(mesh):
    staged = (mesh.shape["row"], mesh.shape["col"]) == (8, 4)
    in_specs = (P(AXES, None), P(), P(), P(), P(), P())
    out_specs = P(AXES, None)
    return jax.shard_map(
        functools.partial(body, staged),
        mesh=mesh,
        in_specs=in_specs,
        out_specs=out_specs,
        check_vma=False,
    )
```

```python
import functools

import jax
import jax.numpy as jnp
from jax import lax
from jax.experimental import pallas as pl
from jax.experimental.pallas import tpu as pltpu
from jax.sharding import PartitionSpec as P

SLOTS = 64
UNIT = 1.0 / 1024
SCALE = 0.55
TOLERANCE = 0.16
BF16 = jnp.bfloat16
F32 = jnp.float32
VMEM = pl.BlockSpec(memory_space=pltpu.VMEM)
SMEM = pl.BlockSpec(memory_space=pltpu.SMEM)
ANYWHERE = pl.BlockSpec(memory_space=pl.ANY)
PARAMS = pltpu.CompilerParams(vmem_limit_bytes=40 * 1024 * 1024)


def nt(a, b):
    return lax.dot_general(a, b, (((1,), (1,)), ((), ())), preferred_element_type=F32)


def nn(a, b):
    return lax.dot_general(a, b, (((1,), (0,)), ((), ())), preferred_element_type=F32)


def split(a):
    high = a.astype(BF16)
    return high, (a - high.astype(F32)).astype(BF16)


def dot3(dot, a, b):
    (ah, al), (bh, bl) = a, b
    return dot(ah, bh) + (dot(ah, bl) + dot(al, bh))


def row_mean(a):
    return jnp.sum(a, axis=1, keepdims=True) * (1.0 / a.shape[1])


def column(row):
    size = row.shape[1]
    lane = lax.broadcasted_iota(jnp.int32, (size, size), 1)
    sub = lax.broadcasted_iota(jnp.int32, (size, size), 0)
    return jnp.sum(jnp.where(lane == sub, row, jnp.zeros_like(row)), axis=1, keepdims=True)


def both_ways(row):
    as_float = row.astype(F32)
    return as_float, column(as_float)


def select(lanes, points, local, weight):
    value = jnp.zeros(lanes.shape, F32)
    for point in range(points):
        value = jnp.where(lanes % points == point, weight[point], value)
    return jnp.where((lanes // points).astype(F32) == local, value, 0.0)


def rounded(value):
    return value.astype(BF16).astype(F32)


def three_parts(a):
    high = a.astype(BF16)
    rest = a - high.astype(F32)
    middle = rest.astype(BF16)
    return high, middle, (rest - middle.astype(F32)).astype(BF16)


def pick_kernel(place, blocks, weights, state_ref, keep, send, state, arrived):
    load = pltpu.make_async_copy(state_ref, state, arrived)
    load.start()
    device = place[0]
    batches, points, size = weights.shape
    width, members = state.shape
    held = width // points
    lane = lax.broadcasted_iota(jnp.int32, (size, size), 1)
    sub = lax.broadcasted_iota(jnp.int32, (size, size), 0)
    earlier = jnp.where(sub < lane, 1.0, 0.0).astype(BF16)
    row = blocks[...]
    mine = jnp.where(row // (2 * held) == device // 2, 1.0, 0.0)
    rank = nn(mine.astype(BF16), earlier).astype(jnp.int32)
    own = row // held == device
    slots = lax.broadcasted_iota(jnp.int32, (SLOTS, size), 0)
    points_of = lax.broadcasted_iota(jnp.int32, (width, size), 0)
    chosen, selector = [], []
    for batch in range(batches):
        place_of = rank[batch : batch + 1, :]
        place_of = place_of if batch == 0 else SLOTS - 1 - place_of
        place_of = jnp.where(own[batch : batch + 1, :], place_of, -1)
        chosen.append(jnp.where(slots == place_of, 1.0, 0.0))
        value = jnp.zeros((width, size), F32)
        for point in range(points):
            weight = weights[batch, point : point + 1, :]
            value = jnp.where(points_of % points == point, weight, value)
        local = row[batch : batch + 1, :] - device * held
        selector.append(jnp.where(points_of // points == local, value, 0.0))
    chosen = jnp.concatenate(chosen, axis=1).astype(BF16)
    parts = three_parts(jnp.concatenate(selector, axis=1))
    high, middle, low = [nt(chosen, part).astype(BF16) for part in parts]
    load.wait()
    top, mid, end = three_parts(state[...])
    rows = nn(high, end) + nn(middle, mid) + nn(low, top)
    rows = (nn(high, mid) + nn(middle, top)) + rows
    rows = nn(high, top) + rows
    from_first = lax.broadcasted_iota(jnp.int32, (SLOTS, 1), 0).astype(F32)
    from_first = from_first < jnp.sum(mine[:1, :], axis=1, keepdims=True)
    rows = jnp.where(from_first, rounded(rows), rows)
    code = jnp.round(rows * (1.0 / UNIT)).astype(jnp.int32)
    left, right = code[:, : members // 2], code[:, members // 2 :]
    first = device % 2 == 0
    keep[...] = jnp.where(first, left, right).astype(jnp.int16)
    send[...] = jnp.where(first, right, left).astype(jnp.int16)


def pick(place, blocks, weights, state):
    return pl.pallas_call(
        pick_kernel,
        out_shape=[jax.ShapeDtypeStruct((SLOTS, state.shape[1] // 2), jnp.int16)] * 2,
        in_specs=[SMEM, VMEM, VMEM, ANYWHERE],
        out_specs=[VMEM] * 2,
        scratch_shapes=[pltpu.VMEM(state.shape, F32), pltpu.SemaphoreType.DMA],
        compiler_params=PARAMS,
        name="pick",
    )(place, blocks, weights, state)


def pick_all_kernel(place, blocks, weights, state, out):
    device = place[0]
    batches, points, size = weights.shape
    width = state.shape[0]
    lanes = lax.broadcasted_iota(jnp.int32, (size, width), 1)
    for batch in range(batches):
        columns = [column(weights[batch, point : point + 1, :]) for point in range(points)]
        local = column((blocks[batch : batch + 1, :] - device * (width // points)).astype(F32))
        rows = jnp.dot(
            select(lanes, points, local, columns),
            state[...],
            precision=lax.Precision.HIGHEST,
            preferred_element_type=F32,
        )
        rows = rounded(rows) if batch == 0 else rows
        out[batch * size : (batch + 1) * size, :] = jnp.round(rows * (1.0 / UNIT))


def pick_all(place, blocks, weights, state):
    return pl.pallas_call(
        pick_all_kernel,
        out_shape=jax.ShapeDtypeStruct((blocks.size, state.shape[1]), F32),
        in_specs=[SMEM, VMEM, VMEM, VMEM],
        out_specs=VMEM,
        compiler_params=PARAMS,
        name="pick_all",
    )(place, blocks, weights, state)


def order_kernel(groups, place, blocks, *outs):
    device, held = place[0], place[1]
    size = blocks.shape[1]
    lane = lax.broadcasted_iota(jnp.int32, (size, size), 1)
    sub = lax.broadcasted_iota(jnp.int32, (size, size), 0)
    for batch in range(blocks.shape[0]):
        pair_row, pair_column = both_ways(blocks[batch : batch + 1, :] // (2 * held))
        before = jnp.where((pair_row == pair_column) & (lane < sub), 1.0, 0.0)
        rank = jnp.sum(before, axis=1, keepdims=True).astype(jnp.int32)
        away = (2 * pair_column.astype(jnp.int32)) ^ device
        x, y = (away >> 2) & 1, (away >> 1) & 1
        plane = jnp.where(device % 2 == 0, 2 * x + y, 2 * y + x)
        distance = 8 * ((away >> 3) & 1) + 4 * ((away >> 4) & 1) + plane
        slot = rank if batch == 0 else SLOTS - 1 - rank
        for distances, out in zip(groups, outs):
            where = jnp.full(rank.shape, -SLOTS, jnp.int32)
            for index, known in enumerate(distances):
                where = jnp.where(distance == known, SLOTS * index, where)
            slots = lax.broadcasted_iota(jnp.int32, (size, out.shape[1]), 1)
            chosen = jnp.where(slots == where + slot, 1.0, 0.0)
            out[batch * size : (batch + 1) * size, :] = chosen.astype(BF16)


def order(place, blocks, groups):
    return pl.pallas_call(
        functools.partial(order_kernel, groups),
        out_shape=[
            jax.ShapeDtypeStruct((blocks.size, SLOTS * len(group)), BF16) for group in groups
        ],
        in_specs=[SMEM, VMEM],
        out_specs=[VMEM] * len(groups),
        compiler_params=PARAMS,
        cost_estimate=pl.CostEstimate(flops=10**6, bytes_accessed=10**6, transcendentals=0),
        name="order",
    )(place, blocks)


def put_in_order(chosen, pieces):
    size = chosen.shape[0] // 2
    values = jnp.concatenate([ref[...].reshape(-1, ref.shape[-1]) for ref in pieces], axis=0)
    high, low = split(values.astype(jnp.int32).astype(F32))
    second = chosen[size:, :]
    return nn(chosen[:size, :], high), nn(second, high) + nn(second, low)


def early_kernel(chosen, *refs):
    size = chosen.shape[0] // 2
    refs[-1][:size, :], refs[-1][size:, :] = put_in_order(chosen, refs[:-1])


def late_kernel(chosen, early, *refs):
    size = chosen.shape[0] // 2
    first, second = put_in_order(chosen, refs[:-2])
    refs[-2][...] = ((first + early[:size, :]) * UNIT).astype(BF16)
    refs[-1][...] = (second + early[size:, :]).astype(jnp.int32).astype(jnp.int16)


def early_rows(chosen, pieces):
    return pl.pallas_call(
        early_kernel,
        out_shape=jax.ShapeDtypeStruct((chosen.shape[0], pieces[0].shape[-1]), F32),
        in_specs=[VMEM] * (1 + len(pieces)),
        out_specs=VMEM,
        compiler_params=PARAMS,
        cost_estimate=pl.CostEstimate(flops=10**9, bytes_accessed=4 * 10**6, transcendentals=0),
        name="early_rows",
    )(chosen, *pieces)


def late_rows(chosen, early, pieces):
    shape = (early.shape[0] // 2, early.shape[1])
    return pl.pallas_call(
        late_kernel,
        out_shape=[jax.ShapeDtypeStruct(shape, BF16), jax.ShapeDtypeStruct(shape, jnp.int16)],
        in_specs=[VMEM] * (2 + len(pieces)),
        out_specs=[VMEM] * 2,
        compiler_params=PARAMS,
        name="late_rows",
    )(chosen, early, *pieces)


def eliminate(covariance, work, inverse):
    size = covariance.shape[0]
    lane = lax.broadcasted_iota(jnp.int32, (size, size), 1)
    sub = lax.broadcasted_iota(jnp.int32, (size, size), 0)
    work[...] = covariance
    inverse[...] = jnp.where(lane == sub, 1.0, 0.0)

    def step(k, carry):
        row = work[pl.ds(k, 1), :]
        current = work[...]
        pivot = jnp.sum(jnp.where(lane[:1] == k, row, 0.0), axis=1, keepdims=True)
        column = jnp.sum(jnp.where(lane == k, current, 0.0), axis=1, keepdims=True)
        factor = jnp.where(sub[:, :1] > k, column / pivot, 0.0)
        inverse_row = inverse[pl.ds(k, 1), :]
        work[...] = current - factor * row
        inverse[...] = inverse[...] - factor * inverse_row
        return carry

    lax.fori_loop(0, size, step, 0)
    pivots = jnp.sum(jnp.where(lane == sub, work[...], 0.0), axis=1, keepdims=True)
    inverse[...] = inverse[...] * (1.0 / jnp.sqrt(pivots))


def inverse_factor(covariance):
    size = covariance.shape[0]
    lane = lax.broadcasted_iota(jnp.int32, (size, size), 1)
    sub = lax.broadcasted_iota(jnp.int32, (size, size), 0)
    diagonal = lane == sub
    eye = jnp.where(diagonal, 1.0, 0.0)
    half = jnp.where(lane < sub, 1.0, jnp.where(diagonal, 0.5, 0.0))
    on_diagonal = jnp.where(diagonal, covariance, 0.0)
    scale_row = lax.rsqrt(jnp.sum(on_diagonal, axis=0, keepdims=True) * (1.0 / SCALE))
    scale_column = lax.rsqrt(jnp.sum(on_diagonal, axis=1, keepdims=True) * (1.0 / SCALE))
    scaled = covariance * scale_row * scale_column

    def third_order(error):
        low = error * half
        lowb = low.astype(BF16)
        return (nn(lowb, lowb) + half * nt(lowb, lowb)) - low

    m = scaled
    t = None
    for step in range(3):
        u = third_order(m - eye) + eye
        ub = u.astype(BF16)
        t = u if t is None else nn(ub, t.astype(BF16))
        if step < 2:
            m = nt(nn(ub, m.astype(BF16)).astype(BF16), ub)
    ts = split(t)
    error = dot3(nt, split(dot3(nn, ts, split(scaled))), ts) - eye
    t = t + nn(third_order(error).astype(BF16), ts[0])
    return t * scale_row, jnp.sum(error * error) <= TOLERANCE * TOLERANCE


def whiten(observed, tags, values, load, noise_ref, work, inverse, store):
    members = observed.shape[1]
    size = observed.shape[0]
    mean = row_mean(observed)
    parts = split(observed - mean)
    lane = lax.broadcasted_iota(jnp.int32, (size, size), 1)
    sub = lax.broadcasted_iota(jnp.int32, (size, size), 0)
    variance_row = jnp.where(tags == 0, 0.5, 2.0)
    variance = column(variance_row)
    mean_row = jnp.sum(jnp.where(lane == sub, mean, 0.0), axis=0, keepdims=True)
    covariance = dot3(nt, parts, parts) * (1.0 / (members - 1))
    covariance = covariance + jnp.where(lane == sub, variance, 0.0)
    exact = observed.astype(BF16)

    def finish(t):
        th, tl = split(t)
        nh, nl = split(t * jnp.sqrt(variance_row))
        applied = nn(th, exact) + nn(tl, exact)
        noise = nn(nh, noise_ref[...]) + nn(nl, noise_ref[...])
        mean_part = jnp.sum(t * mean_row, axis=1, keepdims=True)
        value_part = jnp.sum(t * values, axis=1, keepdims=True)
        store((applied - mean_part).astype(BF16), (noise + value_part - applied).astype(BF16))

    t, good = inverse_factor(covariance)
    load.wait()
    finish(t)

    @pl.when(jnp.logical_not(good))
    def _():
        eliminate(covariance, work, inverse)
        finish(inverse[...])


def update(state, whitened, white_innov):
    members = state.shape[1]
    sh, sl = split(state - row_mean(state))
    ph, plow = split(nt(sh, whitened) + nt(sl, whitened))
    return state + (nn(ph, white_innov) + nn(plow, white_innov)) * (1.0 / (members - 1))


def both_halves(place, own, other):
    own, other = own[...].astype(F32), other[...].astype(F32)
    first = place[0] % 2 == 0
    return jnp.concatenate(
        [jnp.where(first, own, other), jnp.where(first, other, own)], axis=1
    )


def first_kernel(
    place, tags, values, noise_ref, own, other, whitened, white_innov, noise, loads, work, inverse
):
    load = pltpu.make_async_copy(noise_ref.at[0], noise, loads.at[0])
    load.start()
    observed = both_halves(place, own, other)

    def store(w, v):
        whitened[...] = w
        white_innov[...] = v

    whiten(observed, tags[:1, :], values[:1, :], load, noise, work, inverse, store)


def second_kernel(
    place,
    tags,
    values,
    noise_ref,
    own,
    other,
    whitened,
    white_innov,
    state_ref,
    analysis,
    noise,
    loads,
    work,
    inverse,
    state,
):
    load = pltpu.make_async_copy(noise_ref.at[1], noise, loads.at[0])
    load_state = pltpu.make_async_copy(state_ref, state, loads.at[1])
    load_state.start()
    load.start()
    prior = both_halves(place, own, other) * UNIT
    w, v = whitened[...], white_innov[...]
    observed = rounded(update(prior, w, v))
    load_state.wait()
    first = update(state[...], w, v)

    def store(w, v):
        analysis[...] = update(first, w, v)

    whiten(observed, tags[1:2, :], values[1:2, :], load, noise, work, inverse, store)


def batch_call(kernel, name, outs, place, tags, values, noise, *arrays, state=()):
    rows, members = noise.shape[1:]
    return pl.pallas_call(
        kernel,
        out_shape=outs,
        in_specs=[SMEM, VMEM, VMEM, ANYWHERE] + [VMEM] * len(arrays) + [ANYWHERE] * len(state),
        out_specs=[VMEM] * len(outs),
        scratch_shapes=[
            pltpu.VMEM((rows, members), BF16),
            pltpu.SemaphoreType.DMA((2,)),
            pltpu.VMEM((rows, rows), F32),
            pltpu.VMEM((rows, rows), F32),
        ]
        + [pltpu.VMEM(array.shape, F32) for array in state],
        compiler_params=PARAMS,
        name=name,
    )(place, tags, values, noise, *arrays, *state)


def batches(place, tags, values, noise, state, observed, prior):
    shape = jax.ShapeDtypeStruct(noise.shape[1:], BF16)
    shared = (place, tags, values, noise)
    white = batch_call(first_kernel, "first_batch", [shape, shape], *shared, *observed)
    analysis = jax.ShapeDtypeStruct(state.shape, F32)
    return batch_call(
        second_kernel, "second_batch", [analysis], *shared, *prior, *white, state=(state,)
    )[0]


AXES = ("row", "col")
CORE, Y, X, NEAR_Z, FAR_Z = 1, 2, 4, 8, 16


def swap(value, mask, odd_mask=None):
    masks = (mask, mask if odd_mask is None else odd_mask)
    return lax.ppermute(value, AXES, [(i, i ^ masks[i % 2]) for i in range(32)])


def along_first(value):
    return swap(value, X, Y)


def along_second(value):
    return swap(value, Y, X)


EARLY = (0, 8, 4, 2, 6, 1, 5, 3, 7, 12, 10, 14)
LATE = (9, 13, 11, 15)


def by_slots(place, ensemble, blocks, weights):
    keep, send = pick(place, blocks, weights, ensemble)
    own = (keep + swap(send, CORE))[None]
    near_own = swap(own, NEAR_Z)
    far = swap(own, FAR_Z)
    here = jnp.concatenate([own, far], axis=0)
    first = along_first(here)
    second = along_second(jnp.concatenate([here, first], axis=0))
    near_far = swap(far, NEAR_Z)
    near = jnp.concatenate([near_own, near_far], axis=0)
    near_first = along_first(near)
    near_second = along_second(jnp.concatenate([near, near_first], axis=0))
    early_places, late_places = order(place, blocks, (EARLY, LATE))
    early = early_rows(early_places, [own, near_own, far, first, second, near_far, near_first])
    return late_rows(late_places, early, [near_second])


def add_by_swaps(value):
    for mask in (CORE, Y, X, NEAR_Z, FAR_Z):
        value = value + swap(value, mask)
    return value


def half_of(value, core):
    rows, members = value.shape
    return lax.dynamic_slice(value, (0, core * (members // 2)), (rows, members // 2))


def by_sum(add_up, other, place, ensemble, blocks, weights):
    rows = blocks.shape[1]
    codes = add_up(pick_all(place, blocks, weights, ensemble))
    codes = half_of(codes, (place[0] + other) % 2)
    return (codes[:rows] * UNIT).astype(BF16), codes[rows:].astype(jnp.int16)


def body(staged, ensemble, obs_blocks, obs_weights, comp_tags, obs_values, obs_noise):
    held = ensemble.shape[0] // obs_weights.shape[2]
    place = jnp.stack([lax.axis_index(AXES), held]).astype(jnp.int32)
    by_point = jnp.swapaxes(obs_weights, 1, 2)
    operands = (place, ensemble, obs_blocks, by_point)
    if staged:
        pair = obs_blocks // (2 * held)
        counts = jnp.sum(
            (pair[:, :, None] == jnp.arange(16, dtype=jnp.int32)).astype(jnp.int32), axis=(0, 1)
        )
        slotted = by_slots(*operands)
        own = lax.cond(
            jnp.max(counts) <= SLOTS,
            lambda slotted, *operands: tuple(slotted),
            lambda slotted, *operands: by_sum(add_by_swaps, 0, *operands),
            slotted,
            *operands,
        )
        pairs = [(half, swap(half, CORE)) for half in own]
    else:
        add_up = lambda value: lax.psum(value, AXES)
        pairs = list(zip(by_sum(add_up, 0, *operands), by_sum(add_up, 1, *operands)))
    return batches(place, comp_tags, obs_values, obs_noise, ensemble, *pairs)


def solution(mesh):
    staged = (mesh.shape["row"], mesh.shape["col"]) == (8, 4)
    in_specs = (P(AXES, None), P(), P(), P(), P(), P())
    out_specs = P(AXES, None)
    return jax.shard_map(
        functools.partial(body, staged),
        mesh=mesh,
        in_specs=in_specs,
        out_specs=out_specs,
        check_vma=False,
    )
```

```python
import functools

import jax
import jax.numpy as jnp
from jax import lax
from jax.experimental import pallas as pl
from jax.experimental.pallas import tpu as pltpu
from jax.sharding import PartitionSpec as P

SLOTS = 64
UNIT = 1.0 / 1024
SCALE = 0.6
RESCALE = 1.25
TOLERANCE = 0.25
BF16 = jnp.bfloat16
F32 = jnp.float32
VMEM = pl.BlockSpec(memory_space=pltpu.VMEM)
SMEM = pl.BlockSpec(memory_space=pltpu.SMEM)
ANYWHERE = pl.BlockSpec(memory_space=pl.ANY)
PARAMS = pltpu.CompilerParams(vmem_limit_bytes=40 * 1024 * 1024)


def nt(a, b):
    return lax.dot_general(a, b, (((1,), (1,)), ((), ())), preferred_element_type=F32)


def nn(a, b):
    return lax.dot_general(a, b, (((1,), (0,)), ((), ())), preferred_element_type=F32)


def split(a):
    high = a.astype(BF16)
    return high, (a - high.astype(F32)).astype(BF16)


def dot3(dot, a, b):
    (ah, al), (bh, bl) = a, b
    return dot(ah, bh) + (dot(ah, bl) + dot(al, bh))


def row_mean(a):
    return jnp.sum(a, axis=1, keepdims=True) * (1.0 / a.shape[1])


def column(row):
    size = row.shape[1]
    lane = lax.broadcasted_iota(jnp.int32, (size, size), 1)
    sub = lax.broadcasted_iota(jnp.int32, (size, size), 0)
    return jnp.sum(jnp.where(lane == sub, row, jnp.zeros_like(row)), axis=1, keepdims=True)


def both_ways(row):
    as_float = row.astype(F32)
    return as_float, column(as_float)


def select(lanes, points, local, weight):
    value = jnp.zeros(lanes.shape, F32)
    for point in range(points):
        value = jnp.where(lanes % points == point, weight[point], value)
    return jnp.where((lanes // points).astype(F32) == local, value, 0.0)


def rounded(value):
    return value.astype(BF16).astype(F32)


def three_parts(a):
    high = a.astype(BF16)
    rest = a - high.astype(F32)
    middle = rest.astype(BF16)
    return high, middle, (rest - middle.astype(F32)).astype(BF16)


def pick_kernel(place, blocks, weights, state_ref, keep, send, state, arrived):
    load = pltpu.make_async_copy(state_ref, state, arrived)
    load.start()
    device = place[0]
    batches, points, size = weights.shape
    width, members = state.shape
    held = width // points
    lane = lax.broadcasted_iota(jnp.int32, (size, size), 1)
    sub = lax.broadcasted_iota(jnp.int32, (size, size), 0)
    earlier = jnp.where(sub < lane, 1.0, 0.0).astype(BF16)
    row = blocks[...]
    mine = jnp.where(row // (2 * held) == device // 2, 1.0, 0.0)
    rank = nn(mine.astype(BF16), earlier).astype(jnp.int32)
    own = row // held == device
    slots = lax.broadcasted_iota(jnp.int32, (SLOTS, size), 0)
    points_of = lax.broadcasted_iota(jnp.int32, (width, size), 0)
    chosen, selector = [], []
    for batch in range(batches):
        place_of = rank[batch : batch + 1, :]
        place_of = place_of if batch == 0 else SLOTS - 1 - place_of
        place_of = jnp.where(own[batch : batch + 1, :], place_of, -1)
        chosen.append(jnp.where(slots == place_of, 1.0, 0.0))
        value = jnp.zeros((width, size), F32)
        for point in range(points):
            weight = weights[batch, point : point + 1, :]
            value = jnp.where(points_of % points == point, weight, value)
        local = row[batch : batch + 1, :] - device * held
        selector.append(jnp.where(points_of // points == local, value, 0.0))
    chosen = jnp.concatenate(chosen, axis=1).astype(BF16)
    parts = three_parts(jnp.concatenate(selector, axis=1))
    high, middle, low = [nt(chosen, part).astype(BF16) for part in parts]
    load.wait()
    top, mid, end = three_parts(state[...])
    rows = nn(high, end) + nn(middle, mid) + nn(low, top)
    rows = (nn(high, mid) + nn(middle, top)) + rows
    rows = nn(high, top) + rows
    from_first = lax.broadcasted_iota(jnp.int32, (SLOTS, 1), 0).astype(F32)
    from_first = from_first < jnp.sum(mine[:1, :], axis=1, keepdims=True)
    rows = jnp.where(from_first, rounded(rows), rows)
    code = jnp.round(rows * (1.0 / UNIT)).astype(jnp.int32)
    left, right = code[:, : members // 2], code[:, members // 2 :]
    first = device % 2 == 0
    keep[...] = jnp.where(first, left, right).astype(jnp.int16)
    send[...] = jnp.where(first, right, left).astype(jnp.int16)


def pick(place, blocks, weights, state):
    return pl.pallas_call(
        pick_kernel,
        out_shape=[jax.ShapeDtypeStruct((SLOTS, state.shape[1] // 2), jnp.int16)] * 2,
        in_specs=[SMEM, VMEM, VMEM, ANYWHERE],
        out_specs=[VMEM] * 2,
        scratch_shapes=[pltpu.VMEM(state.shape, F32), pltpu.SemaphoreType.DMA],
        compiler_params=PARAMS,
        name="pick",
    )(place, blocks, weights, state)


def pick_all_kernel(place, blocks, weights, state, out):
    device = place[0]
    batches, points, size = weights.shape
    width = state.shape[0]
    lanes = lax.broadcasted_iota(jnp.int32, (size, width), 1)
    for batch in range(batches):
        columns = [column(weights[batch, point : point + 1, :]) for point in range(points)]
        local = column((blocks[batch : batch + 1, :] - device * (width // points)).astype(F32))
        rows = jnp.dot(
            select(lanes, points, local, columns),
            state[...],
            precision=lax.Precision.HIGHEST,
            preferred_element_type=F32,
        )
        rows = rounded(rows) if batch == 0 else rows
        out[batch * size : (batch + 1) * size, :] = jnp.round(rows * (1.0 / UNIT))


def pick_all(place, blocks, weights, state):
    return pl.pallas_call(
        pick_all_kernel,
        out_shape=jax.ShapeDtypeStruct((blocks.size, state.shape[1]), F32),
        in_specs=[SMEM, VMEM, VMEM, VMEM],
        out_specs=VMEM,
        compiler_params=PARAMS,
        name="pick_all",
    )(place, blocks, weights, state)


def order_kernel(groups, place, blocks, *outs):
    outs, fits = outs[:-1], outs[-1]
    device, held = place[0], place[1]
    size = blocks.shape[1]
    lane = lax.broadcasted_iota(jnp.int32, (size, size), 1)
    sub = lax.broadcasted_iota(jnp.int32, (size, size), 0)
    for batch in range(blocks.shape[0]):
        pair_row, pair_column = both_ways(blocks[batch : batch + 1, :] // (2 * held))
        before = jnp.where((pair_row == pair_column) & (lane < sub), 1.0, 0.0)
        rank = jnp.sum(before, axis=1, keepdims=True).astype(jnp.int32)
        away = (2 * pair_column.astype(jnp.int32)) ^ device
        distance = 8 * ((away >> 3) & 1) + 4 * ((away >> 4) & 1) + ((away >> 1) & 3)
        slot = rank if batch == 0 else SLOTS - 1 - rank
        for distances, out in zip(groups, outs):
            where = jnp.full(rank.shape, -SLOTS, jnp.int32)
            for index, known in enumerate(distances):
                where = jnp.where(distance == known, SLOTS * index, where)
            slots = lax.broadcasted_iota(jnp.int32, (size, out.shape[1]), 1)
            chosen = jnp.where(slots == where + slot, 1.0, 0.0)
            out[batch * size : (batch + 1) * size, :] = chosen.astype(BF16)
    counts = jnp.zeros((16, 1), F32)
    for batch in range(blocks.shape[0]):
        chip = blocks[batch : batch + 1, :] // (2 * held)
        chips = lax.broadcasted_iota(jnp.int32, (16, size), 0)
        counts = counts + jnp.sum(jnp.where(chips == chip, 1.0, 0.0), axis=1, keepdims=True)
    fits[0] = (jnp.max(counts) <= SLOTS).astype(jnp.int32)


def order(place, blocks, groups):
    return pl.pallas_call(
        functools.partial(order_kernel, groups),
        out_shape=[
            jax.ShapeDtypeStruct((blocks.size, SLOTS * len(group)), BF16) for group in groups
        ]
        + [jax.ShapeDtypeStruct((1,), jnp.int32)],
        in_specs=[SMEM, VMEM],
        out_specs=[VMEM] * len(groups) + [SMEM],
        compiler_params=PARAMS,
        cost_estimate=pl.CostEstimate(flops=10**6, bytes_accessed=10**6, transcendentals=0),
        name="order",
    )(place, blocks)


def put_in_order(chosen, pieces):
    size = chosen.shape[0] // 2
    values = jnp.concatenate([ref[...].reshape(-1, ref.shape[-1]) for ref in pieces], axis=0)
    high, low = split(values.astype(jnp.int32).astype(F32))
    second = chosen[size:, :]
    return nn(chosen[:size, :], high), nn(second, high) + nn(second, low)


def early_kernel(chosen, *refs):
    size = chosen.shape[0] // 2
    refs[-1][:size, :], refs[-1][size:, :] = put_in_order(chosen, refs[:-1])


def late_kernel(chosen, early, *refs):
    size = chosen.shape[0] // 2
    first, second = put_in_order(chosen, refs[:-2])
    refs[-2][...] = ((first + early[:size, :]) * UNIT).astype(BF16)
    refs[-1][...] = (second + early[size:, :]).astype(jnp.int32).astype(jnp.int16)


def early_rows(chosen, pieces):
    return pl.pallas_call(
        early_kernel,
        out_shape=jax.ShapeDtypeStruct((chosen.shape[0], pieces[0].shape[-1]), F32),
        in_specs=[VMEM] * (1 + len(pieces)),
        out_specs=VMEM,
        compiler_params=PARAMS,
        cost_estimate=pl.CostEstimate(flops=10**9, bytes_accessed=4 * 10**6, transcendentals=0),
        name="early_rows",
    )(chosen, *pieces)


def late_rows(chosen, early, pieces):
    shape = (early.shape[0] // 2, early.shape[1])
    return pl.pallas_call(
        late_kernel,
        out_shape=[jax.ShapeDtypeStruct(shape, BF16), jax.ShapeDtypeStruct(shape, jnp.int16)],
        in_specs=[VMEM] * (2 + len(pieces)),
        out_specs=[VMEM] * 2,
        compiler_params=PARAMS,
        name="late_rows",
    )(chosen, early, *pieces)


def eliminate(covariance, work, inverse):
    size = covariance.shape[0]
    lane = lax.broadcasted_iota(jnp.int32, (size, size), 1)
    sub = lax.broadcasted_iota(jnp.int32, (size, size), 0)
    work[...] = covariance
    inverse[...] = jnp.where(lane == sub, 1.0, 0.0)

    def step(k, carry):
        row = work[pl.ds(k, 1), :]
        current = work[...]
        pivot = jnp.sum(jnp.where(lane[:1] == k, row, 0.0), axis=1, keepdims=True)
        column = jnp.sum(jnp.where(lane == k, current, 0.0), axis=1, keepdims=True)
        factor = jnp.where(sub[:, :1] > k, column / pivot, 0.0)
        inverse_row = inverse[pl.ds(k, 1), :]
        work[...] = current - factor * row
        inverse[...] = inverse[...] - factor * inverse_row
        return carry

    lax.fori_loop(0, size, step, 0)
    pivots = jnp.sum(jnp.where(lane == sub, work[...], 0.0), axis=1, keepdims=True)
    inverse[...] = inverse[...] * (1.0 / jnp.sqrt(pivots))


def squared(a):
    return jnp.sum(a * a)


def newton(scaled):
    size = scaled.shape[0]
    lane = lax.broadcasted_iota(jnp.int32, (size, size), 1)
    sub = lax.broadcasted_iota(jnp.int32, (size, size), 0)
    eye = jnp.where(lane == sub, 1.0, 0.0)
    half = jnp.where(lane < sub, 1.0, jnp.where(lane == sub, 0.5, 0.0))

    def third_order(error):
        low = error * half
        lowb = low.astype(BF16)
        return (nn(lowb, lowb) + half * nt(lowb, lowb)) - low

    def begin():
        first = (third_order(scaled - eye) + eye) * (RESCALE**0.5)
        fb = first.astype(BF16)
        error = nt(nn(fb, scaled.astype(BF16)).astype(BF16), fb) - eye
        return nn((third_order(error) + eye).astype(BF16), fb)

    def step(t):
        ts = split(t)
        error = dot3(nt, split(dot3(nn, ts, split(scaled))), ts) - eye
        return t + nn(third_order(error).astype(BF16), ts[0]), squared(error)

    return begin, step


def inverse_factor(covariance, work, inverse, use):
    size = covariance.shape[0]
    lane = lax.broadcasted_iota(jnp.int32, (size, size), 1)
    sub = lax.broadcasted_iota(jnp.int32, (size, size), 0)
    on_diagonal = jnp.where(lane == sub, covariance, 0.0)
    scale_row = lax.rsqrt(jnp.sum(on_diagonal, axis=0, keepdims=True) * (1.0 / SCALE))
    scale_column = lax.rsqrt(jnp.sum(on_diagonal, axis=1, keepdims=True) * (1.0 / SCALE))
    scaled = covariance * scale_row * scale_column
    begin, step = newton(scaled)
    t, residual = step(begin())
    use(t * scale_row)

    @pl.when(jnp.logical_not(residual <= TOLERANCE**2))
    def _():
        inverse[...] = t

        def again(carry):
            better, left = step(inverse[...])
            inverse[...] = better
            return carry[0] + 1, left

        def wanted(carry):
            return (carry[0] < 6) & jnp.logical_not(carry[1] <= (0.2 * TOLERANCE) ** 2)

        _, left = lax.while_loop(wanted, again, (0, residual))
        inverse[...] = inverse[...] * scale_row

        @pl.when(jnp.logical_not(left <= (0.2 * TOLERANCE) ** 2))
        def _():
            eliminate(covariance, work, inverse)

        use(inverse[...])


def whiten(observed, tags, values, load, noise_ref, work, inverse, store):
    members = observed.shape[1]
    size = observed.shape[0]
    mean = row_mean(observed)
    parts = split(observed - mean)
    lane = lax.broadcasted_iota(jnp.int32, (size, size), 1)
    sub = lax.broadcasted_iota(jnp.int32, (size, size), 0)
    variance_row = jnp.where(tags == 0, 0.5, 2.0)
    variance = column(variance_row)
    mean_row = jnp.sum(jnp.where(lane == sub, mean, 0.0), axis=0, keepdims=True)
    covariance = dot3(nt, parts, parts) * (1.0 / (members - 1))
    covariance = covariance + jnp.where(lane == sub, variance, 0.0)
    exact = observed.astype(BF16)

    def finish(t):
        th, tl = split(t)
        nh, nl = split(t * jnp.sqrt(variance_row))
        applied = nn(th, exact) + nn(tl, exact)
        noise = nn(nh, noise_ref[...]) + nn(nl, noise_ref[...])
        mean_part = jnp.sum(t * mean_row, axis=1, keepdims=True)
        value_part = jnp.sum(t * values, axis=1, keepdims=True)
        store((applied - mean_part).astype(BF16), (noise + value_part - applied).astype(BF16))

    load.wait()
    inverse_factor(covariance, work, inverse, finish)


def update(state, whitened, white_innov):
    members = state.shape[1]
    sh, sl = split(state - row_mean(state))
    ph, plow = split(nt(sh, whitened) + nt(sl, whitened))
    return state + (nn(ph, white_innov) + nn(plow, white_innov)) * (1.0 / (members - 1))


def both_halves(place, own, other):
    own, other = own[...].astype(F32), other[...].astype(F32)
    first = place[0] % 2 == 0
    return jnp.concatenate(
        [jnp.where(first, own, other), jnp.where(first, other, own)], axis=1
    )


def first_kernel(
    place, tags, values, noise_ref, own, other, whitened, white_innov, noise, loads, work, inverse
):
    load = pltpu.make_async_copy(noise_ref.at[0], noise, loads.at[0])
    load.start()
    observed = both_halves(place, own, other)

    def store(w, v):
        whitened[...] = w
        white_innov[...] = v

    whiten(observed, tags[:1, :], values[:1, :], load, noise, work, inverse, store)


def second_kernel(
    place,
    tags,
    values,
    noise_ref,
    own,
    other,
    whitened,
    white_innov,
    state_ref,
    analysis,
    noise,
    loads,
    work,
    inverse,
    state,
):
    load = pltpu.make_async_copy(noise_ref.at[1], noise, loads.at[0])
    load_state = pltpu.make_async_copy(state_ref, state, loads.at[1])
    load_state.start()
    load.start()
    prior = both_halves(place, own, other) * UNIT
    w, v = whitened[...], white_innov[...]
    observed = rounded(update(prior, w, v))
    load_state.wait()
    first = update(state[...], w, v)

    def store(w, v):
        analysis[...] = update(first, w, v)

    whiten(observed, tags[1:2, :], values[1:2, :], load, noise, work, inverse, store)


def batch_call(kernel, name, outs, place, tags, values, noise, *arrays, state=()):
    rows, members = noise.shape[1:]
    return pl.pallas_call(
        kernel,
        out_shape=outs,
        in_specs=[SMEM, VMEM, VMEM, ANYWHERE] + [VMEM] * len(arrays) + [ANYWHERE] * len(state),
        out_specs=[VMEM] * len(outs),
        scratch_shapes=[
            pltpu.VMEM((rows, members), BF16),
            pltpu.SemaphoreType.DMA((2,)),
            pltpu.VMEM((rows, rows), F32),
            pltpu.VMEM((rows, rows), F32),
        ]
        + [pltpu.VMEM(array.shape, F32) for array in state],
        compiler_params=PARAMS,
        name=name,
    )(place, tags, values, noise, *arrays, *state)


def batches(place, tags, values, noise, state, observed, prior):
    shape = jax.ShapeDtypeStruct(noise.shape[1:], BF16)
    shared = (place, tags, values, noise)
    white = batch_call(first_kernel, "first_batch", [shape, shape], *shared, *observed)
    analysis = jax.ShapeDtypeStruct(state.shape, F32)
    return batch_call(
        second_kernel, "second_batch", [analysis], *shared, *prior, *white, state=(state,)
    )[0]


AXES = ("row", "col")
CORE, Y, X, NEAR_Z, FAR_Z = 1, 2, 4, 8, 16


def swap(value, mask):
    return lax.ppermute(value, AXES, [(i, i ^ mask) for i in range(32)])


def after(value, other):
    return lax.optimization_barrier((value, other))[0]


def joined(first, second):
    return jnp.concatenate([first, second], axis=0)


EARLY = (0, 4, 8, 12, 2, 10, 5, 13, 1, 9, 3, 11, 6, 7)
LATE = (14, 15)


def by_slots(place, ensemble, blocks, weights):
    keep, send = pick(place, blocks, weights, ensemble)
    own = (keep + swap(send, CORE))[None]
    far, near = swap(own, FAR_Z), swap(own, NEAR_Z)
    near_far = swap(far, NEAR_Z)
    both = joined(own, near)
    both_x = swap(both, X)
    far_y = swap(after(far, near), Y)
    near_far_y = swap(near_far, Y)
    both_y = swap(after(joined(both, both_x), near_far), Y)
    far_x = swap(joined(far, far_y), X)
    near_far_x = swap(joined(near_far, near_far_y), X)
    early_places, late_places, fits = order(place, blocks, (EARLY, LATE))
    pieces = [own, far, near, near_far, both_x, far_y, near_far_y, both_y, far_x]
    early = early_rows(early_places, pieces)
    return late_rows(late_places, early, [near_far_x]), fits


def add_by_swaps(value):
    for mask in (CORE, Y, X, NEAR_Z, FAR_Z):
        value = value + swap(value, mask)
    return value


def half_of(value, core):
    rows, members = value.shape
    return lax.dynamic_slice(value, (0, core * (members // 2)), (rows, members // 2))


def by_sum(add_up, other, place, ensemble, blocks, weights):
    rows = blocks.shape[1]
    codes = add_up(pick_all(place, blocks, weights, ensemble))
    codes = half_of(codes, (place[0] + other) % 2)
    return (codes[:rows] * UNIT).astype(BF16), codes[rows:].astype(jnp.int16)


def body(staged, ensemble, obs_blocks, obs_weights, comp_tags, obs_values, obs_noise):
    held = ensemble.shape[0] // obs_weights.shape[2]
    place = jnp.stack([lax.axis_index(AXES), held]).astype(jnp.int32)
    by_point = jnp.swapaxes(obs_weights, 1, 2)
    operands = (place, ensemble, obs_blocks, by_point)
    if staged:
        slotted, fits = by_slots(*operands)
        own = lax.cond(
            fits[0] == 1,
            lambda slotted, *operands: tuple(slotted),
            lambda slotted, *operands: by_sum(add_by_swaps, 0, *operands),
            slotted,
            *operands,
        )
        pairs = [(half, swap(half, CORE)) for half in own]
    else:
        add_up = lambda value: lax.psum(value, AXES)
        pairs = list(zip(by_sum(add_up, 0, *operands), by_sum(add_up, 1, *operands)))
    return batches(place, comp_tags, obs_values, obs_noise, ensemble, *pairs)


def solution(mesh):
    staged = (mesh.shape["row"], mesh.shape["col"]) == (8, 4)
    in_specs = (P(AXES, None), P(), P(), P(), P(), P())
    out_specs = P(AXES, None)
    return jax.shard_map(
        functools.partial(body, staged),
        mesh=mesh,
        in_specs=in_specs,
        out_specs=out_specs,
        check_vma=False,
    )
```

```python
import functools

import jax
import jax.numpy as jnp
from jax import lax
from jax.experimental import pallas as pl
from jax.experimental.pallas import tpu as pltpu
from jax.sharding import PartitionSpec as P

SLOTS = 64
LANES = 128
UNIT = 1.0 / 1024
SCALE = 0.6
RESCALE = 1.25
TOLERANCE = 0.25
BF16 = jnp.bfloat16
F32 = jnp.float32
VMEM = pl.BlockSpec(memory_space=pltpu.VMEM)
SMEM = pl.BlockSpec(memory_space=pltpu.SMEM)
ANYWHERE = pl.BlockSpec(memory_space=pl.ANY)
PARAMS = pltpu.CompilerParams(vmem_limit_bytes=40 * 1024 * 1024)


def nt(a, b):
    return lax.dot_general(a, b, (((1,), (1,)), ((), ())), preferred_element_type=F32)


def nn(a, b):
    return lax.dot_general(a, b, (((1,), (0,)), ((), ())), preferred_element_type=F32)


def split(a):
    high = a.astype(BF16)
    return high, (a - high.astype(F32)).astype(BF16)


def dot3(dot, a, b):
    (ah, al), (bh, bl) = a, b
    return dot(ah, bh) + (dot(ah, bl) + dot(al, bh))


def row_mean(a):
    return jnp.sum(a, axis=1, keepdims=True) * (1.0 / a.shape[1])


def column(row):
    size = row.shape[1]
    lane = lax.broadcasted_iota(jnp.int32, (size, size), 1)
    sub = lax.broadcasted_iota(jnp.int32, (size, size), 0)
    return jnp.sum(jnp.where(lane == sub, row, jnp.zeros_like(row)), axis=1, keepdims=True)


def both_ways(row):
    as_float = row.astype(F32)
    return as_float, column(as_float)


def select(lanes, points, local, weight):
    value = jnp.zeros(lanes.shape, F32)
    for point in range(points):
        value = jnp.where(lanes % points == point, weight[point], value)
    return jnp.where((lanes // points).astype(F32) == local, value, 0.0)


def rounded(value):
    return value.astype(BF16).astype(F32)


def three_parts(a):
    high = a.astype(BF16)
    rest = a - high.astype(F32)
    middle = rest.astype(BF16)
    return high, middle, (rest - middle.astype(F32)).astype(BF16)


def pick_kernel(place, blocks, weights, state_ref, keep, send, state, arrived):
    load = pltpu.make_async_copy(state_ref, state, arrived)
    load.start()
    device = place[0]
    batches, points, size = weights.shape
    width, members = state.shape
    held = width // points
    lane = lax.broadcasted_iota(jnp.int32, (size, size), 1)
    sub = lax.broadcasted_iota(jnp.int32, (size, size), 0)
    earlier = jnp.where(sub < lane, 1.0, 0.0).astype(BF16)
    row = blocks[...]
    mine = jnp.where(row // (2 * held) == device // 2, 1.0, 0.0)
    rank = nn(mine.astype(BF16), earlier).astype(jnp.int32)
    own = row // held == device
    slots = lax.broadcasted_iota(jnp.int32, (SLOTS, size), 0)
    points_of = lax.broadcasted_iota(jnp.int32, (width, size), 0)
    chosen, selector = [], []
    for batch in range(batches):
        place_of = rank[batch : batch + 1, :]
        place_of = place_of if batch == 0 else SLOTS - 1 - place_of
        place_of = jnp.where(own[batch : batch + 1, :], place_of, -1)
        chosen.append(jnp.where(slots == place_of, 1.0, 0.0))
        value = jnp.zeros((width, size), F32)
        for point in range(points):
            weight = weights[batch, point : point + 1, :]
            value = jnp.where(points_of % points == point, weight, value)
        local = row[batch : batch + 1, :] - device * held
        selector.append(jnp.where(points_of // points == local, value, 0.0))
    chosen = jnp.concatenate(chosen, axis=1).astype(BF16)
    parts = three_parts(jnp.concatenate(selector, axis=1))
    high, middle, low = [nt(chosen, part).astype(BF16) for part in parts]
    load.wait()
    top, mid, end = three_parts(state[...])
    rows = nn(high, end) + nn(middle, mid) + nn(low, top)
    rows = (nn(high, mid) + nn(middle, top)) + rows
    rows = nn(high, top) + rows
    from_first = lax.broadcasted_iota(jnp.int32, (SLOTS, 1), 0).astype(F32)
    from_first = from_first < jnp.sum(mine[:1, :], axis=1, keepdims=True)
    rows = jnp.where(from_first, rounded(rows), rows)
    code = jnp.round(rows * (1.0 / UNIT)).astype(jnp.int32)
    left, right = code[:, : members // 2], code[:, members // 2 :]
    first = device % 2 == 0
    keep[...] = jnp.where(first, left, right).astype(jnp.int16)
    send[...] = jnp.where(first, right, left).astype(jnp.int16)


def pick(place, blocks, weights, state):
    return pl.pallas_call(
        pick_kernel,
        out_shape=[jax.ShapeDtypeStruct((SLOTS, state.shape[1] // 2), jnp.int16)] * 2,
        in_specs=[SMEM, VMEM, VMEM, ANYWHERE],
        out_specs=[VMEM] * 2,
        scratch_shapes=[pltpu.VMEM(state.shape, F32), pltpu.SemaphoreType.DMA],
        compiler_params=PARAMS,
        name="pick",
    )(place, blocks, weights, state)


def pick_all_kernel(place, blocks, weights, state, out):
    device = place[0]
    batches, points, size = weights.shape
    width = state.shape[0]
    lanes = lax.broadcasted_iota(jnp.int32, (size, width), 1)
    for batch in range(batches):
        columns = [column(weights[batch, point : point + 1, :]) for point in range(points)]
        local = column((blocks[batch : batch + 1, :] - device * (width // points)).astype(F32))
        rows = jnp.dot(
            select(lanes, points, local, columns),
            state[...],
            precision=lax.Precision.HIGHEST,
            preferred_element_type=F32,
        )
        rows = rounded(rows) if batch == 0 else rows
        out[batch * size : (batch + 1) * size, :] = jnp.round(rows * (1.0 / UNIT))


def pick_all(place, blocks, weights, state):
    return pl.pallas_call(
        pick_all_kernel,
        out_shape=jax.ShapeDtypeStruct((blocks.size, state.shape[1]), F32),
        in_specs=[SMEM, VMEM, VMEM, VMEM],
        out_specs=VMEM,
        compiler_params=PARAMS,
        name="pick_all",
    )(place, blocks, weights, state)


def order_kernel(groups, place, blocks, *outs):
    outs, fits = outs[:-1], outs[-1]
    device, held = place[0], place[1]
    size = blocks.shape[1]
    lane = lax.broadcasted_iota(jnp.int32, (size, size), 1)
    sub = lax.broadcasted_iota(jnp.int32, (size, size), 0)
    lanes = lax.broadcasted_iota(jnp.int32, (size, LANES), 1)
    ones = jnp.ones((size, LANES), BF16)
    for batch in range(blocks.shape[0]):
        pair_row = (blocks[batch : batch + 1, :] // (2 * held)).astype(F32)
        pair = nn(jnp.where(lane == sub, pair_row, 0.0).astype(BF16), ones)
        wide = jnp.concatenate([pair] * (size // LANES), axis=1)
        before = jnp.where((pair_row == wide) & (lane < sub), 1.0, 0.0)
        rank = nn(before.astype(BF16), ones).astype(jnp.int32)
        away = (2 * pair.astype(jnp.int32)) ^ device
        distance = 8 * ((away >> 3) & 1) + 4 * ((away >> 4) & 1) + ((away >> 1) & 3)
        slot = rank if batch == 0 else SLOTS - 1 - rank
        for distances, out in zip(groups, outs):
            where = jnp.full(rank.shape, -SLOTS, jnp.int32)
            for index, known in enumerate(distances):
                where = jnp.where(distance == known, SLOTS * index, where)
            for start in range(0, out.shape[1], LANES):
                chosen = jnp.where(where + slot == lanes + start, 1.0, 0.0).astype(BF16)
                out[batch * size : (batch + 1) * size, start : start + LANES] = chosen
    counts = jnp.zeros((16, 1), F32)
    for batch in range(blocks.shape[0]):
        chip = blocks[batch : batch + 1, :] // (2 * held)
        chips = lax.broadcasted_iota(jnp.int32, (16, size), 0)
        counts = counts + jnp.sum(jnp.where(chips == chip, 1.0, 0.0), axis=1, keepdims=True)
    fits[0] = (jnp.max(counts) <= SLOTS).astype(jnp.int32)


def order(place, blocks, groups):
    return pl.pallas_call(
        functools.partial(order_kernel, groups),
        out_shape=[
            jax.ShapeDtypeStruct((blocks.size, SLOTS * len(group)), BF16) for group in groups
        ]
        + [jax.ShapeDtypeStruct((1,), jnp.int32)],
        in_specs=[SMEM, VMEM],
        out_specs=[VMEM] * len(groups) + [SMEM],
        compiler_params=PARAMS,
        cost_estimate=pl.CostEstimate(flops=10**6, bytes_accessed=10**6, transcendentals=0),
        name="order",
    )(place, blocks)


def put_in_order(chosen, pieces):
    size = chosen.shape[0] // 2
    values = jnp.concatenate([ref[...].reshape(-1, ref.shape[-1]) for ref in pieces], axis=0)
    high, low = split(values.astype(jnp.int32).astype(F32))
    second = chosen[size:, :]
    return nn(chosen[:size, :], high), nn(second, high) + nn(second, low)


def early_kernel(chosen, *refs):
    size = chosen.shape[0] // 2
    refs[-1][:size, :], refs[-1][size:, :] = put_in_order(chosen, refs[:-1])


def late_kernel(chosen, early, *refs):
    size = chosen.shape[0] // 2
    first, second = put_in_order(chosen, refs[:-2])
    refs[-2][...] = ((first + early[:size, :]) * UNIT).astype(BF16)
    refs[-1][...] = (second + early[size:, :]).astype(jnp.int32).astype(jnp.int16)


def early_rows(chosen, pieces):
    return pl.pallas_call(
        early_kernel,
        out_shape=jax.ShapeDtypeStruct((chosen.shape[0], pieces[0].shape[-1]), F32),
        in_specs=[VMEM] * (1 + len(pieces)),
        out_specs=VMEM,
        compiler_params=PARAMS,
        cost_estimate=pl.CostEstimate(flops=10**9, bytes_accessed=4 * 10**6, transcendentals=0),
        name="early_rows",
    )(chosen, *pieces)


def late_rows(chosen, early, pieces):
    shape = (early.shape[0] // 2, early.shape[1])
    return pl.pallas_call(
        late_kernel,
        out_shape=[jax.ShapeDtypeStruct(shape, BF16), jax.ShapeDtypeStruct(shape, jnp.int16)],
        in_specs=[VMEM] * (2 + len(pieces)),
        out_specs=[VMEM] * 2,
        compiler_params=PARAMS,
        name="late_rows",
    )(chosen, early, *pieces)


def eliminate(covariance, work, inverse):
    size = covariance.shape[0]
    lane = lax.broadcasted_iota(jnp.int32, (size, size), 1)
    sub = lax.broadcasted_iota(jnp.int32, (size, size), 0)
    work[...] = covariance
    inverse[...] = jnp.where(lane == sub, 1.0, 0.0)

    def step(k, carry):
        row = work[pl.ds(k, 1), :]
        current = work[...]
        pivot = jnp.sum(jnp.where(lane[:1] == k, row, 0.0), axis=1, keepdims=True)
        column = jnp.sum(jnp.where(lane == k, current, 0.0), axis=1, keepdims=True)
        factor = jnp.where(sub[:, :1] > k, column / pivot, 0.0)
        inverse_row = inverse[pl.ds(k, 1), :]
        work[...] = current - factor * row
        inverse[...] = inverse[...] - factor * inverse_row
        return carry

    lax.fori_loop(0, size, step, 0)
    pivots = jnp.sum(jnp.where(lane == sub, work[...], 0.0), axis=1, keepdims=True)
    inverse[...] = inverse[...] * (1.0 / jnp.sqrt(pivots))


def squared(a):
    return jnp.sum(a * a)


def newton(scaled):
    size = scaled.shape[0]
    lane = lax.broadcasted_iota(jnp.int32, (size, size), 1)
    sub = lax.broadcasted_iota(jnp.int32, (size, size), 0)
    eye = jnp.where(lane == sub, 1.0, 0.0)
    half = jnp.where(lane < sub, 1.0, jnp.where(lane == sub, 0.5, 0.0))

    def third_order(error):
        low = error * half
        lowb = low.astype(BF16)
        return (nn(lowb, lowb) + half * nt(lowb, lowb)) - low

    def begin():
        first = (third_order(scaled - eye) + eye) * (RESCALE**0.5)
        fb = first.astype(BF16)
        error = nt(nn(fb, scaled.astype(BF16)).astype(BF16), fb) - eye
        return nn((third_order(error) + eye).astype(BF16), fb)

    def step(t):
        ts = split(t)
        error = dot3(nt, split(dot3(nn, ts, split(scaled))), ts) - eye
        return t + nn(third_order(error).astype(BF16), ts[0]), squared(error)

    return begin, step


def inverse_factor(covariance, work, inverse, use):
    size = covariance.shape[0]
    lane = lax.broadcasted_iota(jnp.int32, (size, size), 1)
    sub = lax.broadcasted_iota(jnp.int32, (size, size), 0)
    on_diagonal = jnp.where(lane == sub, covariance, 0.0)
    scale_row = lax.rsqrt(jnp.sum(on_diagonal, axis=0, keepdims=True) * (1.0 / SCALE))
    scale_column = lax.rsqrt(jnp.sum(on_diagonal, axis=1, keepdims=True) * (1.0 / SCALE))
    scaled = covariance * scale_row * scale_column
    begin, step = newton(scaled)
    t, residual = step(begin())
    use(t * scale_row)

    @pl.when(jnp.logical_not(residual <= TOLERANCE**2))
    def _():
        inverse[...] = t

        def again(carry):
            better, left = step(inverse[...])
            inverse[...] = better
            return carry[0] + 1, left

        def wanted(carry):
            return (carry[0] < 6) & jnp.logical_not(carry[1] <= (0.2 * TOLERANCE) ** 2)

        _, left = lax.while_loop(wanted, again, (0, residual))
        inverse[...] = inverse[...] * scale_row

        @pl.when(jnp.logical_not(left <= (0.2 * TOLERANCE) ** 2))
        def _():
            eliminate(covariance, work, inverse)

        use(inverse[...])


def whiten(observed, tags, values, load, noise_ref, work, inverse, store):
    members = observed.shape[1]
    size = observed.shape[0]
    mean = row_mean(observed)
    lane = lax.broadcasted_iota(jnp.int32, (size, size), 1)
    sub = lax.broadcasted_iota(jnp.int32, (size, size), 0)
    variance_row = jnp.where(tags == 0, 0.5, 2.0)
    mean_row = jnp.sum(jnp.where(lane == sub, mean, 0.0), axis=0, keepdims=True)
    exact = observed.astype(BF16)
    covariance = (nt(exact, exact) - mean * (mean_row * members)) * (1.0 / (members - 1))
    covariance = covariance + jnp.where(lane == sub, variance_row, 0.0)

    def finish(t):
        th, tl = split(t)
        nh, nl = split(t * jnp.sqrt(variance_row))
        applied = nn(th, exact) + nn(tl, exact)
        noise = nn(nh, noise_ref[...]) + nn(nl, noise_ref[...])
        mean_part = jnp.sum(t * mean_row, axis=1, keepdims=True)
        value_part = jnp.sum(t * values, axis=1, keepdims=True)
        store((applied - mean_part).astype(BF16), (noise + value_part - applied).astype(BF16))

    load.wait()
    inverse_factor(covariance, work, inverse, finish)


def row_sums(array):
    return nt(jnp.ones((8, array.shape[1]), BF16), array)[:1, :]


def update(state, whitened, white_innov):
    members = state.shape[1]
    sh, sl = split(state)
    projected = nt(sh, whitened) + nt(sl, whitened) - row_mean(state) * row_sums(whitened)
    ph, plow = split(projected)
    return state + (nn(ph, white_innov) + nn(plow, white_innov)) * (1.0 / (members - 1))


def both_halves(place, own, other):
    own, other = own[...].astype(F32), other[...].astype(F32)
    first = place[0] % 2 == 0
    return jnp.concatenate(
        [jnp.where(first, own, other), jnp.where(first, other, own)], axis=1
    )


def first_kernel(
    place, tags, values, noise_ref, own, other, whitened, white_innov, noise, loads, work, inverse
):
    load = pltpu.make_async_copy(noise_ref.at[0], noise, loads.at[0])
    load.start()
    observed = both_halves(place, own, other)

    def store(w, v):
        whitened[...] = w
        white_innov[...] = v

    whiten(observed, tags[:1, :], values[:1, :], load, noise, work, inverse, store)


def second_kernel(
    place,
    tags,
    values,
    noise_ref,
    own,
    other,
    whitened,
    white_innov,
    state_ref,
    analysis,
    noise,
    loads,
    work,
    inverse,
    state,
):
    load = pltpu.make_async_copy(noise_ref.at[1], noise, loads.at[0])
    load_state = pltpu.make_async_copy(state_ref, state, loads.at[1])
    load_state.start()
    load.start()
    w, v = whitened[...], white_innov[...]
    observed = rounded(update(both_halves(place, own, other), w, v) * UNIT)
    load_state.wait()
    first = update(state[...], w, v)

    def store(w, v):
        analysis[...] = update(first, w, v)

    whiten(observed, tags[1:2, :], values[1:2, :], load, noise, work, inverse, store)


def batch_call(kernel, name, outs, place, tags, values, noise, *arrays, state=()):
    rows, members = noise.shape[1:]
    return pl.pallas_call(
        kernel,
        out_shape=outs,
        in_specs=[SMEM, VMEM, VMEM, ANYWHERE] + [VMEM] * len(arrays) + [ANYWHERE] * len(state),
        out_specs=[VMEM] * len(outs),
        scratch_shapes=[
            pltpu.VMEM((rows, members), BF16),
            pltpu.SemaphoreType.DMA((2,)),
            pltpu.VMEM((rows, rows), F32),
            pltpu.VMEM((rows, rows), F32),
        ]
        + [pltpu.VMEM(array.shape, F32) for array in state],
        compiler_params=PARAMS,
        name=name,
    )(place, tags, values, noise, *arrays, *state)


def batches(place, tags, values, noise, state, observed, prior):
    shape = jax.ShapeDtypeStruct(noise.shape[1:], BF16)
    shared = (place, tags, values, noise)
    white = batch_call(first_kernel, "first_batch", [shape, shape], *shared, *observed)
    analysis = jax.ShapeDtypeStruct(state.shape, F32)
    return batch_call(
        second_kernel, "second_batch", [analysis], *shared, *prior, *white, state=(state,)
    )[0]


AXES = ("row", "col")
CORE, Y, X, NEAR_Z, FAR_Z = 1, 2, 4, 8, 16


def swap(value, mask):
    return lax.ppermute(value, AXES, [(i, i ^ mask) for i in range(32)])


def after(value, other):
    return lax.optimization_barrier((value, other))[0]


def joined(first, second):
    return jnp.concatenate([first, second], axis=0)


EARLY = (0, 4, 8, 12, 2, 10, 5, 1, 13, 9, 3, 11, 6, 7)
LATE = (14, 15)


def by_slots(place, ensemble, blocks, weights):
    keep, send = pick(place, blocks, weights, ensemble)
    own = (keep + swap(send, CORE))[None]
    far, near = swap(own, FAR_Z), swap(own, NEAR_Z)
    near_far = swap(far, NEAR_Z)
    both = joined(own, near)
    both_x = swap(both, X)
    far_y = swap(after(joined(far, own), near), Y)
    near_far_y = swap(near_far, Y)
    both_y = swap(after(joined(near, both_x), near_far), Y)
    far_x = swap(joined(far, far_y[:1]), X)
    near_far_x = swap(joined(near_far, near_far_y), X)
    early_places, late_places, fits = order(place, blocks, (EARLY, LATE))
    pieces = [own, far, near, near_far, both_x, far_y, near_far_y, both_y, far_x]
    early = early_rows(early_places, pieces)
    return late_rows(late_places, early, [near_far_x]), fits


def add_by_swaps(value):
    for mask in (CORE, Y, X, NEAR_Z, FAR_Z):
        value = value + swap(value, mask)
    return value


def half_of(value, core):
    rows, members = value.shape
    return lax.dynamic_slice(value, (0, core * (members // 2)), (rows, members // 2))


def by_sum(add_up, other, place, ensemble, blocks, weights):
    rows = blocks.shape[1]
    codes = add_up(pick_all(place, blocks, weights, ensemble))
    codes = half_of(codes, (place[0] + other) % 2)
    return (codes[:rows] * UNIT).astype(BF16), codes[rows:].astype(jnp.int16)


def body(staged, ensemble, obs_blocks, obs_weights, comp_tags, obs_values, obs_noise):
    held = ensemble.shape[0] // obs_weights.shape[2]
    place = jnp.stack([lax.axis_index(AXES), held]).astype(jnp.int32)
    by_point = jnp.swapaxes(obs_weights, 1, 2)
    operands = (place, ensemble, obs_blocks, by_point)
    if staged:
        slotted, fits = by_slots(*operands)
        own = lax.cond(
            fits[0] == 1,
            lambda slotted, *operands: tuple(slotted),
            lambda slotted, *operands: by_sum(add_by_swaps, 0, *operands),
            slotted,
            *operands,
        )
        pairs = [(half, swap(half, CORE)) for half in own]
    else:
        add_up = lambda value: lax.psum(value, AXES)
        pairs = list(zip(by_sum(add_up, 0, *operands), by_sum(add_up, 1, *operands)))
    return batches(place, comp_tags, obs_values, obs_noise, ensemble, *pairs)


def solution(mesh):
    staged = (mesh.shape["row"], mesh.shape["col"]) == (8, 4)
    in_specs = (P(AXES, None), P(), P(), P(), P(), P())
    out_specs = P(AXES, None)
    return jax.shard_map(
        functools.partial(body, staged),
        mesh=mesh,
        in_specs=in_specs,
        out_specs=out_specs,
        check_vma=False,
    )
```

```python
import functools

import jax
import jax.numpy as jnp
from jax import lax
from jax.experimental import pallas as pl
from jax.experimental.pallas import tpu as pltpu
from jax.sharding import PartitionSpec as P

SLOTS = 64
UNIT = 1.0 / 1024
SCALE = 0.6
RESCALE = 1.25
TOLERANCE = 0.25
BF16 = jnp.bfloat16
F32 = jnp.float32
VMEM = pl.BlockSpec(memory_space=pltpu.VMEM)
SMEM = pl.BlockSpec(memory_space=pltpu.SMEM)
ANYWHERE = pl.BlockSpec(memory_space=pl.ANY)
PARAMS = pltpu.CompilerParams(vmem_limit_bytes=40 * 1024 * 1024)


def nt(a, b):
    return lax.dot_general(a, b, (((1,), (1,)), ((), ())), preferred_element_type=F32)


def nn(a, b):
    return lax.dot_general(a, b, (((1,), (0,)), ((), ())), preferred_element_type=F32)


def split(a):
    high = a.astype(BF16)
    return high, (a - high.astype(F32)).astype(BF16)


def dot2(dot, a, b):
    rows = a[0].shape[0]
    both = dot(jnp.concatenate(a, axis=0), b)
    return both[:rows] + both[rows:]


def dot3(dot, a, b):
    return dot2(dot, a, b[0]) + dot(a[0], b[1])


def row_mean(a):
    return jnp.sum(a, axis=1, keepdims=True) * (1.0 / a.shape[1])


def column(row):
    size = row.shape[1]
    lane = lax.broadcasted_iota(jnp.int32, (size, size), 1)
    sub = lax.broadcasted_iota(jnp.int32, (size, size), 0)
    return jnp.sum(jnp.where(lane == sub, row, jnp.zeros_like(row)), axis=1, keepdims=True)


def both_ways(row):
    as_float = row.astype(F32)
    return as_float, column(as_float)


def select(lanes, points, local, weight):
    value = jnp.zeros(lanes.shape, F32)
    for point in range(points):
        value = jnp.where(lanes % points == point, weight[point], value)
    return jnp.where((lanes // points).astype(F32) == local, value, 0.0)


def rounded(value):
    return value.astype(BF16).astype(F32)


def three_parts(a):
    high = a.astype(BF16)
    rest = a - high.astype(F32)
    middle = rest.astype(BF16)
    return high, middle, (rest - middle.astype(F32)).astype(BF16)


def pick_kernel(place, blocks, weights, state_ref, keep, send, state, arrived):
    load = pltpu.make_async_copy(state_ref, state, arrived)
    load.start()
    device = place[0]
    batches, points, size = weights.shape
    width, members = state.shape
    held = width // points
    lane = lax.broadcasted_iota(jnp.int32, (size, size), 1)
    sub = lax.broadcasted_iota(jnp.int32, (size, size), 0)
    earlier = jnp.where(sub < lane, 1.0, 0.0).astype(BF16)
    row = blocks[...]
    mine = jnp.where(row // (2 * held) == device // 2, 1.0, 0.0)
    rank = nn(mine.astype(BF16), earlier).astype(jnp.int32)
    own = row // held == device
    slots = lax.broadcasted_iota(jnp.int32, (SLOTS, size), 0)
    points_of = lax.broadcasted_iota(jnp.int32, (width, size), 0)
    chosen, selector = [], []
    for batch in range(batches):
        place_of = rank[batch : batch + 1, :]
        place_of = place_of if batch == 0 else SLOTS - 1 - place_of
        place_of = jnp.where(own[batch : batch + 1, :], place_of, -1)
        chosen.append(jnp.where(slots == place_of, 1.0, 0.0))
        value = jnp.zeros((width, size), F32)
        for point in range(points):
            weight = weights[batch, point : point + 1, :]
            value = jnp.where(points_of % points == point, weight, value)
        local = row[batch : batch + 1, :] - device * held
        selector.append(jnp.where(points_of // points == local, value, 0.0))
    chosen = jnp.concatenate(chosen, axis=1).astype(BF16)
    parts = three_parts(jnp.concatenate(selector, axis=1))
    high, middle, low = [nt(chosen, part).astype(BF16) for part in parts]
    load.wait()
    top, mid, end = three_parts(state[...])
    rows = nn(high, end) + nn(middle, mid) + nn(low, top)
    rows = (nn(high, mid) + nn(middle, top)) + rows
    rows = nn(high, top) + rows
    from_first = lax.broadcasted_iota(jnp.int32, (SLOTS, 1), 0).astype(F32)
    from_first = from_first < jnp.sum(mine[:1, :], axis=1, keepdims=True)
    rows = jnp.where(from_first, rounded(rows), rows)
    code = jnp.round(rows * (1.0 / UNIT)).astype(jnp.int32)
    left, right = code[:, : members // 2], code[:, members // 2 :]
    first = device % 2 == 0
    keep[...] = jnp.where(first, left, right).astype(jnp.int16)
    send[...] = jnp.where(first, right, left).astype(jnp.int16)


def pick(place, blocks, weights, state):
    return pl.pallas_call(
        pick_kernel,
        out_shape=[jax.ShapeDtypeStruct((SLOTS, state.shape[1] // 2), jnp.int16)] * 2,
        in_specs=[SMEM, VMEM, VMEM, ANYWHERE],
        out_specs=[VMEM] * 2,
        scratch_shapes=[pltpu.VMEM(state.shape, F32), pltpu.SemaphoreType.DMA],
        compiler_params=PARAMS,
        name="pick",
    )(place, blocks, weights, state)


def pick_all_kernel(place, blocks, weights, state, out):
    device = place[0]
    batches, points, size = weights.shape
    width = state.shape[0]
    lanes = lax.broadcasted_iota(jnp.int32, (size, width), 1)
    for batch in range(batches):
        columns = [column(weights[batch, point : point + 1, :]) for point in range(points)]
        local = column((blocks[batch : batch + 1, :] - device * (width // points)).astype(F32))
        rows = jnp.dot(
            select(lanes, points, local, columns),
            state[...],
            precision=lax.Precision.HIGHEST,
            preferred_element_type=F32,
        )
        rows = rounded(rows) if batch == 0 else rows
        out[batch * size : (batch + 1) * size, :] = jnp.round(rows * (1.0 / UNIT))


def pick_all(place, blocks, weights, state):
    return pl.pallas_call(
        pick_all_kernel,
        out_shape=jax.ShapeDtypeStruct((blocks.size, state.shape[1]), F32),
        in_specs=[SMEM, VMEM, VMEM, VMEM],
        out_specs=VMEM,
        compiler_params=PARAMS,
        name="pick_all",
    )(place, blocks, weights, state)


def order_kernel(groups, place, blocks, *outs):
    outs, fits = outs[:-1], outs[-1]
    device, held = place[0], place[1]
    size = blocks.shape[1]
    lane = lax.broadcasted_iota(jnp.int32, (size, size), 1)
    sub = lax.broadcasted_iota(jnp.int32, (size, size), 0)
    for batch in range(blocks.shape[0]):
        pair_row, pair_column = both_ways(blocks[batch : batch + 1, :] // (2 * held))
        before = jnp.where((pair_row == pair_column) & (lane < sub), 1.0, 0.0)
        rank = jnp.sum(before, axis=1, keepdims=True).astype(jnp.int32)
        away = (2 * pair_column.astype(jnp.int32)) ^ device
        distance = 8 * ((away >> 3) & 1) + 4 * ((away >> 4) & 1) + ((away >> 1) & 3)
        slot = rank if batch == 0 else SLOTS - 1 - rank
        for distances, out in zip(groups, outs):
            where = jnp.full(rank.shape, -SLOTS, jnp.int32)
            for index, known in enumerate(distances):
                where = jnp.where(distance == known, SLOTS * index, where)
            slots = lax.broadcasted_iota(jnp.int32, (size, out.shape[1]), 1)
            chosen = jnp.where(slots == where + slot, 1.0, 0.0)
            out[batch * size : (batch + 1) * size, :] = chosen.astype(BF16)
    counts = jnp.zeros((16, 1), F32)
    for batch in range(blocks.shape[0]):
        chip = blocks[batch : batch + 1, :] // (2 * held)
        chips = lax.broadcasted_iota(jnp.int32, (16, size), 0)
        counts = counts + jnp.sum(jnp.where(chips == chip, 1.0, 0.0), axis=1, keepdims=True)
    fits[0] = (jnp.max(counts) <= SLOTS).astype(jnp.int32)


def order(place, blocks, groups):
    return pl.pallas_call(
        functools.partial(order_kernel, groups),
        out_shape=[
            jax.ShapeDtypeStruct((blocks.size, SLOTS * len(group)), BF16) for group in groups
        ]
        + [jax.ShapeDtypeStruct((1,), jnp.int32)],
        in_specs=[SMEM, VMEM],
        out_specs=[VMEM] * len(groups) + [SMEM],
        compiler_params=PARAMS,
        cost_estimate=pl.CostEstimate(flops=10**6, bytes_accessed=10**6, transcendentals=0),
        name="order",
    )(place, blocks)


def put_in_order(chosen, pieces):
    size = chosen.shape[0] // 2
    values = jnp.concatenate([ref[...].reshape(-1, ref.shape[-1]) for ref in pieces], axis=0)
    high, low = split(values.astype(jnp.int32).astype(F32))
    second = chosen[size:, :]
    return nn(chosen[:size, :], high), nn(second, high) + nn(second, low)


def early_kernel(chosen, *refs):
    size = chosen.shape[0] // 2
    refs[-1][:size, :], refs[-1][size:, :] = put_in_order(chosen, refs[:-1])


def late_kernel(chosen, early, *refs):
    size = chosen.shape[0] // 2
    first, second = put_in_order(chosen, refs[:-2])
    refs[-2][...] = ((first + early[:size, :]) * UNIT).astype(BF16)
    refs[-1][...] = (second + early[size:, :]).astype(jnp.int32).astype(jnp.int16)


def early_rows(chosen, pieces):
    return pl.pallas_call(
        early_kernel,
        out_shape=jax.ShapeDtypeStruct((chosen.shape[0], pieces[0].shape[-1]), F32),
        in_specs=[VMEM] * (1 + len(pieces)),
        out_specs=VMEM,
        compiler_params=PARAMS,
        cost_estimate=pl.CostEstimate(flops=10**9, bytes_accessed=4 * 10**6, transcendentals=0),
        name="early_rows",
    )(chosen, *pieces)


def late_rows(chosen, early, pieces):
    shape = (early.shape[0] // 2, early.shape[1])
    return pl.pallas_call(
        late_kernel,
        out_shape=[jax.ShapeDtypeStruct(shape, BF16), jax.ShapeDtypeStruct(shape, jnp.int16)],
        in_specs=[VMEM] * (2 + len(pieces)),
        out_specs=[VMEM] * 2,
        compiler_params=PARAMS,
        name="late_rows",
    )(chosen, early, *pieces)


def eliminate(covariance, work, inverse):
    size = covariance.shape[0]
    lane = lax.broadcasted_iota(jnp.int32, (size, size), 1)
    sub = lax.broadcasted_iota(jnp.int32, (size, size), 0)
    work[...] = covariance
    inverse[...] = jnp.where(lane == sub, 1.0, 0.0)

    def step(k, carry):
        row = work[pl.ds(k, 1), :]
        current = work[...]
        pivot = jnp.sum(jnp.where(lane[:1] == k, row, 0.0), axis=1, keepdims=True)
        column = jnp.sum(jnp.where(lane == k, current, 0.0), axis=1, keepdims=True)
        factor = jnp.where(sub[:, :1] > k, column / pivot, 0.0)
        inverse_row = inverse[pl.ds(k, 1), :]
        work[...] = current - factor * row
        inverse[...] = inverse[...] - factor * inverse_row
        return carry

    lax.fori_loop(0, size, step, 0)
    pivots = jnp.sum(jnp.where(lane == sub, work[...], 0.0), axis=1, keepdims=True)
    inverse[...] = inverse[...] * (1.0 / jnp.sqrt(pivots))


def squared(a):
    return jnp.sum(a * a)


def newton(scaled):
    size = scaled.shape[0]
    lane = lax.broadcasted_iota(jnp.int32, (size, size), 1)
    sub = lax.broadcasted_iota(jnp.int32, (size, size), 0)
    eye = jnp.where(lane == sub, 1.0, 0.0)
    half = jnp.where(lane < sub, 1.0, jnp.where(lane == sub, 0.5, 0.0))

    def third_order(error):
        low = error * half
        lowb = low.astype(BF16)
        return (nn(lowb, lowb) + half * nt(lowb, lowb)) - low

    def begin():
        first = (third_order(scaled - eye) + eye) * (RESCALE**0.5)
        fb = first.astype(BF16)
        error = nt(nn(fb, scaled.astype(BF16)).astype(BF16), fb) - eye
        return nn((third_order(error) + eye).astype(BF16), fb)

    def step(t):
        ts = split(t)
        error = dot3(nt, split(dot3(nn, ts, split(scaled))), ts) - eye
        return t + nn(third_order(error).astype(BF16), ts[0]), squared(error)

    return begin, step


def inverse_factor(covariance, work, inverse, use):
    size = covariance.shape[0]
    lane = lax.broadcasted_iota(jnp.int32, (size, size), 1)
    sub = lax.broadcasted_iota(jnp.int32, (size, size), 0)
    on_diagonal = jnp.where(lane == sub, covariance, 0.0)
    scale_row = lax.rsqrt(jnp.sum(on_diagonal, axis=0, keepdims=True) * (1.0 / SCALE))
    scale_column = lax.rsqrt(jnp.sum(on_diagonal, axis=1, keepdims=True) * (1.0 / SCALE))
    scaled = covariance * scale_row * scale_column
    begin, step = newton(scaled)
    t, residual = step(begin())
    use(t * scale_row)

    @pl.when(jnp.logical_not(residual <= TOLERANCE**2))
    def _():
        inverse[...] = t

        def again(carry):
            better, left = step(inverse[...])
            inverse[...] = better
            return carry[0] + 1, left

        def wanted(carry):
            return (carry[0] < 6) & jnp.logical_not(carry[1] <= (0.2 * TOLERANCE) ** 2)

        _, left = lax.while_loop(wanted, again, (0, residual))
        inverse[...] = inverse[...] * scale_row

        @pl.when(jnp.logical_not(left <= (0.2 * TOLERANCE) ** 2))
        def _():
            eliminate(covariance, work, inverse)

        use(inverse[...])


def whiten(observed, tags, values, load, noise_ref, work, inverse, store):
    members = observed.shape[1]
    size = observed.shape[0]
    mean = row_mean(observed)
    lane = lax.broadcasted_iota(jnp.int32, (size, size), 1)
    sub = lax.broadcasted_iota(jnp.int32, (size, size), 0)
    variance_row = jnp.where(tags == 0, 0.5, 2.0)
    mean_row = jnp.sum(jnp.where(lane == sub, mean, 0.0), axis=0, keepdims=True)
    exact = observed.astype(BF16)
    covariance = (nt(exact, exact) - mean * (mean_row * members)) * (1.0 / (members - 1))
    covariance = covariance + jnp.where(lane == sub, variance_row, 0.0)

    def finish(t):
        applied = dot2(nn, split(t), exact)
        noise = dot2(nn, split(t * jnp.sqrt(variance_row)), noise_ref[...])
        mean_part = jnp.sum(t * mean_row, axis=1, keepdims=True)
        value_part = jnp.sum(t * values, axis=1, keepdims=True)
        store((applied - mean_part).astype(BF16), (noise + value_part - applied).astype(BF16))

    load.wait()
    inverse_factor(covariance, work, inverse, finish)


def row_sums(array):
    return nt(jnp.ones((8, array.shape[1]), BF16), array)[:1, :]


def update(state, whitened, white_innov):
    members = state.shape[1]
    projected = dot2(nt, split(state), whitened) - row_mean(state) * row_sums(whitened)
    return state + dot2(nn, split(projected), white_innov) * (1.0 / (members - 1))


def both_halves(place, own, other):
    own, other = own[...].astype(F32), other[...].astype(F32)
    first = place[0] % 2 == 0
    return jnp.concatenate(
        [jnp.where(first, own, other), jnp.where(first, other, own)], axis=1
    )


def first_kernel(
    place, tags, values, noise_ref, own, other, whitened, white_innov, noise, loads, work, inverse
):
    load = pltpu.make_async_copy(noise_ref.at[0], noise, loads.at[0])
    load.start()
    observed = both_halves(place, own, other)

    def store(w, v):
        whitened[...] = w
        white_innov[...] = v

    whiten(observed, tags[:1, :], values[:1, :], load, noise, work, inverse, store)


def second_kernel(
    place,
    tags,
    values,
    noise_ref,
    own,
    other,
    whitened,
    white_innov,
    state_ref,
    analysis,
    noise,
    loads,
    work,
    inverse,
    state,
):
    load = pltpu.make_async_copy(noise_ref.at[1], noise, loads.at[0])
    load_state = pltpu.make_async_copy(state_ref, state, loads.at[1])
    load_state.start()
    load.start()
    w, v = whitened[...], white_innov[...]
    observed = rounded(update(both_halves(place, own, other), w, v) * UNIT)
    load_state.wait()
    first = update(state[...], w, v)

    def store(w, v):
        analysis[...] = update(first, w, v)

    whiten(observed, tags[1:2, :], values[1:2, :], load, noise, work, inverse, store)


def batch_call(kernel, name, outs, place, tags, values, noise, *arrays, state=()):
    rows, members = noise.shape[1:]
    return pl.pallas_call(
        kernel,
        out_shape=outs,
        in_specs=[SMEM, VMEM, VMEM, ANYWHERE] + [VMEM] * len(arrays) + [ANYWHERE] * len(state),
        out_specs=[VMEM] * len(outs),
        scratch_shapes=[
            pltpu.VMEM((rows, members), BF16),
            pltpu.SemaphoreType.DMA((2,)),
            pltpu.VMEM((rows, rows), F32),
            pltpu.VMEM((rows, rows), F32),
        ]
        + [pltpu.VMEM(array.shape, F32) for array in state],
        compiler_params=PARAMS,
        name=name,
    )(place, tags, values, noise, *arrays, *state)


def batches(place, tags, values, noise, state, observed, prior):
    shape = jax.ShapeDtypeStruct(noise.shape[1:], BF16)
    shared = (place, tags, values, noise)
    white = batch_call(first_kernel, "first_batch", [shape, shape], *shared, *observed)
    analysis = jax.ShapeDtypeStruct(state.shape, F32)
    return batch_call(
        second_kernel, "second_batch", [analysis], *shared, *prior, *white, state=(state,)
    )[0]


AXES = ("row", "col")
CORE, Y, X, NEAR_Z, FAR_Z = 1, 2, 4, 8, 16


def swap(value, mask):
    return lax.ppermute(value, AXES, [(i, i ^ mask) for i in range(32)])


def after(value, other):
    return lax.optimization_barrier((value, other))[0]


def joined(first, second):
    return jnp.concatenate([first, second], axis=0)


EARLY = (0, 4, 8, 12, 2, 10, 5, 13, 1, 9, 3, 11, 6, 7)
LATE = (14, 15)


def by_slots(place, ensemble, blocks, weights):
    keep, send = pick(place, blocks, weights, ensemble)
    own = (keep + swap(send, CORE))[None]
    far, near = swap(own, FAR_Z), swap(own, NEAR_Z)
    near_far = swap(far, NEAR_Z)
    both = joined(own, near)
    both_x = swap(both, X)
    far_y = swap(after(far, near), Y)
    near_far_y = swap(near_far, Y)
    both_y = swap(after(joined(both, both_x), near_far), Y)
    far_x = swap(joined(far, far_y), X)
    near_far_x = swap(joined(near_far, near_far_y), X)
    early_places, late_places, fits = order(place, blocks, (EARLY, LATE))
    pieces = [own, far, near, near_far, both_x, far_y, near_far_y, both_y, far_x]
    early = early_rows(early_places, pieces)
    return late_rows(late_places, early, [near_far_x]), fits


def add_by_swaps(value):
    for mask in (CORE, Y, X, NEAR_Z, FAR_Z):
        value = value + swap(value, mask)
    return value


def half_of(value, core):
    rows, members = value.shape
    return lax.dynamic_slice(value, (0, core * (members // 2)), (rows, members // 2))


def by_sum(add_up, other, place, ensemble, blocks, weights):
    rows = blocks.shape[1]
    codes = add_up(pick_all(place, blocks, weights, ensemble))
    codes = half_of(codes, (place[0] + other) % 2)
    return (codes[:rows] * UNIT).astype(BF16), codes[rows:].astype(jnp.int16)


def body(staged, ensemble, obs_blocks, obs_weights, comp_tags, obs_values, obs_noise):
    held = ensemble.shape[0] // obs_weights.shape[2]
    place = jnp.stack([lax.axis_index(AXES), held]).astype(jnp.int32)
    by_point = jnp.swapaxes(obs_weights, 1, 2)
    operands = (place, ensemble, obs_blocks, by_point)
    if staged:
        slotted, fits = by_slots(*operands)
        own = lax.cond(
            fits[0] == 1,
            lambda slotted, *operands: tuple(slotted),
            lambda slotted, *operands: by_sum(add_by_swaps, 0, *operands),
            slotted,
            *operands,
        )
        pairs = [(half, swap(half, CORE)) for half in own]
    else:
        add_up = lambda value: lax.psum(value, AXES)
        pairs = list(zip(by_sum(add_up, 0, *operands), by_sum(add_up, 1, *operands)))
    return batches(place, comp_tags, obs_values, obs_noise, ensemble, *pairs)


def solution(mesh):
    staged = (mesh.shape["row"], mesh.shape["col"]) == (8, 4)
    in_specs = (P(AXES, None), P(), P(), P(), P(), P())
    out_specs = P(AXES, None)
    return jax.shard_map(
        functools.partial(body, staged),
        mesh=mesh,
        in_specs=in_specs,
        out_specs=out_specs,
        check_vma=False,
    )
```

```python
import functools

import jax
import jax.numpy as jnp
from jax import lax
from jax.experimental import pallas as pl
from jax.experimental.pallas import tpu as pltpu
from jax.sharding import PartitionSpec as P

SLOTS = 56
UNIT = 1.0 / 1024
SCALE = 0.6
RESCALE = 1.25
TOLERANCE = 0.25
BF16 = jnp.bfloat16
F32 = jnp.float32
VMEM = pl.BlockSpec(memory_space=pltpu.VMEM)
SMEM = pl.BlockSpec(memory_space=pltpu.SMEM)
ANYWHERE = pl.BlockSpec(memory_space=pl.ANY)
PARAMS = pltpu.CompilerParams(vmem_limit_bytes=40 * 1024 * 1024)


def nt(a, b):
    return lax.dot_general(a, b, (((1,), (1,)), ((), ())), preferred_element_type=F32)


def nn(a, b):
    return lax.dot_general(a, b, (((1,), (0,)), ((), ())), preferred_element_type=F32)


def split(a):
    high = a.astype(BF16)
    return high, (a - high.astype(F32)).astype(BF16)


def dot2(dot, a, b):
    rows = a[0].shape[0]
    both = dot(jnp.concatenate(a, axis=0), b)
    return both[:rows] + both[rows:]


def dot3(dot, a, b):
    return dot2(dot, a, b[0]) + dot(a[0], b[1])


def row_mean(a):
    return jnp.sum(a, axis=1, keepdims=True) * (1.0 / a.shape[1])


def column(row):
    size = row.shape[1]
    lane = lax.broadcasted_iota(jnp.int32, (size, size), 1)
    sub = lax.broadcasted_iota(jnp.int32, (size, size), 0)
    return jnp.sum(jnp.where(lane == sub, row, jnp.zeros_like(row)), axis=1, keepdims=True)


def both_ways(row):
    as_float = row.astype(F32)
    return as_float, column(as_float)


def select(lanes, points, local, weight):
    value = jnp.zeros(lanes.shape, F32)
    for point in range(points):
        value = jnp.where(lanes % points == point, weight[point], value)
    return jnp.where((lanes // points).astype(F32) == local, value, 0.0)


def rounded(value):
    return value.astype(BF16).astype(F32)


def pick_kernel(place, blocks, weights, state_ref, keep, send, state, arrived):
    load = pltpu.make_async_copy(state_ref, state, arrived)
    load.start()
    device = place[0]
    batches, points, size = weights.shape
    width, members = state.shape
    held = width // points
    lane = lax.broadcasted_iota(jnp.int32, (size, size), 1)
    sub = lax.broadcasted_iota(jnp.int32, (size, size), 0)
    earlier = jnp.where(sub < lane, 1.0, 0.0).astype(BF16)
    row = blocks[...]
    mine = jnp.where(row // (2 * held) == device // 2, 1.0, 0.0)
    rank = nn(mine.astype(BF16), earlier).astype(jnp.int32)
    own = row // held == device
    slots = lax.broadcasted_iota(jnp.int32, (SLOTS, size), 0)
    points_of = lax.broadcasted_iota(jnp.int32, (width, size), 0)
    chosen, selector = [], []
    for batch in range(batches):
        place_of = rank[batch : batch + 1, :]
        place_of = place_of if batch == 0 else SLOTS - 1 - place_of
        place_of = jnp.where(own[batch : batch + 1, :], place_of, -1)
        chosen.append(jnp.where(slots == place_of, 1.0, 0.0))
        value = jnp.zeros((width, size), F32)
        for point in range(points):
            weight = weights[batch, point : point + 1, :]
            value = jnp.where(points_of % points == point, weight, value)
        local = row[batch : batch + 1, :] - device * held
        selector.append(jnp.where(points_of // points == local, value, 0.0))
    chosen = jnp.concatenate(chosen, axis=1).astype(BF16)
    parts = [nt(chosen, part).astype(BF16) for part in split(jnp.concatenate(selector, axis=1))]
    load.wait()
    rows = dot3(nn, parts, split(state[...]))
    from_first = lax.broadcasted_iota(jnp.int32, (SLOTS, 1), 0).astype(F32)
    from_first = from_first < jnp.sum(mine[:1, :], axis=1, keepdims=True)
    rows = jnp.where(from_first, rounded(rows), rows)
    code = jnp.round(rows * (1.0 / UNIT)).astype(jnp.int32)
    left, right = code[:, : members // 2], code[:, members // 2 :]
    first = device % 2 == 0
    keep[...] = jnp.where(first, left, right).astype(jnp.int16)
    send[...] = jnp.where(first, right, left).astype(jnp.int16)


def pick(place, blocks, weights, state):
    return pl.pallas_call(
        pick_kernel,
        out_shape=[jax.ShapeDtypeStruct((SLOTS, state.shape[1] // 2), jnp.int16)] * 2,
        in_specs=[SMEM, VMEM, VMEM, ANYWHERE],
        out_specs=[VMEM] * 2,
        scratch_shapes=[pltpu.VMEM(state.shape, F32), pltpu.SemaphoreType.DMA],
        compiler_params=PARAMS,
        name="pick",
    )(place, blocks, weights, state)


def pick_all_kernel(place, blocks, weights, state, out):
    device = place[0]
    batches, points, size = weights.shape
    width = state.shape[0]
    lanes = lax.broadcasted_iota(jnp.int32, (size, width), 1)
    for batch in range(batches):
        columns = [column(weights[batch, point : point + 1, :]) for point in range(points)]
        local = column((blocks[batch : batch + 1, :] - device * (width // points)).astype(F32))
        rows = jnp.dot(
            select(lanes, points, local, columns),
            state[...],
            precision=lax.Precision.HIGHEST,
            preferred_element_type=F32,
        )
        rows = rounded(rows) if batch == 0 else rows
        out[batch * size : (batch + 1) * size, :] = jnp.round(rows * (1.0 / UNIT))


def pick_all(place, blocks, weights, state):
    return pl.pallas_call(
        pick_all_kernel,
        out_shape=jax.ShapeDtypeStruct((blocks.size, state.shape[1]), F32),
        in_specs=[SMEM, VMEM, VMEM, VMEM],
        out_specs=VMEM,
        compiler_params=PARAMS,
        name="pick_all",
    )(place, blocks, weights, state)


def order_kernel(groups, place, blocks, *outs):
    outs, fits = outs[:-1], outs[-1]
    device, held = place[0], place[1]
    size = blocks.shape[1]
    lane = lax.broadcasted_iota(jnp.int32, (size, size), 1)
    sub = lax.broadcasted_iota(jnp.int32, (size, size), 0)
    for batch in range(blocks.shape[0]):
        pair_row, pair_column = both_ways(blocks[batch : batch + 1, :] // (2 * held))
        before = jnp.where((pair_row == pair_column) & (lane < sub), 1.0, 0.0)
        rank = jnp.sum(before, axis=1, keepdims=True).astype(jnp.int32)
        away = (2 * pair_column.astype(jnp.int32)) ^ device
        distance = 8 * ((away >> 3) & 1) + 4 * ((away >> 4) & 1) + ((away >> 1) & 3)
        slot = rank if batch == 0 else SLOTS - 1 - rank
        for distances, out in zip(groups, outs):
            where = jnp.full(rank.shape, -SLOTS, jnp.int32)
            for index, known in enumerate(distances):
                where = jnp.where(distance == known, SLOTS * index, where)
            slots = lax.broadcasted_iota(jnp.int32, (size, out.shape[1]), 1)
            chosen = jnp.where(slots == where + slot, 1.0, 0.0)
            out[batch * size : (batch + 1) * size, :] = chosen.astype(BF16)
    counts = jnp.zeros((16, 1), F32)
    for batch in range(blocks.shape[0]):
        chip = blocks[batch : batch + 1, :] // (2 * held)
        chips = lax.broadcasted_iota(jnp.int32, (16, size), 0)
        counts = counts + jnp.sum(jnp.where(chips == chip, 1.0, 0.0), axis=1, keepdims=True)
    fits[0] = (jnp.max(counts) <= SLOTS).astype(jnp.int32)


def order(place, blocks, groups):
    return pl.pallas_call(
        functools.partial(order_kernel, groups),
        out_shape=[
            jax.ShapeDtypeStruct((blocks.size, SLOTS * len(group)), BF16) for group in groups
        ]
        + [jax.ShapeDtypeStruct((1,), jnp.int32)],
        in_specs=[SMEM, VMEM],
        out_specs=[VMEM] * len(groups) + [SMEM],
        compiler_params=PARAMS,
        cost_estimate=pl.CostEstimate(flops=10**6, bytes_accessed=10**6, transcendentals=0),
        name="order",
    )(place, blocks)


def put_in_order(chosen, pieces):
    size = chosen.shape[0] // 2
    values = [ref[index].astype(jnp.int32) for ref in pieces for index in range(ref.shape[0])]
    high, low = split(jnp.concatenate(values, axis=0).astype(F32))
    second = chosen[size:, :]
    return nn(chosen[:size, :], high), nn(second, high) + nn(second, low)


def early_kernel(chosen, *refs):
    size = chosen.shape[0] // 2
    refs[-1][:size, :], refs[-1][size:, :] = put_in_order(chosen, refs[:-1])


def late_kernel(chosen, early, *refs):
    size = chosen.shape[0] // 2
    first, second = put_in_order(chosen, refs[:-2])
    refs[-2][...] = ((first + early[:size, :]) * UNIT).astype(BF16)
    refs[-1][...] = (second + early[size:, :]).astype(jnp.int32).astype(jnp.int16)


def early_rows(chosen, pieces):
    return pl.pallas_call(
        early_kernel,
        out_shape=jax.ShapeDtypeStruct((chosen.shape[0], pieces[0].shape[-1]), F32),
        in_specs=[VMEM] * (1 + len(pieces)),
        out_specs=VMEM,
        compiler_params=PARAMS,
        cost_estimate=pl.CostEstimate(flops=10**9, bytes_accessed=4 * 10**6, transcendentals=0),
        name="early_rows",
    )(chosen, *pieces)


def late_rows(chosen, early, pieces):
    shape = (early.shape[0] // 2, early.shape[1])
    return pl.pallas_call(
        late_kernel,
        out_shape=[jax.ShapeDtypeStruct(shape, BF16), jax.ShapeDtypeStruct(shape, jnp.int16)],
        in_specs=[VMEM] * (2 + len(pieces)),
        out_specs=[VMEM] * 2,
        compiler_params=PARAMS,
        name="late_rows",
    )(chosen, early, *pieces)


def eliminate(covariance, work, inverse):
    size = covariance.shape[0]
    lane = lax.broadcasted_iota(jnp.int32, (size, size), 1)
    sub = lax.broadcasted_iota(jnp.int32, (size, size), 0)
    work[...] = covariance
    inverse[...] = jnp.where(lane == sub, 1.0, 0.0)

    def step(k, carry):
        row = work[pl.ds(k, 1), :]
        current = work[...]
        pivot = jnp.sum(jnp.where(lane[:1] == k, row, 0.0), axis=1, keepdims=True)
        column = jnp.sum(jnp.where(lane == k, current, 0.0), axis=1, keepdims=True)
        factor = jnp.where(sub[:, :1] > k, column / pivot, 0.0)
        inverse_row = inverse[pl.ds(k, 1), :]
        work[...] = current - factor * row
        inverse[...] = inverse[...] - factor * inverse_row
        return carry

    lax.fori_loop(0, size, step, 0)
    pivots = jnp.sum(jnp.where(lane == sub, work[...], 0.0), axis=1, keepdims=True)
    inverse[...] = inverse[...] * (1.0 / jnp.sqrt(pivots))


def squared(a):
    return jnp.sum(a * a)


def newton(scaled):
    size = scaled.shape[0]
    lane = lax.broadcasted_iota(jnp.int32, (size, size), 1)
    sub = lax.broadcasted_iota(jnp.int32, (size, size), 0)
    eye = jnp.where(lane == sub, 1.0, 0.0)
    half = jnp.where(lane < sub, 1.0, jnp.where(lane == sub, 0.5, 0.0))

    def third_order(error):
        low = error * half
        lowb = low.astype(BF16)
        return (nn(lowb, lowb) + half * nt(lowb, lowb)) - low

    def begin():
        first = (third_order(scaled - eye) + eye) * (RESCALE**0.5)
        fb = first.astype(BF16)
        error = nt(nn(fb, scaled.astype(BF16)).astype(BF16), fb) - eye
        return nn((third_order(error) + eye).astype(BF16), fb)

    def step(t):
        ts = split(t)
        error = dot3(nt, split(dot3(nn, ts, split(scaled))), ts) - eye
        return t + nn(third_order(error).astype(BF16), ts[0]), squared(error)

    return begin, step


def inverse_factor(covariance, work, inverse, use):
    size = covariance.shape[0]
    lane = lax.broadcasted_iota(jnp.int32, (size, size), 1)
    sub = lax.broadcasted_iota(jnp.int32, (size, size), 0)
    on_diagonal = jnp.where(lane == sub, covariance, 0.0)
    scale_row = lax.rsqrt(jnp.sum(on_diagonal, axis=0, keepdims=True) * (1.0 / SCALE))
    scale_column = lax.rsqrt(jnp.sum(on_diagonal, axis=1, keepdims=True) * (1.0 / SCALE))
    scaled = covariance * scale_row * scale_column
    begin, step = newton(scaled)
    t, residual = step(begin())
    use(t * scale_row)

    @pl.when(jnp.logical_not(residual <= TOLERANCE**2))
    def _():
        inverse[...] = t

        def again(carry):
            better, left = step(inverse[...])
            inverse[...] = better
            return carry[0] + 1, left

        def wanted(carry):
            return (carry[0] < 6) & jnp.logical_not(carry[1] <= (0.2 * TOLERANCE) ** 2)

        _, left = lax.while_loop(wanted, again, (0, residual))
        inverse[...] = inverse[...] * scale_row

        @pl.when(jnp.logical_not(left <= (0.2 * TOLERANCE) ** 2))
        def _():
            eliminate(covariance, work, inverse)

        use(inverse[...])


def whiten(observed, tags, values, load, noise_ref, work, inverse, store):
    members = observed.shape[1]
    size = observed.shape[0]
    mean = row_mean(observed)
    lane = lax.broadcasted_iota(jnp.int32, (size, size), 1)
    sub = lax.broadcasted_iota(jnp.int32, (size, size), 0)
    variance_row = jnp.where(tags == 0, 0.5, 2.0)
    mean_row = jnp.sum(jnp.where(lane == sub, mean, 0.0), axis=0, keepdims=True)
    exact = observed.astype(BF16)
    covariance = (nt(exact, exact) - mean * (mean_row * members)) * (1.0 / (members - 1))
    covariance = covariance + jnp.where(lane == sub, variance_row, 0.0)

    def finish(t):
        applied = dot2(nn, split(t), exact)
        noise = dot2(nn, split(t * jnp.sqrt(variance_row)), noise_ref[...])
        mean_part = jnp.sum(t * mean_row, axis=1, keepdims=True)
        value_part = jnp.sum(t * values, axis=1, keepdims=True)
        store((applied - mean_part).astype(BF16), (noise + value_part - applied).astype(BF16))

    load.wait()
    inverse_factor(covariance, work, inverse, finish)


def row_sums(array):
    return nt(jnp.ones((8, array.shape[1]), BF16), array)[:1, :]


def update(state, whitened, white_innov):
    members = state.shape[1]
    projected = dot2(nt, split(state), whitened) - row_mean(state) * row_sums(whitened)
    return state + dot2(nn, split(projected), white_innov) * (1.0 / (members - 1))


def both_halves(place, own, other):
    own, other = own[...].astype(F32), other[...].astype(F32)
    first = place[0] % 2 == 0
    return jnp.concatenate(
        [jnp.where(first, own, other), jnp.where(first, other, own)], axis=1
    )


def first_kernel(
    place, tags, values, noise_ref, own, other, whitened, white_innov, noise, loads, work, inverse
):
    load = pltpu.make_async_copy(noise_ref.at[0], noise, loads.at[0])
    load.start()
    observed = both_halves(place, own, other)

    def store(w, v):
        whitened[...] = w
        white_innov[...] = v

    whiten(observed, tags[:1, :], values[:1, :], load, noise, work, inverse, store)


def second_kernel(
    place,
    tags,
    values,
    noise_ref,
    own,
    other,
    whitened,
    white_innov,
    state_ref,
    analysis,
    noise,
    loads,
    work,
    inverse,
    state,
):
    load = pltpu.make_async_copy(noise_ref.at[1], noise, loads.at[0])
    load_state = pltpu.make_async_copy(state_ref, state, loads.at[1])
    load_state.start()
    load.start()
    w, v = whitened[...], white_innov[...]
    observed = rounded(update(both_halves(place, own, other), w, v) * UNIT)
    load_state.wait()
    first = update(state[...], w, v)

    def store(w, v):
        analysis[...] = update(first, w, v)

    whiten(observed, tags[1:2, :], values[1:2, :], load, noise, work, inverse, store)


def batch_call(kernel, name, outs, place, tags, values, noise, *arrays, state=()):
    rows, members = noise.shape[1:]
    return pl.pallas_call(
        kernel,
        out_shape=outs,
        in_specs=[SMEM, VMEM, VMEM, ANYWHERE] + [VMEM] * len(arrays) + [ANYWHERE] * len(state),
        out_specs=[VMEM] * len(outs),
        scratch_shapes=[
            pltpu.VMEM((rows, members), BF16),
            pltpu.SemaphoreType.DMA((2,)),
            pltpu.VMEM((rows, rows), F32),
            pltpu.VMEM((rows, rows), F32),
        ]
        + [pltpu.VMEM(array.shape, F32) for array in state],
        compiler_params=PARAMS,
        name=name,
    )(place, tags, values, noise, *arrays, *state)


def batches(place, tags, values, noise, state, observed, prior):
    shape = jax.ShapeDtypeStruct(noise.shape[1:], BF16)
    shared = (place, tags, values, noise)
    white = batch_call(first_kernel, "first_batch", [shape, shape], *shared, *observed)
    analysis = jax.ShapeDtypeStruct(state.shape, F32)
    return batch_call(
        second_kernel, "second_batch", [analysis], *shared, *prior, *white, state=(state,)
    )[0]


AXES = ("row", "col")
CORE, Y, X, NEAR_Z, FAR_Z = 1, 2, 4, 8, 16


def swap(value, mask):
    return lax.ppermute(value, AXES, [(i, i ^ mask) for i in range(32)])


def after(value, other):
    return lax.optimization_barrier((value, other))[0]


def joined(first, second):
    return jnp.concatenate([first, second], axis=0)


EARLY = (0, 4, 8, 12, 2, 10, 5, 13, 1, 9, 3, 11, 6, 7)
LATE = (14, 15)


def by_slots(place, ensemble, blocks, weights):
    keep, send = pick(place, blocks, weights, ensemble)
    own = (keep + swap(send, CORE))[None]
    far, near = swap(own, FAR_Z), swap(own, NEAR_Z)
    near_far = swap(far, NEAR_Z)
    both = joined(own, near)
    both_x = swap(both, X)
    far_y = swap(after(far, near), Y)
    near_far_y = swap(near_far, Y)
    both_y = swap(after(joined(both, both_x), near_far), Y)
    far_x = swap(joined(far, far_y), X)
    near_far_x = swap(joined(near_far, near_far_y), X)
    early_places, late_places, fits = order(place, blocks, (EARLY, LATE))
    pieces = [own, far, near, near_far, both_x, far_y, near_far_y, both_y, far_x]
    early = early_rows(early_places, pieces)
    return late_rows(late_places, early, [near_far_x]), fits


def add_by_swaps(value):
    for mask in (CORE, Y, X, NEAR_Z, FAR_Z):
        value = value + swap(value, mask)
    return value


def half_of(value, core):
    rows, members = value.shape
    return lax.dynamic_slice(value, (0, core * (members // 2)), (rows, members // 2))


def by_sum(add_up, other, place, ensemble, blocks, weights):
    rows = blocks.shape[1]
    codes = add_up(pick_all(place, blocks, weights, ensemble))
    codes = half_of(codes, (place[0] + other) % 2)
    return (codes[:rows] * UNIT).astype(BF16), codes[rows:].astype(jnp.int16)


def body(staged, ensemble, obs_blocks, obs_weights, comp_tags, obs_values, obs_noise):
    held = ensemble.shape[0] // obs_weights.shape[2]
    place = jnp.stack([lax.axis_index(AXES), held]).astype(jnp.int32)
    by_point = jnp.swapaxes(obs_weights, 1, 2)
    operands = (place, ensemble, obs_blocks, by_point)
    if staged:
        slotted, fits = by_slots(*operands)
        own = lax.cond(
            fits[0] == 1,
            lambda slotted, *operands: tuple(slotted),
            lambda slotted, *operands: by_sum(add_by_swaps, 0, *operands),
            slotted,
            *operands,
        )
        pairs = [(half, swap(half, CORE)) for half in own]
    else:
        add_up = lambda value: lax.psum(value, AXES)
        pairs = list(zip(by_sum(add_up, 0, *operands), by_sum(add_up, 1, *operands)))
    return batches(place, comp_tags, obs_values, obs_noise, ensemble, *pairs)


def solution(mesh):
    staged = (mesh.shape["row"], mesh.shape["col"]) == (8, 4)
    in_specs = (P(AXES, None), P(), P(), P(), P(), P())
    out_specs = P(AXES, None)
    return jax.shard_map(
        functools.partial(body, staged),
        mesh=mesh,
        in_specs=in_specs,
        out_specs=out_specs,
        check_vma=False,
    )
```

```python
import functools

import jax
import jax.numpy as jnp
from jax import lax
from jax.experimental import pallas as pl
from jax.experimental.pallas import tpu as pltpu
from jax.sharding import PartitionSpec as P

SLOTS = 56
UNIT = 1.0 / 1024
SCALE = 0.6
RESCALE = 1.25
TOLERANCE = 0.25
BF16 = jnp.bfloat16
F32 = jnp.float32
VMEM = pl.BlockSpec(memory_space=pltpu.VMEM)
SMEM = pl.BlockSpec(memory_space=pltpu.SMEM)
ANYWHERE = pl.BlockSpec(memory_space=pl.ANY)
PARAMS = pltpu.CompilerParams(vmem_limit_bytes=40 * 1024 * 1024)


def nt(a, b):
    return lax.dot_general(a, b, (((1,), (1,)), ((), ())), preferred_element_type=F32)


def nn(a, b):
    return lax.dot_general(a, b, (((1,), (0,)), ((), ())), preferred_element_type=F32)


def split(a):
    high = a.astype(BF16)
    return high, (a - high.astype(F32)).astype(BF16)


def dot2(dot, a, b):
    rows = a[0].shape[0]
    both = dot(jnp.concatenate(a, axis=0), b)
    return both[:rows] + both[rows:]


def dot3(dot, a, b):
    return dot2(dot, a, b[0]) + dot(a[0], b[1])


def row_mean(a):
    return jnp.sum(a, axis=1, keepdims=True) * (1.0 / a.shape[1])


def column(row):
    size = row.shape[1]
    lane = lax.broadcasted_iota(jnp.int32, (size, size), 1)
    sub = lax.broadcasted_iota(jnp.int32, (size, size), 0)
    return jnp.sum(jnp.where(lane == sub, row, jnp.zeros_like(row)), axis=1, keepdims=True)


def both_ways(row):
    as_float = row.astype(F32)
    return as_float, column(as_float)


def select(lanes, points, local, weight):
    value = jnp.zeros(lanes.shape, F32)
    for point in range(points):
        value = jnp.where(lanes % points == point, weight[point], value)
    return jnp.where((lanes // points).astype(F32) == local, value, 0.0)


def rounded(value):
    return value.astype(BF16).astype(F32)


def pick_kernel(place, blocks, weights, state_ref, keep, send, fits, state, arrived):
    load = pltpu.make_async_copy(state_ref, state, arrived)
    load.start()
    device = place[0]
    batches, points, size = weights.shape
    width, members = state.shape
    held = width // points
    lane = lax.broadcasted_iota(jnp.int32, (size, size), 1)
    sub = lax.broadcasted_iota(jnp.int32, (size, size), 0)
    earlier = jnp.where(sub < lane, 1.0, 0.0).astype(BF16)
    row = blocks[...]
    mine = jnp.where(row // (2 * held) == device // 2, 1.0, 0.0)
    rank = nn(mine.astype(BF16), earlier).astype(jnp.int32)
    own = row // held == device
    slots = lax.broadcasted_iota(jnp.int32, (SLOTS, size), 0)
    points_of = lax.broadcasted_iota(jnp.int32, (width, size), 0)
    chosen, selector = [], []
    for batch in range(batches):
        place_of = rank[batch : batch + 1, :]
        place_of = place_of if batch == 0 else SLOTS - 1 - place_of
        place_of = jnp.where(own[batch : batch + 1, :], place_of, -1)
        chosen.append(jnp.where(slots == place_of, 1.0, 0.0))
        value = jnp.zeros((width, size), F32)
        for point in range(points):
            weight = weights[batch, point : point + 1, :]
            value = jnp.where(points_of % points == point, weight, value)
        local = row[batch : batch + 1, :] - device * held
        selector.append(jnp.where(points_of // points == local, value, 0.0))
    chosen = jnp.concatenate(chosen, axis=1).astype(BF16)
    parts = [nt(chosen, part).astype(BF16) for part in split(jnp.concatenate(selector, axis=1))]
    load.wait()
    rows = dot3(nn, parts, split(state[...]))
    from_first = lax.broadcasted_iota(jnp.int32, (SLOTS, 1), 0).astype(F32)
    from_first = from_first < jnp.sum(mine[:1, :], axis=1, keepdims=True)
    rows = jnp.where(from_first, rounded(rows), rows)
    code = jnp.round(rows * (1.0 / UNIT)).astype(jnp.int32)
    left, right = code[:, : members // 2], code[:, members // 2 :]
    first = device % 2 == 0
    keep[...] = jnp.where(first, left, right).astype(jnp.int16)
    send[...] = jnp.where(first, right, left).astype(jnp.int16)
    chips = lax.broadcasted_iota(jnp.int32, (16, size), 0)
    counts = jnp.zeros((16, 1), F32)
    for batch in range(batches):
        here = jnp.where(chips == row[batch : batch + 1, :] // (2 * held), 1.0, 0.0)
        counts = counts + jnp.sum(here, axis=1, keepdims=True)
    fits[0] = (jnp.max(counts) <= SLOTS).astype(jnp.int32)


def pick(place, blocks, weights, state):
    return pl.pallas_call(
        pick_kernel,
        out_shape=[jax.ShapeDtypeStruct((SLOTS, state.shape[1] // 2), jnp.int16)] * 2
        + [jax.ShapeDtypeStruct((1,), jnp.int32)],
        in_specs=[SMEM, VMEM, VMEM, ANYWHERE],
        out_specs=[VMEM] * 2 + [SMEM],
        scratch_shapes=[pltpu.VMEM(state.shape, F32), pltpu.SemaphoreType.DMA],
        compiler_params=PARAMS,
        name="pick",
    )(place, blocks, weights, state)


def pick_all_kernel(place, blocks, weights, state, out):
    device = place[0]
    batches, points, size = weights.shape
    width = state.shape[0]
    lanes = lax.broadcasted_iota(jnp.int32, (size, width), 1)
    for batch in range(batches):
        columns = [column(weights[batch, point : point + 1, :]) for point in range(points)]
        local = column((blocks[batch : batch + 1, :] - device * (width // points)).astype(F32))
        rows = jnp.dot(
            select(lanes, points, local, columns),
            state[...],
            precision=lax.Precision.HIGHEST,
            preferred_element_type=F32,
        )
        rows = rounded(rows) if batch == 0 else rows
        out[batch * size : (batch + 1) * size, :] = jnp.round(rows * (1.0 / UNIT))


def pick_all(place, blocks, weights, state):
    return pl.pallas_call(
        pick_all_kernel,
        out_shape=jax.ShapeDtypeStruct((blocks.size, state.shape[1]), F32),
        in_specs=[SMEM, VMEM, VMEM, VMEM],
        out_specs=VMEM,
        compiler_params=PARAMS,
        name="pick_all",
    )(place, blocks, weights, state)


def order_kernel(batch, groups, place, blocks, *outs):
    device, held = place[0], place[1]
    size = blocks.shape[1]
    lane = lax.broadcasted_iota(jnp.int32, (size, size), 1)
    sub = lax.broadcasted_iota(jnp.int32, (size, size), 0)
    pair_row, pair_column = both_ways(blocks[batch : batch + 1, :] // (2 * held))
    before = jnp.where((pair_row == pair_column) & (lane < sub), 1.0, 0.0)
    rank = jnp.sum(before, axis=1, keepdims=True).astype(jnp.int32)
    away = (2 * pair_column.astype(jnp.int32)) ^ device
    distance = 8 * ((away >> 3) & 1) + 4 * ((away >> 4) & 1) + ((away >> 1) & 3)
    slot = rank if batch == 0 else SLOTS - 1 - rank
    for distances, out in zip(groups, outs):
        where = jnp.full(rank.shape, -SLOTS, jnp.int32)
        for index, known in enumerate(distances):
            where = jnp.where(distance == known, SLOTS * index, where)
        slots = lax.broadcasted_iota(jnp.int32, out.shape, 1)
        out[...] = jnp.where(slots == where + slot, 1.0, 0.0).astype(BF16)


def order(batch, place, blocks, groups):
    rows = blocks.shape[1]
    return pl.pallas_call(
        functools.partial(order_kernel, batch, groups),
        out_shape=[jax.ShapeDtypeStruct((rows, SLOTS * len(group)), BF16) for group in groups],
        in_specs=[SMEM, VMEM],
        out_specs=[VMEM] * len(groups),
        compiler_params=PARAMS,
        cost_estimate=pl.CostEstimate(flops=10**6, bytes_accessed=10**6, transcendentals=0),
        name="order",
    )(place, blocks)


def put_in_order(chosen, pieces):
    values = [ref[index].astype(jnp.int32) for ref in pieces for index in range(ref.shape[0])]
    high, low = split(jnp.concatenate(values, axis=0).astype(F32))
    first, second = chosen[0][...], chosen[1][...]
    return nn(first, high), nn(second, high) + nn(second, low)


def early_kernel(first, second, *refs):
    size = first.shape[0]
    refs[-1][:size, :], refs[-1][size:, :] = put_in_order((first, second), refs[:-1])


def late_kernel(first, second, early, *refs):
    size = first.shape[0]
    codes = put_in_order((first, second), refs[:-2])
    refs[-2][...] = ((codes[0] + early[:size, :]) * UNIT).astype(BF16)
    refs[-1][...] = (codes[1] + early[size:, :]).astype(jnp.int32).astype(jnp.int16)


def early_rows(chosen, pieces):
    rows = chosen[0].shape[0]
    return pl.pallas_call(
        early_kernel,
        out_shape=jax.ShapeDtypeStruct((2 * rows, pieces[0].shape[-1]), F32),
        in_specs=[VMEM] * (2 + len(pieces)),
        out_specs=VMEM,
        compiler_params=PARAMS,
        cost_estimate=pl.CostEstimate(flops=10**9, bytes_accessed=4 * 10**6, transcendentals=0),
        name="early_rows",
    )(*chosen, *pieces)


def late_rows(chosen, early, pieces):
    shape = (early.shape[0] // 2, early.shape[1])
    return pl.pallas_call(
        late_kernel,
        out_shape=[jax.ShapeDtypeStruct(shape, BF16), jax.ShapeDtypeStruct(shape, jnp.int16)],
        in_specs=[VMEM] * (3 + len(pieces)),
        out_specs=[VMEM] * 2,
        compiler_params=PARAMS,
        name="late_rows",
    )(*chosen, early, *pieces)


def eliminate(covariance, work, inverse):
    size = covariance.shape[0]
    lane = lax.broadcasted_iota(jnp.int32, (size, size), 1)
    sub = lax.broadcasted_iota(jnp.int32, (size, size), 0)
    work[...] = covariance
    inverse[...] = jnp.where(lane == sub, 1.0, 0.0)

    def step(k, carry):
        row = work[pl.ds(k, 1), :]
        current = work[...]
        pivot = jnp.sum(jnp.where(lane[:1] == k, row, 0.0), axis=1, keepdims=True)
        column = jnp.sum(jnp.where(lane == k, current, 0.0), axis=1, keepdims=True)
        factor = jnp.where(sub[:, :1] > k, column / pivot, 0.0)
        inverse_row = inverse[pl.ds(k, 1), :]
        work[...] = current - factor * row
        inverse[...] = inverse[...] - factor * inverse_row
        return carry

    lax.fori_loop(0, size, step, 0)
    pivots = jnp.sum(jnp.where(lane == sub, work[...], 0.0), axis=1, keepdims=True)
    inverse[...] = inverse[...] * (1.0 / jnp.sqrt(pivots))


def squared(a):
    return jnp.sum(a * a)


def newton(scaled):
    size = scaled.shape[0]
    lane = lax.broadcasted_iota(jnp.int32, (size, size), 1)
    sub = lax.broadcasted_iota(jnp.int32, (size, size), 0)
    eye = jnp.where(lane == sub, 1.0, 0.0)
    half = jnp.where(lane < sub, 1.0, jnp.where(lane == sub, 0.5, 0.0))

    def third_order(error):
        low = error * half
        lowb = low.astype(BF16)
        return (nn(lowb, lowb) + half * nt(lowb, lowb)) - low

    def begin():
        first = (third_order(scaled - eye) + eye) * (RESCALE**0.5)
        fb = first.astype(BF16)
        error = nt(nn(fb, scaled.astype(BF16)).astype(BF16), fb) - eye
        return nn((third_order(error) + eye).astype(BF16), fb)

    def step(t):
        ts = split(t)
        error = dot3(nt, split(dot3(nn, ts, split(scaled))), ts) - eye
        return t + nn(third_order(error).astype(BF16), ts[0]), squared(error)

    return begin, step


def inverse_factor(covariance, work, inverse, use):
    size = covariance.shape[0]
    lane = lax.broadcasted_iota(jnp.int32, (size, size), 1)
    sub = lax.broadcasted_iota(jnp.int32, (size, size), 0)
    on_diagonal = jnp.where(lane == sub, covariance, 0.0)
    scale_row = lax.rsqrt(jnp.sum(on_diagonal, axis=0, keepdims=True) * (1.0 / SCALE))
    scale_column = lax.rsqrt(jnp.sum(on_diagonal, axis=1, keepdims=True) * (1.0 / SCALE))
    scaled = covariance * scale_row * scale_column
    begin, step = newton(scaled)
    t, residual = step(begin())
    use(t * scale_row)

    @pl.when(jnp.logical_not(residual <= TOLERANCE**2))
    def _():
        inverse[...] = t

        def again(carry):
            better, left = step(inverse[...])
            inverse[...] = better
            return carry[0] + 1, left

        def wanted(carry):
            return (carry[0] < 6) & jnp.logical_not(carry[1] <= (0.2 * TOLERANCE) ** 2)

        _, left = lax.while_loop(wanted, again, (0, residual))
        inverse[...] = inverse[...] * scale_row

        @pl.when(jnp.logical_not(left <= (0.2 * TOLERANCE) ** 2))
        def _():
            eliminate(covariance, work, inverse)

        use(inverse[...])


def whiten(observed, tags, values, load, noise_ref, work, inverse, store):
    members = observed.shape[1]
    size = observed.shape[0]
    mean = row_mean(observed)
    lane = lax.broadcasted_iota(jnp.int32, (size, size), 1)
    sub = lax.broadcasted_iota(jnp.int32, (size, size), 0)
    variance_row = jnp.where(tags == 0, 0.5, 2.0)
    mean_row = jnp.sum(jnp.where(lane == sub, mean, 0.0), axis=0, keepdims=True)
    exact = observed.astype(BF16)
    covariance = (nt(exact, exact) - mean * (mean_row * members)) * (1.0 / (members - 1))
    covariance = covariance + jnp.where(lane == sub, variance_row, 0.0)

    def finish(t):
        applied = dot2(nn, split(t), exact)
        noise = dot2(nn, split(t * jnp.sqrt(variance_row)), noise_ref[...])
        mean_part = jnp.sum(t * mean_row, axis=1, keepdims=True)
        value_part = jnp.sum(t * values, axis=1, keepdims=True)
        store((applied - mean_part).astype(BF16), (noise + value_part - applied).astype(BF16))

    load.wait()
    inverse_factor(covariance, work, inverse, finish)


def row_sums(array):
    return nt(jnp.ones((8, array.shape[1]), BF16), array)[:1, :]


def update(state, whitened, white_innov):
    members = state.shape[1]
    projected = dot2(nt, split(state), whitened) - row_mean(state) * row_sums(whitened)
    return state + dot2(nn, split(projected), white_innov) * (1.0 / (members - 1))


def both_halves(place, own, other):
    own, other = own[...].astype(F32), other[...].astype(F32)
    first = place[0] % 2 == 0
    return jnp.concatenate(
        [jnp.where(first, own, other), jnp.where(first, other, own)], axis=1
    )


def first_kernel(
    place, tags, values, noise_ref, own, other, whitened, white_innov, noise, loads, work, inverse
):
    load = pltpu.make_async_copy(noise_ref.at[0], noise, loads.at[0])
    load.start()
    observed = both_halves(place, own, other)

    def store(w, v):
        whitened[...] = w
        white_innov[...] = v

    whiten(observed, tags[:1, :], values[:1, :], load, noise, work, inverse, store)


def second_kernel(
    place,
    tags,
    values,
    noise_ref,
    own,
    other,
    whitened,
    white_innov,
    state_ref,
    analysis,
    noise,
    loads,
    work,
    inverse,
    state,
):
    load = pltpu.make_async_copy(noise_ref.at[1], noise, loads.at[0])
    load_state = pltpu.make_async_copy(state_ref, state, loads.at[1])
    load_state.start()
    load.start()
    w, v = whitened[...], white_innov[...]
    observed = rounded(update(both_halves(place, own, other), w, v) * UNIT)
    load_state.wait()
    first = update(state[...], w, v)

    def store(w, v):
        analysis[...] = update(first, w, v)

    whiten(observed, tags[1:2, :], values[1:2, :], load, noise, work, inverse, store)


def batch_call(kernel, name, outs, place, tags, values, noise, *arrays, state=()):
    rows, members = noise.shape[1:]
    return pl.pallas_call(
        kernel,
        out_shape=outs,
        in_specs=[SMEM, VMEM, VMEM, ANYWHERE] + [VMEM] * len(arrays) + [ANYWHERE] * len(state),
        out_specs=[VMEM] * len(outs),
        scratch_shapes=[
            pltpu.VMEM((rows, members), BF16),
            pltpu.SemaphoreType.DMA((2,)),
            pltpu.VMEM((rows, rows), F32),
            pltpu.VMEM((rows, rows), F32),
        ]
        + [pltpu.VMEM(array.shape, F32) for array in state],
        compiler_params=PARAMS,
        name=name,
    )(place, tags, values, noise, *arrays, *state)


def batches(place, tags, values, noise, state, observed, prior):
    shape = jax.ShapeDtypeStruct(noise.shape[1:], BF16)
    shared = (place, tags, values, noise)
    white = batch_call(first_kernel, "first_batch", [shape, shape], *shared, *observed)
    analysis = jax.ShapeDtypeStruct(state.shape, F32)
    return batch_call(
        second_kernel, "second_batch", [analysis], *shared, *prior, *white, state=(state,)
    )[0]


AXES = ("row", "col")
CORE, Y, X, NEAR_Z, FAR_Z = 1, 2, 4, 8, 16


def swap(value, mask):
    return lax.ppermute(value, AXES, [(i, i ^ mask) for i in range(32)])


def after(value, other):
    return lax.optimization_barrier((value, other))[0]


def joined(first, second):
    return jnp.concatenate([first, second], axis=0)


EARLY = (0, 4, 8, 12, 2, 10, 5, 13, 1, 9, 3, 11, 6, 7)
LATE = (14, 15)


def by_slots(place, ensemble, blocks, weights):
    keep, send, fits = pick(place, blocks, weights, ensemble)
    own = (keep + swap(send, CORE))[None]
    far, near = swap(own, FAR_Z), swap(own, NEAR_Z)
    near_far = swap(far, NEAR_Z)
    both = joined(own, near)
    both_x = swap(both, X)
    far_y = swap(after(far, near), Y)
    places = [order(0, place, blocks, (EARLY, LATE))]
    near_far_y = swap(after(near_far, places[0]), Y)
    both_y = swap(after(joined(both, both_x), near_far), Y)
    far_x = swap(joined(far, far_y), X)
    places.append(order(1, place, after(blocks, far_y), (EARLY, LATE)))
    near_far_x = swap(after(joined(near_far, near_far_y), places[1]), X)
    early_places, late_places = zip(*places)
    pieces = [own, far, near, near_far, both_x, far_y, near_far_y, both_y, far_x]
    early = early_rows(early_places, pieces)
    return late_rows(late_places, early, [near_far_x]), after(fits, near)


def add_by_swaps(value):
    for mask in (CORE, Y, X, NEAR_Z, FAR_Z):
        value = value + swap(value, mask)
    return value


def half_of(value, core):
    rows, members = value.shape
    return lax.dynamic_slice(value, (0, core * (members // 2)), (rows, members // 2))


def by_sum(add_up, other, place, ensemble, blocks, weights):
    rows = blocks.shape[1]
    codes = add_up(pick_all(place, blocks, weights, ensemble))
    codes = half_of(codes, (place[0] + other) % 2)
    return (codes[:rows] * UNIT).astype(BF16), codes[rows:].astype(jnp.int16)


def body(staged, ensemble, obs_blocks, obs_weights, comp_tags, obs_values, obs_noise):
    held = ensemble.shape[0] // obs_weights.shape[2]
    place = jnp.stack([lax.axis_index(AXES), held]).astype(jnp.int32)
    by_point = jnp.swapaxes(obs_weights, 1, 2)
    operands = (place, ensemble, obs_blocks, by_point)
    if staged:
        slotted, fits = by_slots(*operands)
        own = lax.cond(
            fits[0] == 1,
            lambda slotted, *operands: tuple(slotted),
            lambda slotted, *operands: by_sum(add_by_swaps, 0, *operands),
            slotted,
            *operands,
        )
        pairs = [(half, swap(half, CORE)) for half in own]
    else:
        add_up = lambda value: lax.psum(value, AXES)
        pairs = list(zip(by_sum(add_up, 0, *operands), by_sum(add_up, 1, *operands)))
    return batches(place, comp_tags, obs_values, obs_noise, ensemble, *pairs)


def solution(mesh):
    staged = (mesh.shape["row"], mesh.shape["col"]) == (8, 4)
    in_specs = (P(AXES, None), P(), P(), P(), P(), P())
    out_specs = P(AXES, None)
    return jax.shard_map(
        functools.partial(body, staged),
        mesh=mesh,
        in_specs=in_specs,
        out_specs=out_specs,
        check_vma=False,
    )
```

```python
import functools

import jax
import jax.numpy as jnp
from jax import lax
from jax.experimental import pallas as pl
from jax.experimental.pallas import tpu as pltpu
from jax.sharding import PartitionSpec as P

SLOTS = 56
UNIT = 1.0 / 1024
SCALE = 0.6
RESCALE = 1.25
TOLERANCE = 0.25
BF16 = jnp.bfloat16
F32 = jnp.float32
VMEM = pl.BlockSpec(memory_space=pltpu.VMEM)
SMEM = pl.BlockSpec(memory_space=pltpu.SMEM)
ANYWHERE = pl.BlockSpec(memory_space=pl.ANY)
PARAMS = pltpu.CompilerParams(vmem_limit_bytes=40 * 1024 * 1024)


def nt(a, b):
    return lax.dot_general(a, b, (((1,), (1,)), ((), ())), preferred_element_type=F32)


def nn(a, b):
    return lax.dot_general(a, b, (((1,), (0,)), ((), ())), preferred_element_type=F32)


def split(a):
    high = a.astype(BF16)
    return high, (a - high.astype(F32)).astype(BF16)


def dot2(dot, a, b):
    rows = a[0].shape[0]
    both = dot(jnp.concatenate(a, axis=0), b)
    return both[:rows] + both[rows:]


def dot3(dot, a, b):
    return dot2(dot, a, b[0]) + dot(a[0], b[1])


def row_mean(a):
    return jnp.sum(a, axis=1, keepdims=True) * (1.0 / a.shape[1])


def column(row):
    size = row.shape[1]
    lane = lax.broadcasted_iota(jnp.int32, (size, size), 1)
    sub = lax.broadcasted_iota(jnp.int32, (size, size), 0)
    return jnp.sum(jnp.where(lane == sub, row, jnp.zeros_like(row)), axis=1, keepdims=True)


def both_ways(row):
    as_float = row.astype(F32)
    return as_float, column(as_float)


def select(lanes, points, local, weight):
    value = jnp.zeros(lanes.shape, F32)
    for point in range(points):
        value = jnp.where(lanes % points == point, weight[point], value)
    return jnp.where((lanes // points).astype(F32) == local, value, 0.0)


def rounded(value):
    return value.astype(BF16).astype(F32)


def pick_kernel(place, blocks, weights, state_ref, keep, send, state, arrived):
    load = pltpu.make_async_copy(state_ref, state, arrived)
    load.start()
    device = place[0]
    batches, points, size = weights.shape
    width, members = state.shape
    held = width // points
    lane = lax.broadcasted_iota(jnp.int32, (size, size), 1)
    sub = lax.broadcasted_iota(jnp.int32, (size, size), 0)
    earlier = jnp.where(sub < lane, 1.0, 0.0).astype(BF16)
    row = blocks[...]
    mine = jnp.where(row // (2 * held) == device // 2, 1.0, 0.0)
    rank = nn(mine.astype(BF16), earlier).astype(jnp.int32)
    own = row // held == device
    slots = lax.broadcasted_iota(jnp.int32, (SLOTS, size), 0)
    points_of = lax.broadcasted_iota(jnp.int32, (width, size), 0)
    chosen, selector = [], []
    for batch in range(batches):
        place_of = rank[batch : batch + 1, :]
        place_of = place_of if batch == 0 else SLOTS - 1 - place_of
        place_of = jnp.where(own[batch : batch + 1, :], place_of, -1)
        chosen.append(jnp.where(slots == place_of, 1.0, 0.0))
        value = jnp.zeros((width, size), F32)
        for point in range(points):
            weight = weights[batch, point : point + 1, :]
            value = jnp.where(points_of % points == point, weight, value)
        local = row[batch : batch + 1, :] - device * held
        selector.append(jnp.where(points_of // points == local, value, 0.0))
    chosen = jnp.concatenate(chosen, axis=1).astype(BF16)
    parts = [nt(chosen, part).astype(BF16) for part in split(jnp.concatenate(selector, axis=1))]
    load.wait()
    rows = dot3(nn, parts, split(state[...]))
    from_first = lax.broadcasted_iota(jnp.int32, (SLOTS, 1), 0).astype(F32)
    from_first = from_first < jnp.sum(mine[:1, :], axis=1, keepdims=True)
    rows = jnp.where(from_first, rounded(rows), rows)
    code = jnp.round(rows * (1.0 / UNIT)).astype(jnp.int32)
    left, right = code[:, : members // 2], code[:, members // 2 :]
    first = device % 2 == 0
    keep[...] = jnp.where(first, left, right).astype(jnp.int16)
    send[...] = jnp.where(first, right, left).astype(jnp.int16)


def pick(place, blocks, weights, state):
    return pl.pallas_call(
        pick_kernel,
        out_shape=[jax.ShapeDtypeStruct((SLOTS, state.shape[1] // 2), jnp.int16)] * 2,
        in_specs=[SMEM, VMEM, VMEM, ANYWHERE],
        out_specs=[VMEM] * 2,
        scratch_shapes=[pltpu.VMEM(state.shape, F32), pltpu.SemaphoreType.DMA],
        compiler_params=PARAMS,
        name="pick",
    )(place, blocks, weights, state)


def pick_all_kernel(place, blocks, weights, state, out):
    device = place[0]
    batches, points, size = weights.shape
    width = state.shape[0]
    lanes = lax.broadcasted_iota(jnp.int32, (size, width), 1)
    for batch in range(batches):
        columns = [column(weights[batch, point : point + 1, :]) for point in range(points)]
        local = column((blocks[batch : batch + 1, :] - device * (width // points)).astype(F32))
        rows = jnp.dot(
            select(lanes, points, local, columns),
            state[...],
            precision=lax.Precision.HIGHEST,
            preferred_element_type=F32,
        )
        rows = rounded(rows) if batch == 0 else rows
        out[batch * size : (batch + 1) * size, :] = jnp.round(rows * (1.0 / UNIT))


def pick_all(place, blocks, weights, state):
    return pl.pallas_call(
        pick_all_kernel,
        out_shape=jax.ShapeDtypeStruct((blocks.size, state.shape[1]), F32),
        in_specs=[SMEM, VMEM, VMEM, VMEM],
        out_specs=VMEM,
        compiler_params=PARAMS,
        name="pick_all",
    )(place, blocks, weights, state)


def order_kernel(groups, place, blocks, *outs):
    outs, fits = outs[:-1], outs[-1]
    device, held = place[0], place[1]
    size = blocks.shape[1]
    lane = lax.broadcasted_iota(jnp.int32, (size, size), 1)
    sub = lax.broadcasted_iota(jnp.int32, (size, size), 0)
    for batch in range(blocks.shape[0]):
        pair_row, pair_column = both_ways(blocks[batch : batch + 1, :] // (2 * held))
        before = jnp.where((pair_row == pair_column) & (lane < sub), 1.0, 0.0)
        rank = jnp.sum(before, axis=1, keepdims=True).astype(jnp.int32)
        away = (2 * pair_column.astype(jnp.int32)) ^ device
        distance = 8 * ((away >> 3) & 1) + 4 * ((away >> 4) & 1) + ((away >> 1) & 3)
        slot = rank if batch == 0 else SLOTS - 1 - rank
        for distances, out in zip(groups, outs):
            where = jnp.full(rank.shape, -SLOTS, jnp.int32)
            for index, known in enumerate(distances):
                where = jnp.where(distance == known, SLOTS * index, where)
            slots = lax.broadcasted_iota(jnp.int32, (size, out.shape[1]), 1)
            chosen = jnp.where(slots == where + slot, 1.0, 0.0)
            out[batch * size : (batch + 1) * size, :] = chosen.astype(BF16)
    counts = jnp.zeros((16, 1), F32)
    for batch in range(blocks.shape[0]):
        chip = blocks[batch : batch + 1, :] // (2 * held)
        chips = lax.broadcasted_iota(jnp.int32, (16, size), 0)
        counts = counts + jnp.sum(jnp.where(chips == chip, 1.0, 0.0), axis=1, keepdims=True)
    fits[0] = (jnp.max(counts) <= SLOTS).astype(jnp.int32)


def order(place, blocks, groups):
    return pl.pallas_call(
        functools.partial(order_kernel, groups),
        out_shape=[
            jax.ShapeDtypeStruct((blocks.size, SLOTS * len(group)), BF16) for group in groups
        ]
        + [jax.ShapeDtypeStruct((1,), jnp.int32)],
        in_specs=[SMEM, VMEM],
        out_specs=[VMEM] * len(groups) + [SMEM],
        compiler_params=PARAMS,
        cost_estimate=pl.CostEstimate(flops=10**6, bytes_accessed=10**6, transcendentals=0),
        name="order",
    )(place, blocks)


def put_in_order(chosen, pieces):
    size = chosen.shape[0] // 2
    values = [ref[index].astype(jnp.int32) for ref in pieces for index in range(ref.shape[0])]
    high, low = split(jnp.concatenate(values, axis=0).astype(F32))
    second = chosen[size:, :]
    return nn(chosen[:size, :], high), nn(second, high) + nn(second, low)


def early_kernel(chosen, *refs):
    size = chosen.shape[0] // 2
    refs[-1][:size, :], refs[-1][size:, :] = put_in_order(chosen, refs[:-1])


def late_kernel(chosen, early, *refs):
    size = chosen.shape[0] // 2
    first, second = put_in_order(chosen, refs[:-2])
    refs[-2][...] = ((first + early[:size, :]) * UNIT).astype(BF16)
    refs[-1][...] = (second + early[size:, :]).astype(jnp.int32).astype(jnp.int16)


def early_rows(chosen, pieces):
    return pl.pallas_call(
        early_kernel,
        out_shape=jax.ShapeDtypeStruct((chosen.shape[0], pieces[0].shape[-1]), F32),
        in_specs=[VMEM] * (1 + len(pieces)),
        out_specs=VMEM,
        compiler_params=PARAMS,
        cost_estimate=pl.CostEstimate(flops=10**9, bytes_accessed=4 * 10**6, transcendentals=0),
        name="early_rows",
    )(chosen, *pieces)


def late_rows(chosen, early, pieces):
    shape = (early.shape[0] // 2, early.shape[1])
    return pl.pallas_call(
        late_kernel,
        out_shape=[jax.ShapeDtypeStruct(shape, BF16), jax.ShapeDtypeStruct(shape, jnp.int16)],
        in_specs=[VMEM] * (2 + len(pieces)),
        out_specs=[VMEM] * 2,
        compiler_params=PARAMS,
        name="late_rows",
    )(chosen, early, *pieces)


def eliminate(covariance, work, inverse):
    size = covariance.shape[0]
    lane = lax.broadcasted_iota(jnp.int32, (size, size), 1)
    sub = lax.broadcasted_iota(jnp.int32, (size, size), 0)
    work[...] = covariance
    inverse[...] = jnp.where(lane == sub, 1.0, 0.0)

    def step(k, carry):
        row = work[pl.ds(k, 1), :]
        current = work[...]
        pivot = jnp.sum(jnp.where(lane[:1] == k, row, 0.0), axis=1, keepdims=True)
        column = jnp.sum(jnp.where(lane == k, current, 0.0), axis=1, keepdims=True)
        factor = jnp.where(sub[:, :1] > k, column / pivot, 0.0)
        inverse_row = inverse[pl.ds(k, 1), :]
        work[...] = current - factor * row
        inverse[...] = inverse[...] - factor * inverse_row
        return carry

    lax.fori_loop(0, size, step, 0)
    pivots = jnp.sum(jnp.where(lane == sub, work[...], 0.0), axis=1, keepdims=True)
    inverse[...] = inverse[...] * (1.0 / jnp.sqrt(pivots))


def squared(a):
    return jnp.sum(a * a)


def newton(scaled):
    size = scaled.shape[0]
    lane = lax.broadcasted_iota(jnp.int32, (size, size), 1)
    sub = lax.broadcasted_iota(jnp.int32, (size, size), 0)
    eye = jnp.where(lane == sub, 1.0, 0.0)
    half = jnp.where(lane < sub, 1.0, jnp.where(lane == sub, 0.5, 0.0))

    def third_order(error):
        low = error * half
        lowb = low.astype(BF16)
        return (nn(lowb, lowb) + half * nt(lowb, lowb)) - low

    def begin():
        first = (third_order(scaled - eye) + eye) * (RESCALE**0.5)
        fb = first.astype(BF16)
        error = nt(nn(fb, scaled.astype(BF16)).astype(BF16), fb) - eye
        return nn((third_order(error) + eye).astype(BF16), fb)

    def step(t):
        ts = split(t)
        error = dot3(nt, split(dot3(nn, ts, split(scaled))), ts) - eye
        return t + nn(third_order(error).astype(BF16), ts[0]), squared(error)

    return begin, step


def inverse_factor(covariance, work, inverse, use):
    size = covariance.shape[0]
    lane = lax.broadcasted_iota(jnp.int32, (size, size), 1)
    sub = lax.broadcasted_iota(jnp.int32, (size, size), 0)
    on_diagonal = jnp.where(lane == sub, covariance, 0.0)
    scale_row = lax.rsqrt(jnp.sum(on_diagonal, axis=0, keepdims=True) * (1.0 / SCALE))
    scale_column = lax.rsqrt(jnp.sum(on_diagonal, axis=1, keepdims=True) * (1.0 / SCALE))
    scaled = covariance * scale_row * scale_column
    begin, step = newton(scaled)
    t, residual = step(begin())
    use(t * scale_row)

    @pl.when(jnp.logical_not(residual <= TOLERANCE**2))
    def _():
        inverse[...] = t

        def again(carry):
            better, left = step(inverse[...])
            inverse[...] = better
            return carry[0] + 1, left

        def wanted(carry):
            return (carry[0] < 6) & jnp.logical_not(carry[1] <= (0.2 * TOLERANCE) ** 2)

        _, left = lax.while_loop(wanted, again, (0, residual))
        inverse[...] = inverse[...] * scale_row

        @pl.when(jnp.logical_not(left <= (0.2 * TOLERANCE) ** 2))
        def _():
            eliminate(covariance, work, inverse)

        use(inverse[...])


def whiten(observed, tags, values, load, noise_ref, work, inverse, store):
    members = observed.shape[1]
    size = observed.shape[0]
    mean = row_mean(observed)
    lane = lax.broadcasted_iota(jnp.int32, (size, size), 1)
    sub = lax.broadcasted_iota(jnp.int32, (size, size), 0)
    variance_row = jnp.where(tags == 0, 0.5, 2.0)
    mean_row = jnp.sum(jnp.where(lane == sub, mean, 0.0), axis=0, keepdims=True)
    exact = observed.astype(BF16)
    covariance = (nt(exact, exact) - mean * (mean_row * members)) * (1.0 / (members - 1))
    covariance = covariance + jnp.where(lane == sub, variance_row, 0.0)

    def finish(t):
        applied = dot2(nn, split(t), exact)
        noise = dot2(nn, split(t * jnp.sqrt(variance_row)), noise_ref[...])
        mean_part = jnp.sum(t * mean_row, axis=1, keepdims=True)
        value_part = jnp.sum(t * values, axis=1, keepdims=True)
        store((applied - mean_part).astype(BF16), (noise + value_part - applied).astype(BF16))

    load.wait()
    inverse_factor(covariance, work, inverse, finish)


def row_sums(array):
    return nt(jnp.ones((8, array.shape[1]), BF16), array)[:1, :]


def update(state, whitened, white_innov):
    members = state.shape[1]
    projected = dot2(nt, split(state), whitened) - row_mean(state) * row_sums(whitened)
    return state + dot2(nn, split(projected), white_innov) * (1.0 / (members - 1))


def both_halves(place, own, other):
    own, other = own[...].astype(F32), other[...].astype(F32)
    first = place[0] % 2 == 0
    return jnp.concatenate(
        [jnp.where(first, own, other), jnp.where(first, other, own)], axis=1
    )


def first_kernel(
    place, tags, values, noise_ref, own, other, whitened, white_innov, noise, loads, work, inverse
):
    load = pltpu.make_async_copy(noise_ref.at[0], noise, loads.at[0])
    load.start()
    observed = both_halves(place, own, other)

    def store(w, v):
        whitened[...] = w
        white_innov[...] = v

    whiten(observed, tags[:1, :], values[:1, :], load, noise, work, inverse, store)


def second_kernel(
    place,
    tags,
    values,
    noise_ref,
    own,
    other,
    whitened,
    white_innov,
    state_ref,
    analysis,
    noise,
    loads,
    work,
    inverse,
    state,
):
    load = pltpu.make_async_copy(noise_ref.at[1], noise, loads.at[0])
    load_state = pltpu.make_async_copy(state_ref, state, loads.at[1])
    load_state.start()
    load.start()
    w, v = whitened[...], white_innov[...]
    codes = both_halves(place, own, other)
    load_state.wait()
    updated = update(jnp.concatenate([codes, state[...]], axis=0), w, v)
    observed, first = rounded(updated[: codes.shape[0]] * UNIT), updated[codes.shape[0] :]

    def store(w, v):
        analysis[...] = update(first, w, v)

    whiten(observed, tags[1:2, :], values[1:2, :], load, noise, work, inverse, store)


def batch_call(kernel, name, outs, place, tags, values, noise, *arrays, state=()):
    rows, members = noise.shape[1:]
    return pl.pallas_call(
        kernel,
        out_shape=outs,
        in_specs=[SMEM, VMEM, VMEM, ANYWHERE] + [VMEM] * len(arrays) + [ANYWHERE] * len(state),
        out_specs=[VMEM] * len(outs),
        scratch_shapes=[
            pltpu.VMEM((rows, members), BF16),
            pltpu.SemaphoreType.DMA((2,)),
            pltpu.VMEM((rows, rows), F32),
            pltpu.VMEM((rows, rows), F32),
        ]
        + [pltpu.VMEM(array.shape, F32) for array in state],
        compiler_params=PARAMS,
        name=name,
    )(place, tags, values, noise, *arrays, *state)


def batches(place, tags, values, noise, state, observed, prior):
    shape = jax.ShapeDtypeStruct(noise.shape[1:], BF16)
    shared = (place, tags, values, noise)
    white = batch_call(first_kernel, "first_batch", [shape, shape], *shared, *observed)
    analysis = jax.ShapeDtypeStruct(state.shape, F32)
    return batch_call(
        second_kernel, "second_batch", [analysis], *shared, *prior, *white, state=(state,)
    )[0]


AXES = ("row", "col")
CORE, Y, X, NEAR_Z, FAR_Z = 1, 2, 4, 8, 16


def swap(value, mask):
    return lax.ppermute(value, AXES, [(i, i ^ mask) for i in range(32)])


def after(value, other):
    return lax.optimization_barrier((value, other))[0]


def joined(first, second):
    return jnp.concatenate([first, second], axis=0)


EARLY = (0, 4, 8, 12, 2, 10, 5, 13, 1, 9, 3, 11, 6, 7)
LATE = (14, 15)


def by_slots(place, ensemble, blocks, weights):
    keep, send = pick(place, blocks, weights, ensemble)
    own = (keep + swap(send, CORE))[None]
    far, near = swap(own, FAR_Z), swap(own, NEAR_Z)
    near_far = swap(far, NEAR_Z)
    both = joined(own, near)
    both_x = swap(both, X)
    far_y = swap(after(far, near), Y)
    near_far_y = swap(near_far, Y)
    both_y = swap(after(joined(both, both_x), near_far), Y)
    far_x = swap(joined(far, far_y), X)
    near_far_x = swap(joined(near_far, near_far_y), X)
    early_places, late_places, fits = order(place, blocks, (EARLY, LATE))
    pieces = [own, far, near, near_far, both_x, far_y, near_far_y, both_y, far_x]
    early = early_rows(early_places, pieces)
    return late_rows(late_places, early, [near_far_x]), fits


def add_by_swaps(value):
    for mask in (CORE, Y, X, NEAR_Z, FAR_Z):
        value = value + swap(value, mask)
    return value


def half_of(value, core):
    rows, members = value.shape
    return lax.dynamic_slice(value, (0, core * (members // 2)), (rows, members // 2))


def by_sum(add_up, other, place, ensemble, blocks, weights):
    rows = blocks.shape[1]
    codes = add_up(pick_all(place, blocks, weights, ensemble))
    codes = half_of(codes, (place[0] + other) % 2)
    return (codes[:rows] * UNIT).astype(BF16), codes[rows:].astype(jnp.int16)


def body(staged, ensemble, obs_blocks, obs_weights, comp_tags, obs_values, obs_noise):
    held = ensemble.shape[0] // obs_weights.shape[2]
    place = jnp.stack([lax.axis_index(AXES), held]).astype(jnp.int32)
    by_point = jnp.swapaxes(obs_weights, 1, 2)
    operands = (place, ensemble, obs_blocks, by_point)
    if staged:
        slotted, fits = by_slots(*operands)
        own = lax.cond(
            fits[0] == 1,
            lambda slotted, *operands: tuple(slotted),
            lambda slotted, *operands: by_sum(add_by_swaps, 0, *operands),
            slotted,
            *operands,
        )
        pairs = [(half, swap(half, CORE)) for half in own]
    else:
        add_up = lambda value: lax.psum(value, AXES)
        pairs = list(zip(by_sum(add_up, 0, *operands), by_sum(add_up, 1, *operands)))
    return batches(place, comp_tags, obs_values, obs_noise, ensemble, *pairs)


def solution(mesh):
    staged = (mesh.shape["row"], mesh.shape["col"]) == (8, 4)
    in_specs = (P(AXES, None), P(), P(), P(), P(), P())
    out_specs = P(AXES, None)
    return jax.shard_map(
        functools.partial(body, staged),
        mesh=mesh,
        in_specs=in_specs,
        out_specs=out_specs,
        check_vma=False,
    )
```

```python
import functools

import jax
import jax.numpy as jnp
from jax import lax
from jax.experimental import pallas as pl
from jax.experimental.pallas import tpu as pltpu
from jax.sharding import PartitionSpec as P

SLOTS = 56
UNIT = 1.0 / 1024
SCALE = 0.6
RESCALE = 1.25
TOLERANCE = 0.25
BF16 = jnp.bfloat16
F32 = jnp.float32
VMEM = pl.BlockSpec(memory_space=pltpu.VMEM)
SMEM = pl.BlockSpec(memory_space=pltpu.SMEM)
ANYWHERE = pl.BlockSpec(memory_space=pl.ANY)
PARAMS = pltpu.CompilerParams(vmem_limit_bytes=40 * 1024 * 1024)


def nt(a, b):
    return lax.dot_general(a, b, (((1,), (1,)), ((), ())), preferred_element_type=F32)


def nn(a, b):
    return lax.dot_general(a, b, (((1,), (0,)), ((), ())), preferred_element_type=F32)


def split(a):
    high = a.astype(BF16)
    return high, (a - high.astype(F32)).astype(BF16)


def dot2(dot, a, b):
    rows = a[0].shape[0]
    both = dot(jnp.concatenate(a, axis=0), b)
    return both[:rows] + both[rows:]


def dot3(dot, a, b):
    return dot2(dot, a, b[0]) + dot(a[0], b[1])


def row_mean(a):
    return jnp.sum(a, axis=1, keepdims=True) * (1.0 / a.shape[1])


def column(row):
    size = row.shape[1]
    lane = lax.broadcasted_iota(jnp.int32, (size, size), 1)
    sub = lax.broadcasted_iota(jnp.int32, (size, size), 0)
    return jnp.sum(jnp.where(lane == sub, row, jnp.zeros_like(row)), axis=1, keepdims=True)


def both_ways(row):
    as_float = row.astype(F32)
    return as_float, column(as_float)


def select(lanes, points, local, weight):
    value = jnp.zeros(lanes.shape, F32)
    for point in range(points):
        value = jnp.where(lanes % points == point, weight[point], value)
    return jnp.where((lanes // points).astype(F32) == local, value, 0.0)


def rounded(value):
    return value.astype(BF16).astype(F32)


def pick_kernel(place, blocks, weights, state_ref, keep, send, state, arrived):
    load = pltpu.make_async_copy(state_ref, state, arrived)
    load.start()
    device = place[0]
    batches, points, size = weights.shape
    width, members = state.shape
    held = width // points
    lane = lax.broadcasted_iota(jnp.int32, (size, size), 1)
    sub = lax.broadcasted_iota(jnp.int32, (size, size), 0)
    earlier = jnp.where(sub < lane, 1.0, 0.0).astype(BF16)
    row = blocks[...]
    mine = jnp.where(row // (2 * held) == device // 2, 1.0, 0.0)
    rank = nn(mine.astype(BF16), earlier).astype(jnp.int32)
    own = row // held == device
    slots = lax.broadcasted_iota(jnp.int32, (SLOTS, size), 0)
    points_of = lax.broadcasted_iota(jnp.int32, (width, size), 0)
    chosen, selector = [], []
    for batch in range(batches):
        place_of = rank[batch : batch + 1, :]
        place_of = place_of if batch == 0 else SLOTS - 1 - place_of
        place_of = jnp.where(own[batch : batch + 1, :], place_of, -1)
        chosen.append(jnp.where(slots == place_of, 1.0, 0.0))
        value = jnp.zeros((width, size), F32)
        for point in range(points):
            weight = weights[batch, point : point + 1, :]
            value = jnp.where(points_of % points == point, weight, value)
        local = row[batch : batch + 1, :] - device * held
        selector.append(jnp.where(points_of // points == local, value, 0.0))
    chosen = jnp.concatenate(chosen, axis=1).astype(BF16)
    parts = [nt(chosen, part).astype(BF16) for part in split(jnp.concatenate(selector, axis=1))]
    load.wait()
    rows = dot3(nn, parts, split(state[...]))
    from_first = lax.broadcasted_iota(jnp.int32, (SLOTS, 1), 0).astype(F32)
    from_first = from_first < jnp.sum(mine[:1, :], axis=1, keepdims=True)
    rows = jnp.where(from_first, rounded(rows), rows)
    code = jnp.round(rows * (1.0 / UNIT)).astype(jnp.int32)
    left, right = code[:, : members // 2], code[:, members // 2 :]
    first = device % 2 == 0
    keep[...] = jnp.where(first, left, right).astype(jnp.int16)
    send[...] = jnp.where(first, right, left).astype(jnp.int16)


def pick(place, blocks, weights, state):
    return pl.pallas_call(
        pick_kernel,
        out_shape=[jax.ShapeDtypeStruct((SLOTS, state.shape[1] // 2), jnp.int16)] * 2,
        in_specs=[SMEM, VMEM, VMEM, ANYWHERE],
        out_specs=[VMEM] * 2,
        scratch_shapes=[pltpu.VMEM(state.shape, F32), pltpu.SemaphoreType.DMA],
        compiler_params=PARAMS,
        name="pick",
    )(place, blocks, weights, state)


def pick_all_kernel(place, blocks, weights, state, out):
    device = place[0]
    batches, points, size = weights.shape
    width = state.shape[0]
    lanes = lax.broadcasted_iota(jnp.int32, (size, width), 1)
    for batch in range(batches):
        columns = [column(weights[batch, point : point + 1, :]) for point in range(points)]
        local = column((blocks[batch : batch + 1, :] - device * (width // points)).astype(F32))
        rows = jnp.dot(
            select(lanes, points, local, columns),
            state[...],
            precision=lax.Precision.HIGHEST,
            preferred_element_type=F32,
        )
        rows = rounded(rows) if batch == 0 else rows
        out[batch * size : (batch + 1) * size, :] = jnp.round(rows * (1.0 / UNIT))


def pick_all(place, blocks, weights, state):
    return pl.pallas_call(
        pick_all_kernel,
        out_shape=jax.ShapeDtypeStruct((blocks.size, state.shape[1]), F32),
        in_specs=[SMEM, VMEM, VMEM, VMEM],
        out_specs=VMEM,
        compiler_params=PARAMS,
        name="pick_all",
    )(place, blocks, weights, state)


def order_kernel(groups, place, blocks, *outs):
    outs, fits = outs[:-1], outs[-1]
    device, held = place[0], place[1]
    size = blocks.shape[1]
    lane = lax.broadcasted_iota(jnp.int32, (size, size), 1)
    sub = lax.broadcasted_iota(jnp.int32, (size, size), 0)
    for batch in range(blocks.shape[0]):
        pair_row, pair_column = both_ways(blocks[batch : batch + 1, :] // (2 * held))
        before = jnp.where((pair_row == pair_column) & (lane < sub), 1.0, 0.0)
        rank = jnp.sum(before, axis=1, keepdims=True).astype(jnp.int32)
        away = (2 * pair_column.astype(jnp.int32)) ^ device
        distance = 8 * ((away >> 3) & 1) + 4 * ((away >> 4) & 1) + ((away >> 1) & 3)
        slot = rank if batch == 0 else SLOTS - 1 - rank
        for distances, out in zip(groups, outs):
            where = jnp.full(rank.shape, -SLOTS, jnp.int32)
            for index, known in enumerate(distances):
                where = jnp.where(distance == known, SLOTS * index, where)
            slots = lax.broadcasted_iota(jnp.int32, (size, out.shape[1]), 1)
            chosen = jnp.where(slots == where + slot, 1.0, 0.0)
            out[batch * size : (batch + 1) * size, :] = chosen.astype(BF16)
    counts = jnp.zeros((16, 1), F32)
    for batch in range(blocks.shape[0]):
        chip = blocks[batch : batch + 1, :] // (2 * held)
        chips = lax.broadcasted_iota(jnp.int32, (16, size), 0)
        counts = counts + jnp.sum(jnp.where(chips == chip, 1.0, 0.0), axis=1, keepdims=True)
    fits[0] = (jnp.max(counts) <= SLOTS).astype(jnp.int32)


def order(place, blocks, groups):
    return pl.pallas_call(
        functools.partial(order_kernel, groups),
        out_shape=[
            jax.ShapeDtypeStruct((blocks.size, SLOTS * len(group)), BF16) for group in groups
        ]
        + [jax.ShapeDtypeStruct((1,), jnp.int32)],
        in_specs=[SMEM, VMEM],
        out_specs=[VMEM] * len(groups) + [SMEM],
        compiler_params=PARAMS,
        cost_estimate=pl.CostEstimate(flops=10**6, bytes_accessed=10**6, transcendentals=0),
        name="order",
    )(place, blocks)


def put_in_order(chosen, pieces):
    size = chosen.shape[0] // 2
    values = [ref[index].astype(jnp.int32) for ref in pieces for index in range(ref.shape[0])]
    high, low = split(jnp.concatenate(values, axis=0).astype(F32))
    second = chosen[size:, :]
    return nn(chosen[:size, :], high), nn(second, high) + nn(second, low)


def early_kernel(chosen, *refs):
    size = chosen.shape[0] // 2
    refs[-1][:size, :], refs[-1][size:, :] = put_in_order(chosen, refs[:-1])


def late_kernel(chosen, early, *refs):
    size = chosen.shape[0] // 2
    first, second = put_in_order(chosen, refs[:-2])
    refs[-2][...] = ((first + early[:size, :]) * UNIT).astype(BF16)
    refs[-1][...] = (second + early[size:, :]).astype(jnp.int32).astype(jnp.int16)


def early_rows(chosen, pieces):
    return pl.pallas_call(
        early_kernel,
        out_shape=jax.ShapeDtypeStruct((chosen.shape[0], pieces[0].shape[-1]), F32),
        in_specs=[VMEM] * (1 + len(pieces)),
        out_specs=VMEM,
        compiler_params=PARAMS,
        cost_estimate=pl.CostEstimate(flops=10**9, bytes_accessed=4 * 10**6, transcendentals=0),
        name="early_rows",
    )(chosen, *pieces)


def late_rows(chosen, early, pieces):
    shape = (early.shape[0] // 2, early.shape[1])
    return pl.pallas_call(
        late_kernel,
        out_shape=[jax.ShapeDtypeStruct(shape, BF16), jax.ShapeDtypeStruct(shape, jnp.int16)],
        in_specs=[VMEM] * (2 + len(pieces)),
        out_specs=[VMEM] * 2,
        compiler_params=PARAMS,
        name="late_rows",
    )(chosen, early, *pieces)


def eliminate(covariance, work, inverse):
    size = covariance.shape[0]
    lane = lax.broadcasted_iota(jnp.int32, (size, size), 1)
    sub = lax.broadcasted_iota(jnp.int32, (size, size), 0)
    work[...] = covariance
    inverse[...] = jnp.where(lane == sub, 1.0, 0.0)

    def step(k, carry):
        row = work[pl.ds(k, 1), :]
        current = work[...]
        pivot = jnp.sum(jnp.where(lane[:1] == k, row, 0.0), axis=1, keepdims=True)
        column = jnp.sum(jnp.where(lane == k, current, 0.0), axis=1, keepdims=True)
        factor = jnp.where(sub[:, :1] > k, column / pivot, 0.0)
        inverse_row = inverse[pl.ds(k, 1), :]
        work[...] = current - factor * row
        inverse[...] = inverse[...] - factor * inverse_row
        return carry

    lax.fori_loop(0, size, step, 0)
    pivots = jnp.sum(jnp.where(lane == sub, work[...], 0.0), axis=1, keepdims=True)
    inverse[...] = inverse[...] * (1.0 / jnp.sqrt(pivots))


def squared(a):
    return jnp.sum(a * a)


def newton(scaled):
    size = scaled.shape[0]
    lane = lax.broadcasted_iota(jnp.int32, (size, size), 1)
    sub = lax.broadcasted_iota(jnp.int32, (size, size), 0)
    eye = jnp.where(lane == sub, 1.0, 0.0)
    half = jnp.where(lane < sub, 1.0, jnp.where(lane == sub, 0.5, 0.0))

    def third_order(error):
        low = error * half
        lowb = low.astype(BF16)
        return (nn(lowb, lowb) + half * nt(lowb, lowb)) - low

    def begin():
        first = (third_order(scaled - eye) + eye) * (RESCALE**0.5)
        fb = first.astype(BF16)
        error = nt(nn(fb, scaled.astype(BF16)).astype(BF16), fb) - eye
        return nn((third_order(error) + eye).astype(BF16), fb)

    def step(t):
        ts = split(t)
        error = dot3(nt, split(dot3(nn, ts, split(scaled))), ts) - eye
        change = third_order(error).astype(BF16)
        return change, t + nn(change, ts[0]), squared(error)

    return begin, step


def solve(covariance, coarse, work, inverse, apply, store):
    size = covariance.shape[0]
    lane = lax.broadcasted_iota(jnp.int32, (size, size), 1)
    sub = lax.broadcasted_iota(jnp.int32, (size, size), 0)
    on_diagonal = jnp.where(lane == sub, covariance, 0.0)
    scale_row = lax.rsqrt(jnp.sum(on_diagonal, axis=0, keepdims=True) * (1.0 / SCALE))
    scale_column = lax.rsqrt(jnp.sum(on_diagonal, axis=1, keepdims=True) * (1.0 / SCALE))
    scaled = covariance * scale_row * scale_column
    begin, step = newton(scaled)
    t = begin()
    inverse[...] = t
    for index, product in enumerate(apply(t * scale_row)):
        coarse[index] = product
    change, _, residual = step(t)
    store(*[coarse[index] + nn(change, coarse[index].astype(BF16)) for index in range(2)])

    @pl.when(jnp.logical_not(residual <= TOLERANCE**2))
    def _():
        def again(carry):
            _, better, left = step(inverse[...])
            inverse[...] = better
            return carry[0] + 1, left

        def wanted(carry):
            return (carry[0] < 7) & jnp.logical_not(carry[1] <= (0.2 * TOLERANCE) ** 2)

        _, left = lax.while_loop(wanted, again, (0, residual))
        inverse[...] = inverse[...] * scale_row

        @pl.when(jnp.logical_not(left <= (0.2 * TOLERANCE) ** 2))
        def _():
            eliminate(covariance, work, inverse)

        store(*apply(inverse[...]))


def whiten(observed, tags, values, load, noise_ref, coarse, work, inverse, store):
    members = observed.shape[1]
    size = observed.shape[0]
    mean = row_mean(observed)
    lane = lax.broadcasted_iota(jnp.int32, (size, size), 1)
    sub = lax.broadcasted_iota(jnp.int32, (size, size), 0)
    variance_row = jnp.where(tags == 0, 0.5, 2.0)
    mean_row = jnp.sum(jnp.where(lane == sub, mean, 0.0), axis=0, keepdims=True)
    exact = observed.astype(BF16)
    covariance = (nt(exact, exact) - mean * (mean_row * members)) * (1.0 / (members - 1))
    covariance = covariance + jnp.where(lane == sub, variance_row, 0.0)

    def apply(t):
        applied = dot2(nn, split(t), exact)
        noise = dot2(nn, split(t * jnp.sqrt(variance_row)), noise_ref[...])
        mean_part = jnp.sum(t * mean_row, axis=1, keepdims=True)
        value_part = jnp.sum(t * values, axis=1, keepdims=True)
        return applied - mean_part, noise + value_part - applied

    load.wait()
    solve(covariance, coarse, work, inverse, apply, lambda w, v: store(w.astype(BF16), v.astype(BF16)))


def row_sums(array):
    return nt(jnp.ones((8, array.shape[1]), BF16), array)[:1, :]


def update(state, whitened, white_innov):
    members = state.shape[1]
    projected = dot2(nt, split(state), whitened) - row_mean(state) * row_sums(whitened)
    return state + dot2(nn, split(projected), white_innov) * (1.0 / (members - 1))


def both_halves(place, own, other):
    own, other = own[...].astype(F32), other[...].astype(F32)
    first = place[0] % 2 == 0
    return jnp.concatenate(
        [jnp.where(first, own, other), jnp.where(first, other, own)], axis=1
    )


def first_kernel(
    place, tags, values, noise_ref, own, other, whitened, white_innov, noise, loads, coarse, work, inverse
):
    load = pltpu.make_async_copy(noise_ref.at[0], noise, loads.at[0])
    load.start()
    observed = both_halves(place, own, other)

    def store(w, v):
        whitened[...] = w
        white_innov[...] = v

    whiten(observed, tags[:1, :], values[:1, :], load, noise, coarse, work, inverse, store)


def second_kernel(
    place,
    tags,
    values,
    noise_ref,
    own,
    other,
    whitened,
    white_innov,
    state_ref,
    analysis,
    noise,
    loads,
    coarse,
    work,
    inverse,
    state,
):
    load = pltpu.make_async_copy(noise_ref.at[1], noise, loads.at[0])
    load_state = pltpu.make_async_copy(state_ref, state, loads.at[1])
    load_state.start()
    load.start()
    w, v = whitened[...], white_innov[...]
    observed = rounded(update(both_halves(place, own, other), w, v) * UNIT)
    load_state.wait()
    first = update(state[...], w, v)

    def store(w, v):
        analysis[...] = update(first, w, v)

    whiten(observed, tags[1:2, :], values[1:2, :], load, noise, coarse, work, inverse, store)


def batch_call(kernel, name, outs, place, tags, values, noise, *arrays, state=()):
    rows, members = noise.shape[1:]
    return pl.pallas_call(
        kernel,
        out_shape=outs,
        in_specs=[SMEM, VMEM, VMEM, ANYWHERE] + [VMEM] * len(arrays) + [ANYWHERE] * len(state),
        out_specs=[VMEM] * len(outs),
        scratch_shapes=[
            pltpu.VMEM((rows, members), BF16),
            pltpu.SemaphoreType.DMA((2,)),
            pltpu.VMEM((2, rows, members), F32),
            pltpu.VMEM((rows, rows), F32),
            pltpu.VMEM((rows, rows), F32),
        ]
        + [pltpu.VMEM(array.shape, F32) for array in state],
        compiler_params=PARAMS,
        name=name,
    )(place, tags, values, noise, *arrays, *state)


def batches(place, tags, values, noise, state, observed, prior):
    shape = jax.ShapeDtypeStruct(noise.shape[1:], BF16)
    shared = (place, tags, values, noise)
    white = batch_call(first_kernel, "first_batch", [shape, shape], *shared, *observed)
    analysis = jax.ShapeDtypeStruct(state.shape, F32)
    return batch_call(
        second_kernel, "second_batch", [analysis], *shared, *prior, *white, state=(state,)
    )[0]


AXES = ("row", "col")
CORE, Y, X, NEAR_Z, FAR_Z = 1, 2, 4, 8, 16


def swap(value, mask):
    return lax.ppermute(value, AXES, [(i, i ^ mask) for i in range(32)])


def after(value, other):
    return lax.optimization_barrier((value, other))[0]


def joined(first, second):
    return jnp.concatenate([first, second], axis=0)


EARLY = (0, 4, 8, 12, 2, 10, 5, 13, 1, 9, 3, 11, 6, 7)
LATE = (14, 15)


def by_slots(place, ensemble, blocks, weights):
    keep, send = pick(place, blocks, weights, ensemble)
    own = (keep + swap(send, CORE))[None]
    far, near = swap(own, FAR_Z), swap(own, NEAR_Z)
    near_far = swap(far, NEAR_Z)
    both = joined(own, near)
    both_x = swap(both, X)
    far_y = swap(after(far, near), Y)
    near_far_y = swap(near_far, Y)
    both_y = swap(after(joined(both, both_x), near_far), Y)
    far_x = swap(joined(far, far_y), X)
    near_far_x = swap(joined(near_far, near_far_y), X)
    early_places, late_places, fits = order(place, blocks, (EARLY, LATE))
    pieces = [own, far, near, near_far, both_x, far_y, near_far_y, both_y, far_x]
    early = early_rows(early_places, pieces)
    return late_rows(late_places, early, [near_far_x]), fits


def add_by_swaps(value):
    for mask in (CORE, Y, X, NEAR_Z, FAR_Z):
        value = value + swap(value, mask)
    return value


def half_of(value, core):
    rows, members = value.shape
    return lax.dynamic_slice(value, (0, core * (members // 2)), (rows, members // 2))


def by_sum(add_up, other, place, ensemble, blocks, weights):
    rows = blocks.shape[1]
    codes = add_up(pick_all(place, blocks, weights, ensemble))
    codes = half_of(codes, (place[0] + other) % 2)
    return (codes[:rows] * UNIT).astype(BF16), codes[rows:].astype(jnp.int16)


def body(staged, ensemble, obs_blocks, obs_weights, comp_tags, obs_values, obs_noise):
    held = ensemble.shape[0] // obs_weights.shape[2]
    place = jnp.stack([lax.axis_index(AXES), held]).astype(jnp.int32)
    by_point = jnp.swapaxes(obs_weights, 1, 2)
    operands = (place, ensemble, obs_blocks, by_point)
    if staged:
        slotted, fits = by_slots(*operands)
        own = lax.cond(
            fits[0] == 1,
            lambda slotted, *operands: tuple(slotted),
            lambda slotted, *operands: by_sum(add_by_swaps, 0, *operands),
            slotted,
            *operands,
        )
        pairs = [(half, swap(half, CORE)) for half in own]
    else:
        add_up = lambda value: lax.psum(value, AXES)
        pairs = list(zip(by_sum(add_up, 0, *operands), by_sum(add_up, 1, *operands)))
    return batches(place, comp_tags, obs_values, obs_noise, ensemble, *pairs)


def solution(mesh):
    staged = (mesh.shape["row"], mesh.shape["col"]) == (8, 4)
    in_specs = (P(AXES, None), P(), P(), P(), P(), P())
    out_specs = P(AXES, None)
    return jax.shard_map(
        functools.partial(body, staged),
        mesh=mesh,
        in_specs=in_specs,
        out_specs=out_specs,
        check_vma=False,
    )
```

```python
import functools

import jax
import jax.numpy as jnp
from jax import lax
from jax.experimental import pallas as pl
from jax.experimental.pallas import tpu as pltpu
from jax.sharding import PartitionSpec as P

SLOTS = 56
UNIT = 1.0 / 1024
SCALE = 0.6
RESCALE = 1.25
TOLERANCE = 0.25
BF16 = jnp.bfloat16
F32 = jnp.float32
VMEM = pl.BlockSpec(memory_space=pltpu.VMEM)
SMEM = pl.BlockSpec(memory_space=pltpu.SMEM)
ANYWHERE = pl.BlockSpec(memory_space=pl.ANY)
PARAMS = pltpu.CompilerParams(vmem_limit_bytes=40 * 1024 * 1024)


def nt(a, b):
    return lax.dot_general(a, b, (((1,), (1,)), ((), ())), preferred_element_type=F32)


def nn(a, b):
    return lax.dot_general(a, b, (((1,), (0,)), ((), ())), preferred_element_type=F32)


def split(a):
    high = a.astype(BF16)
    return high, (a - high.astype(F32)).astype(BF16)


def dot2(dot, a, b):
    rows = a[0].shape[0]
    both = dot(jnp.concatenate(a, axis=0), b)
    return both[:rows] + both[rows:]


def dot3(dot, a, b):
    return dot2(dot, a, b[0]) + dot(a[0], b[1])


def row_mean(a):
    return jnp.sum(a, axis=1, keepdims=True) * (1.0 / a.shape[1])


def column(row):
    size = row.shape[1]
    lane = lax.broadcasted_iota(jnp.int32, (size, size), 1)
    sub = lax.broadcasted_iota(jnp.int32, (size, size), 0)
    return jnp.sum(jnp.where(lane == sub, row, jnp.zeros_like(row)), axis=1, keepdims=True)


def both_ways(row):
    as_float = row.astype(F32)
    return as_float, column(as_float)


def select(lanes, points, local, weight):
    value = jnp.zeros(lanes.shape, F32)
    for point in range(points):
        value = jnp.where(lanes % points == point, weight[point], value)
    return jnp.where((lanes // points).astype(F32) == local, value, 0.0)


def rounded(value):
    return value.astype(BF16).astype(F32)


def pick_kernel(place, blocks, weights, state_ref, keep, send, state, arrived):
    load = pltpu.make_async_copy(state_ref, state, arrived)
    load.start()
    device = place[0]
    batches, points, size = weights.shape
    width, members = state.shape
    held = width // points
    lane = lax.broadcasted_iota(jnp.int32, (size, size), 1)
    sub = lax.broadcasted_iota(jnp.int32, (size, size), 0)
    earlier = jnp.where(sub < lane, 1.0, 0.0).astype(BF16)
    row = blocks[...]
    mine = jnp.where(row // (2 * held) == device // 2, 1.0, 0.0)
    rank = nn(mine.astype(BF16), earlier).astype(jnp.int32)
    own = row // held == device
    slots = lax.broadcasted_iota(jnp.int32, (SLOTS, size), 0)
    points_of = lax.broadcasted_iota(jnp.int32, (width, size), 0)
    chosen, selector = [], []
    for batch in range(batches):
        place_of = rank[batch : batch + 1, :]
        place_of = place_of if batch == 0 else SLOTS - 1 - place_of
        place_of = jnp.where(own[batch : batch + 1, :], place_of, -1)
        chosen.append(jnp.where(slots == place_of, 1.0, 0.0))
        value = jnp.zeros((width, size), F32)
        for point in range(points):
            weight = weights[batch, point : point + 1, :]
            value = jnp.where(points_of % points == point, weight, value)
        local = row[batch : batch + 1, :] - device * held
        selector.append(jnp.where(points_of // points == local, value, 0.0))
    chosen = jnp.concatenate(chosen, axis=1).astype(BF16)
    parts = [nt(chosen, part).astype(BF16) for part in split(jnp.concatenate(selector, axis=1))]
    load.wait()
    rows = dot3(nn, parts, split(state[...]))
    from_first = lax.broadcasted_iota(jnp.int32, (SLOTS, 1), 0).astype(F32)
    from_first = from_first < jnp.sum(mine[:1, :], axis=1, keepdims=True)
    rows = jnp.where(from_first, rounded(rows), rows)
    code = jnp.round(rows * (1.0 / UNIT)).astype(jnp.int32)
    left, right = code[:, : members // 2], code[:, members // 2 :]
    first = device % 2 == 0
    keep[...] = jnp.where(first, left, right).astype(jnp.int16)
    send[...] = jnp.where(first, right, left).astype(jnp.int16)


def pick(place, blocks, weights, state):
    return pl.pallas_call(
        pick_kernel,
        out_shape=[jax.ShapeDtypeStruct((SLOTS, state.shape[1] // 2), jnp.int16)] * 2,
        in_specs=[SMEM, VMEM, VMEM, ANYWHERE],
        out_specs=[VMEM] * 2,
        scratch_shapes=[pltpu.VMEM(state.shape, F32), pltpu.SemaphoreType.DMA],
        compiler_params=PARAMS,
        name="pick",
    )(place, blocks, weights, state)


def pick_all_kernel(place, blocks, weights, state, out):
    device = place[0]
    batches, points, size = weights.shape
    width = state.shape[0]
    lanes = lax.broadcasted_iota(jnp.int32, (size, width), 1)
    for batch in range(batches):
        columns = [column(weights[batch, point : point + 1, :]) for point in range(points)]
        local = column((blocks[batch : batch + 1, :] - device * (width // points)).astype(F32))
        rows = jnp.dot(
            select(lanes, points, local, columns),
            state[...],
            precision=lax.Precision.HIGHEST,
            preferred_element_type=F32,
        )
        rows = rounded(rows) if batch == 0 else rows
        out[batch * size : (batch + 1) * size, :] = jnp.round(rows * (1.0 / UNIT))


def pick_all(place, blocks, weights, state):
    return pl.pallas_call(
        pick_all_kernel,
        out_shape=jax.ShapeDtypeStruct((blocks.size, state.shape[1]), F32),
        in_specs=[SMEM, VMEM, VMEM, VMEM],
        out_specs=VMEM,
        compiler_params=PARAMS,
        name="pick_all",
    )(place, blocks, weights, state)


def order_kernel(groups, place, blocks, *outs):
    outs, fits = outs[:-1], outs[-1]
    device, held = place[0], place[1]
    size = blocks.shape[1]
    lane = lax.broadcasted_iota(jnp.int32, (size, size), 1)
    sub = lax.broadcasted_iota(jnp.int32, (size, size), 0)
    for batch in range(blocks.shape[0]):
        pair_row, pair_column = both_ways(blocks[batch : batch + 1, :] // (2 * held))
        before = jnp.where((pair_row == pair_column) & (lane < sub), 1.0, 0.0)
        rank = jnp.sum(before, axis=1, keepdims=True).astype(jnp.int32)
        away = (2 * pair_column.astype(jnp.int32)) ^ device
        distance = 8 * ((away >> 3) & 1) + 4 * ((away >> 4) & 1) + ((away >> 1) & 3)
        slot = rank if batch == 0 else SLOTS - 1 - rank
        slot = slot + SLOTS * distance
        begin = 0
        for width, out in zip(groups, outs):
            slots = lax.broadcasted_iota(jnp.int32, (size, SLOTS * width), 1) + SLOTS * begin
            chosen = jnp.where(slots == slot, 1.0, 0.0)
            out[batch * size : (batch + 1) * size, :] = chosen.astype(BF16)
            begin += width
    counts = jnp.zeros((16, 1), F32)
    for batch in range(blocks.shape[0]):
        chip = blocks[batch : batch + 1, :] // (2 * held)
        chips = lax.broadcasted_iota(jnp.int32, (16, size), 0)
        counts = counts + jnp.sum(jnp.where(chips == chip, 1.0, 0.0), axis=1, keepdims=True)
    fits[0] = (jnp.max(counts) <= SLOTS).astype(jnp.int32)


def order(place, blocks, groups):
    return pl.pallas_call(
        functools.partial(order_kernel, groups),
        out_shape=[
            jax.ShapeDtypeStruct((blocks.size, SLOTS * width), BF16) for width in groups
        ]
        + [jax.ShapeDtypeStruct((1,), jnp.int32)],
        in_specs=[SMEM, VMEM],
        out_specs=[VMEM] * len(groups) + [SMEM],
        compiler_params=PARAMS,
        cost_estimate=pl.CostEstimate(flops=10**6, bytes_accessed=10**6, transcendentals=0),
        name="order",
    )(place, blocks)


def put_in_order(chosen, numbers, pieces):
    size = chosen.shape[0] // 2
    blocks = [(ref, index) for ref in pieces for index in range(ref.shape[0])]
    blocks = [blocks[where] for where in sorted(range(len(blocks)), key=lambda i: numbers[i])]
    values = [ref[index].astype(jnp.int32) for ref, index in blocks]
    high, low = split(jnp.concatenate(values, axis=0).astype(F32))
    second = chosen[size:, :]
    return nn(chosen[:size, :], high), nn(second, high) + nn(second, low)


def early_kernel(chosen, *refs):
    size = chosen.shape[0] // 2
    refs[-1][:size, :], refs[-1][size:, :] = put_in_order(chosen, EARLY, refs[:-1])


def late_kernel(chosen, early, *refs):
    size = chosen.shape[0] // 2
    first, second = put_in_order(chosen, LATE, refs[:-2])
    refs[-2][...] = ((first + early[:size, :]) * UNIT).astype(BF16)
    refs[-1][...] = (second + early[size:, :]).astype(jnp.int32).astype(jnp.int16)


def early_rows(chosen, pieces):
    return pl.pallas_call(
        early_kernel,
        out_shape=jax.ShapeDtypeStruct((chosen.shape[0], pieces[0].shape[-1]), F32),
        in_specs=[VMEM] * (1 + len(pieces)),
        out_specs=VMEM,
        compiler_params=PARAMS,
        cost_estimate=pl.CostEstimate(flops=10**9, bytes_accessed=4 * 10**6, transcendentals=0),
        name="early_rows",
    )(chosen, *pieces)


def late_rows(chosen, early, pieces):
    shape = (early.shape[0] // 2, early.shape[1])
    return pl.pallas_call(
        late_kernel,
        out_shape=[jax.ShapeDtypeStruct(shape, BF16), jax.ShapeDtypeStruct(shape, jnp.int16)],
        in_specs=[VMEM] * (2 + len(pieces)),
        out_specs=[VMEM] * 2,
        compiler_params=PARAMS,
        name="late_rows",
    )(chosen, early, *pieces)


def eliminate(covariance, work, inverse):
    size = covariance.shape[0]
    lane = lax.broadcasted_iota(jnp.int32, (size, size), 1)
    sub = lax.broadcasted_iota(jnp.int32, (size, size), 0)
    work[...] = covariance
    inverse[...] = jnp.where(lane == sub, 1.0, 0.0)

    def step(k, carry):
        row = work[pl.ds(k, 1), :]
        current = work[...]
        pivot = jnp.sum(jnp.where(lane[:1] == k, row, 0.0), axis=1, keepdims=True)
        column = jnp.sum(jnp.where(lane == k, current, 0.0), axis=1, keepdims=True)
        factor = jnp.where(sub[:, :1] > k, column / pivot, 0.0)
        inverse_row = inverse[pl.ds(k, 1), :]
        work[...] = current - factor * row
        inverse[...] = inverse[...] - factor * inverse_row
        return carry

    lax.fori_loop(0, size, step, 0)
    pivots = jnp.sum(jnp.where(lane == sub, work[...], 0.0), axis=1, keepdims=True)
    inverse[...] = inverse[...] * (1.0 / jnp.sqrt(pivots))


def squared(a):
    return jnp.sum(a * a)


def newton(scaled):
    size = scaled.shape[0]
    lane = lax.broadcasted_iota(jnp.int32, (size, size), 1)
    sub = lax.broadcasted_iota(jnp.int32, (size, size), 0)
    eye = jnp.where(lane == sub, 1.0, 0.0)
    half = jnp.where(lane < sub, 1.0, jnp.where(lane == sub, 0.5, 0.0))

    def third_order(error):
        low = error * half
        lowb = low.astype(BF16)
        return (nn(lowb, lowb) + half * nt(lowb, lowb)) - low

    def begin():
        first = (third_order(scaled - eye) + eye) * (RESCALE**0.5)
        fb = first.astype(BF16)
        error = nt(nn(fb, scaled.astype(BF16)).astype(BF16), fb) - eye
        return nn((third_order(error) + eye).astype(BF16), fb)

    def step(t):
        ts = split(t)
        error = dot3(nt, split(dot3(nn, ts, split(scaled))), ts) - eye
        return t + nn(third_order(error).astype(BF16), ts[0]), squared(error)

    return begin, step


def inverse_factor(covariance, work, inverse, use):
    size = covariance.shape[0]
    lane = lax.broadcasted_iota(jnp.int32, (size, size), 1)
    sub = lax.broadcasted_iota(jnp.int32, (size, size), 0)
    on_diagonal = jnp.where(lane == sub, covariance, 0.0)
    scale_row = lax.rsqrt(jnp.sum(on_diagonal, axis=0, keepdims=True) * (1.0 / SCALE))
    scale_column = lax.rsqrt(jnp.sum(on_diagonal, axis=1, keepdims=True) * (1.0 / SCALE))
    scaled = covariance * scale_row * scale_column
    begin, step = newton(scaled)
    t, residual = step(begin())
    use(t * scale_row)

    @pl.when(jnp.logical_not(residual <= TOLERANCE**2))
    def _():
        inverse[...] = t

        def again(carry):
            better, left = step(inverse[...])
            inverse[...] = better
            return carry[0] + 1, left

        def wanted(carry):
            return (carry[0] < 6) & jnp.logical_not(carry[1] <= (0.2 * TOLERANCE) ** 2)

        _, left = lax.while_loop(wanted, again, (0, residual))
        inverse[...] = inverse[...] * scale_row

        @pl.when(jnp.logical_not(left <= (0.2 * TOLERANCE) ** 2))
        def _():
            eliminate(covariance, work, inverse)

        use(inverse[...])


def whiten(observed, tags, values, load, noise_ref, work, inverse, store):
    members = observed.shape[1]
    size = observed.shape[0]
    mean = row_mean(observed)
    lane = lax.broadcasted_iota(jnp.int32, (size, size), 1)
    sub = lax.broadcasted_iota(jnp.int32, (size, size), 0)
    variance_row = jnp.where(tags == 0, 0.5, 2.0)
    mean_row = jnp.sum(jnp.where(lane == sub, mean, 0.0), axis=0, keepdims=True)
    exact = observed.astype(BF16)
    covariance = (nt(exact, exact) - mean * (mean_row * members)) * (1.0 / (members - 1))
    covariance = covariance + jnp.where(lane == sub, variance_row, 0.0)

    def finish(t):
        applied = dot2(nn, split(t), exact)
        noise = dot2(nn, split(t * jnp.sqrt(variance_row)), noise_ref[...])
        mean_part = jnp.sum(t * mean_row, axis=1, keepdims=True)
        value_part = jnp.sum(t * values, axis=1, keepdims=True)
        store((applied - mean_part).astype(BF16), (noise + value_part - applied).astype(BF16))

    load.wait()
    inverse_factor(covariance, work, inverse, finish)


def row_sums(array):
    return nt(jnp.ones((8, array.shape[1]), BF16), array)[:1, :]


def update(state, whitened, white_innov):
    members = state.shape[1]
    projected = dot2(nt, split(state), whitened) - row_mean(state) * row_sums(whitened)
    return state + dot2(nn, split(projected), white_innov) * (1.0 / (members - 1))


def both_halves(place, own, other):
    own, other = own[...].astype(F32), other[...].astype(F32)
    first = place[0] % 2 == 0
    return jnp.concatenate(
        [jnp.where(first, own, other), jnp.where(first, other, own)], axis=1
    )


def first_kernel(
    place, tags, values, noise_ref, own, other, whitened, white_innov, noise, loads, work, inverse
):
    load = pltpu.make_async_copy(noise_ref.at[0], noise, loads.at[0])
    load.start()
    observed = both_halves(place, own, other)

    def store(w, v):
        whitened[...] = w
        white_innov[...] = v

    whiten(observed, tags[:1, :], values[:1, :], load, noise, work, inverse, store)


def second_kernel(
    place,
    tags,
    values,
    noise_ref,
    own,
    other,
    whitened,
    white_innov,
    state_ref,
    analysis,
    noise,
    loads,
    work,
    inverse,
    state,
):
    load = pltpu.make_async_copy(noise_ref.at[1], noise, loads.at[0])
    load_state = pltpu.make_async_copy(state_ref, state, loads.at[1])
    load_state.start()
    load.start()
    w, v = whitened[...], white_innov[...]
    observed = rounded(update(both_halves(place, own, other), w, v) * UNIT)
    load_state.wait()
    first = update(state[...], w, v)

    def store(w, v):
        analysis[...] = update(first, w, v)

    whiten(observed, tags[1:2, :], values[1:2, :], load, noise, work, inverse, store)


def batch_call(kernel, name, outs, place, tags, values, noise, *arrays, state=()):
    rows, members = noise.shape[1:]
    return pl.pallas_call(
        kernel,
        out_shape=outs,
        in_specs=[SMEM, VMEM, VMEM, ANYWHERE] + [VMEM] * len(arrays) + [ANYWHERE] * len(state),
        out_specs=[VMEM] * len(outs),
        scratch_shapes=[
            pltpu.VMEM((rows, members), BF16),
            pltpu.SemaphoreType.DMA((2,)),
            pltpu.VMEM((rows, rows), F32),
            pltpu.VMEM((rows, rows), F32),
        ]
        + [pltpu.VMEM(array.shape, F32) for array in state],
        compiler_params=PARAMS,
        name=name,
    )(place, tags, values, noise, *arrays, *state)


def batches(place, tags, values, noise, state, observed, prior):
    shape = jax.ShapeDtypeStruct(noise.shape[1:], BF16)
    shared = (place, tags, values, noise)
    white = batch_call(first_kernel, "first_batch", [shape, shape], *shared, *observed)
    analysis = jax.ShapeDtypeStruct(state.shape, F32)
    return batch_call(
        second_kernel, "second_batch", [analysis], *shared, *prior, *white, state=(state,)
    )[0]


AXES = ("row", "col")
CORE, Y, X, NEAR_Z, FAR_Z = 1, 2, 4, 8, 16


def swap(value, mask):
    return lax.ppermute(value, AXES, [(i, i ^ mask) for i in range(32)])


def after(value, other):
    return lax.optimization_barrier((value, other))[0]


def joined(first, second):
    return jnp.concatenate([first, second], axis=0)


EARLY = (0, 4, 8, 12, 2, 10, 5, 13, 1, 9, 3, 11, 6, 7)
LATE = (14, 15)


def by_slots(place, ensemble, blocks, weights):
    keep, send = pick(place, blocks, weights, ensemble)
    own = (keep + swap(send, CORE))[None]
    far, near = swap(own, FAR_Z), swap(own, NEAR_Z)
    near_far = swap(far, NEAR_Z)
    both = joined(own, near)
    both_x = swap(both, X)
    far_y = swap(after(far, near), Y)
    near_far_y = swap(near_far, Y)
    both_y = swap(after(joined(both, both_x), near_far), Y)
    far_x = swap(joined(far, far_y), X)
    near_far_x = swap(joined(near_far, near_far_y), X)
    early_places, late_places, fits = order(place, blocks, (len(EARLY), len(LATE)))
    pieces = [own, far, near, near_far, both_x, far_y, near_far_y, both_y, far_x]
    early = early_rows(early_places, pieces)
    return late_rows(late_places, early, [near_far_x]), fits


def add_by_swaps(value):
    for mask in (CORE, Y, X, NEAR_Z, FAR_Z):
        value = value + swap(value, mask)
    return value


def half_of(value, core):
    rows, members = value.shape
    return lax.dynamic_slice(value, (0, core * (members // 2)), (rows, members // 2))


def by_sum(add_up, other, place, ensemble, blocks, weights):
    rows = blocks.shape[1]
    codes = add_up(pick_all(place, blocks, weights, ensemble))
    codes = half_of(codes, (place[0] + other) % 2)
    return (codes[:rows] * UNIT).astype(BF16), codes[rows:].astype(jnp.int16)


def body(staged, ensemble, obs_blocks, obs_weights, comp_tags, obs_values, obs_noise):
    held = ensemble.shape[0] // obs_weights.shape[2]
    place = jnp.stack([lax.axis_index(AXES), held]).astype(jnp.int32)
    by_point = jnp.swapaxes(obs_weights, 1, 2)
    operands = (place, ensemble, obs_blocks, by_point)
    if staged:
        slotted, fits = by_slots(*operands)
        own = lax.cond(
            fits[0] == 1,
            lambda slotted, *operands: tuple(slotted),
            lambda slotted, *operands: by_sum(add_by_swaps, 0, *operands),
            slotted,
            *operands,
        )
        pairs = [(half, swap(half, CORE)) for half in own]
    else:
        add_up = lambda value: lax.psum(value, AXES)
        pairs = list(zip(by_sum(add_up, 0, *operands), by_sum(add_up, 1, *operands)))
    return batches(place, comp_tags, obs_values, obs_noise, ensemble, *pairs)


def solution(mesh):
    staged = (mesh.shape["row"], mesh.shape["col"]) == (8, 4)
    in_specs = (P(AXES, None), P(), P(), P(), P(), P())
    out_specs = P(AXES, None)
    return jax.shard_map(
        functools.partial(body, staged),
        mesh=mesh,
        in_specs=in_specs,
        out_specs=out_specs,
        check_vma=False,
    )
```

```python
import functools

import jax
import jax.numpy as jnp
from jax import lax
from jax.experimental import pallas as pl
from jax.experimental.pallas import tpu as pltpu
from jax.sharding import PartitionSpec as P

SLOTS = 56
UNIT = 1.0 / 1024
SCALE = 0.6
RESCALE = 1.25
TOLERANCE = 0.25
BF16 = jnp.bfloat16
F32 = jnp.float32
VMEM = pl.BlockSpec(memory_space=pltpu.VMEM)
SMEM = pl.BlockSpec(memory_space=pltpu.SMEM)
ANYWHERE = pl.BlockSpec(memory_space=pl.ANY)
PARAMS = pltpu.CompilerParams(vmem_limit_bytes=40 * 1024 * 1024)


def nt(a, b):
    return lax.dot_general(a, b, (((1,), (1,)), ((), ())), preferred_element_type=F32)


def nn(a, b):
    return lax.dot_general(a, b, (((1,), (0,)), ((), ())), preferred_element_type=F32)


def split(a):
    high = a.astype(BF16)
    return high, (a - high.astype(F32)).astype(BF16)


def dot2(dot, a, b):
    rows = a[0].shape[0]
    both = dot(jnp.concatenate(a, axis=0), b)
    return both[:rows] + both[rows:]


def dot3(dot, a, b):
    return dot2(dot, a, b[0]) + dot(a[0], b[1])


def row_mean(a):
    return jnp.sum(a, axis=1, keepdims=True) * (1.0 / a.shape[1])


def column(row):
    size = row.shape[1]
    lane = lax.broadcasted_iota(jnp.int32, (size, size), 1)
    sub = lax.broadcasted_iota(jnp.int32, (size, size), 0)
    return jnp.sum(jnp.where(lane == sub, row, jnp.zeros_like(row)), axis=1, keepdims=True)


def both_ways(row):
    as_float = row.astype(F32)
    return as_float, column(as_float)


def select(lanes, points, local, weight):
    value = jnp.zeros(lanes.shape, F32)
    for point in range(points):
        value = jnp.where(lanes % points == point, weight[point], value)
    return jnp.where((lanes // points).astype(F32) == local, value, 0.0)


def rounded(value):
    return value.astype(BF16).astype(F32)


def pick_kernel(place, blocks, weights, state_ref, keep, send, state, arrived):
    load = pltpu.make_async_copy(state_ref, state, arrived)
    load.start()
    device = place[0]
    batches, points, size = weights.shape
    width, members = state.shape
    held = width // points
    lane = lax.broadcasted_iota(jnp.int32, (size, size), 1)
    sub = lax.broadcasted_iota(jnp.int32, (size, size), 0)
    earlier = jnp.where(sub < lane, 1.0, 0.0).astype(BF16)
    row = blocks[...]
    mine = jnp.where(row // (2 * held) == device // 2, 1.0, 0.0)
    rank = nn(mine.astype(BF16), earlier).astype(jnp.int32)
    own = row // held == device
    slots = lax.broadcasted_iota(jnp.int32, (SLOTS, size), 0)
    points_of = lax.broadcasted_iota(jnp.int32, (width, size), 0)
    chosen, selector = [], []
    for batch in range(batches):
        place_of = rank[batch : batch + 1, :]
        place_of = place_of if batch == 0 else SLOTS - 1 - place_of
        place_of = jnp.where(own[batch : batch + 1, :], place_of, -1)
        chosen.append(jnp.where(slots == place_of, 1.0, 0.0))
        value = jnp.zeros((width, size), F32)
        for point in range(points):
            weight = weights[batch, point : point + 1, :]
            value = jnp.where(points_of % points == point, weight, value)
        local = row[batch : batch + 1, :] - device * held
        selector.append(jnp.where(points_of // points == local, value, 0.0))
    chosen = jnp.concatenate(chosen, axis=1).astype(BF16)
    parts = [nt(chosen, part).astype(BF16) for part in split(jnp.concatenate(selector, axis=1))]
    load.wait()
    rows = dot3(nn, parts, split(state[...]))
    from_first = lax.broadcasted_iota(jnp.int32, (SLOTS, 1), 0).astype(F32)
    from_first = from_first < jnp.sum(mine[:1, :], axis=1, keepdims=True)
    rows = jnp.where(from_first, rounded(rows), rows)
    code = jnp.round(rows * (1.0 / UNIT)).astype(jnp.int32)
    left, right = code[:, : members // 2], code[:, members // 2 :]
    first = device % 2 == 0
    keep[...] = jnp.where(first, left, right).astype(jnp.int16)
    send[...] = jnp.where(first, right, left).astype(jnp.int16)


def pick(place, blocks, weights, state):
    return pl.pallas_call(
        pick_kernel,
        out_shape=[jax.ShapeDtypeStruct((SLOTS, state.shape[1] // 2), jnp.int16)] * 2,
        in_specs=[SMEM, VMEM, VMEM, ANYWHERE],
        out_specs=[VMEM] * 2,
        scratch_shapes=[pltpu.VMEM(state.shape, F32), pltpu.SemaphoreType.DMA],
        compiler_params=PARAMS,
        name="pick",
    )(place, blocks, weights, state)


def pick_all_kernel(place, blocks, weights, state, out):
    device = place[0]
    batches, points, size = weights.shape
    width = state.shape[0]
    lanes = lax.broadcasted_iota(jnp.int32, (size, width), 1)
    for batch in range(batches):
        columns = [column(weights[batch, point : point + 1, :]) for point in range(points)]
        local = column((blocks[batch : batch + 1, :] - device * (width // points)).astype(F32))
        rows = jnp.dot(
            select(lanes, points, local, columns),
            state[...],
            precision=lax.Precision.HIGHEST,
            preferred_element_type=F32,
        )
        rows = rounded(rows) if batch == 0 else rows
        out[batch * size : (batch + 1) * size, :] = jnp.round(rows * (1.0 / UNIT))


def pick_all(place, blocks, weights, state):
    return pl.pallas_call(
        pick_all_kernel,
        out_shape=jax.ShapeDtypeStruct((blocks.size, state.shape[1]), F32),
        in_specs=[SMEM, VMEM, VMEM, VMEM],
        out_specs=VMEM,
        compiler_params=PARAMS,
        name="pick_all",
    )(place, blocks, weights, state)


def order_kernel(groups, place, blocks, *outs):
    outs, fits = outs[:-1], outs[-1]
    device, held = place[0], place[1]
    size = blocks.shape[1]
    lane = lax.broadcasted_iota(jnp.int32, (size, size), 1)
    sub = lax.broadcasted_iota(jnp.int32, (size, size), 0)
    for batch in range(blocks.shape[0]):
        pair_row, pair_column = both_ways(blocks[batch : batch + 1, :] // (2 * held))
        before = jnp.where((pair_row == pair_column) & (lane < sub), 1.0, 0.0)
        rank = jnp.sum(before, axis=1, keepdims=True).astype(jnp.int32)
        away = (2 * pair_column.astype(jnp.int32)) ^ device
        distance = 8 * ((away >> 3) & 1) + 4 * ((away >> 4) & 1) + ((away >> 1) & 3)
        slot = rank if batch == 0 else SLOTS - 1 - rank
        slot = slot + SLOTS * distance
        begin = 0
        for width, out in zip(groups, outs):
            slots = lax.broadcasted_iota(jnp.int32, (size, SLOTS * width), 1) + SLOTS * begin
            chosen = jnp.where(slots == slot, 1.0, 0.0)
            out[batch * size : (batch + 1) * size, :] = chosen.astype(BF16)
            begin += width
    counts = jnp.zeros((16, 1), F32)
    for batch in range(blocks.shape[0]):
        chip = blocks[batch : batch + 1, :] // (2 * held)
        chips = lax.broadcasted_iota(jnp.int32, (16, size), 0)
        counts = counts + jnp.sum(jnp.where(chips == chip, 1.0, 0.0), axis=1, keepdims=True)
    fits[0] = (jnp.max(counts) <= SLOTS).astype(jnp.int32)


def order(place, blocks, groups):
    return pl.pallas_call(
        functools.partial(order_kernel, groups),
        out_shape=[
            jax.ShapeDtypeStruct((blocks.size, SLOTS * width), BF16) for width in groups
        ]
        + [jax.ShapeDtypeStruct((1,), jnp.int32)],
        in_specs=[SMEM, VMEM],
        out_specs=[VMEM] * len(groups) + [SMEM],
        compiler_params=PARAMS,
        cost_estimate=pl.CostEstimate(flops=10**6, bytes_accessed=10**6, transcendentals=0),
        name="order",
    )(place, blocks)


def put_in_order(chosen, numbers, pieces):
    size = chosen.shape[0] // 2
    blocks = [(ref, index) for ref in pieces for index in range(ref.shape[0])]
    blocks = [blocks[where] for where in sorted(range(len(blocks)), key=lambda i: numbers[i])]
    values = [ref[index].astype(jnp.int32) for ref, index in blocks]
    high, low = split(jnp.concatenate(values, axis=0).astype(F32))
    second = chosen[size:, :]
    return nn(chosen[:size, :], high), nn(second, high) + nn(second, low)


def early_kernel(chosen, *refs):
    size = chosen.shape[0] // 2
    refs[-1][:size, :], refs[-1][size:, :] = put_in_order(chosen, EARLY, refs[:-1])


def late_kernel(chosen, early, *refs):
    size = chosen.shape[0] // 2
    first, second = put_in_order(chosen, LATE, refs[:-2])
    refs[-2][...] = ((first + early[:size, :]) * UNIT).astype(BF16)
    refs[-1][...] = (second + early[size:, :]).astype(jnp.int32).astype(jnp.int16)


def early_rows(chosen, pieces):
    return pl.pallas_call(
        early_kernel,
        out_shape=jax.ShapeDtypeStruct((chosen.shape[0], pieces[0].shape[-1]), F32),
        in_specs=[VMEM] * (1 + len(pieces)),
        out_specs=VMEM,
        compiler_params=PARAMS,
        cost_estimate=pl.CostEstimate(flops=10**9, bytes_accessed=4 * 10**6, transcendentals=0),
        name="early_rows",
    )(chosen, *pieces)


def late_rows(chosen, early, pieces):
    shape = (early.shape[0] // 2, early.shape[1])
    return pl.pallas_call(
        late_kernel,
        out_shape=[jax.ShapeDtypeStruct(shape, BF16), jax.ShapeDtypeStruct(shape, jnp.int16)],
        in_specs=[VMEM] * (2 + len(pieces)),
        out_specs=[VMEM] * 2,
        compiler_params=PARAMS,
        name="late_rows",
    )(chosen, early, *pieces)


def eliminate(covariance, work, inverse):
    size = covariance.shape[0]
    lane = lax.broadcasted_iota(jnp.int32, (size, size), 1)
    sub = lax.broadcasted_iota(jnp.int32, (size, size), 0)
    work[...] = covariance
    inverse[...] = jnp.where(lane == sub, 1.0, 0.0)

    def step(k, carry):
        row = work[pl.ds(k, 1), :]
        current = work[...]
        pivot = jnp.sum(jnp.where(lane[:1] == k, row, 0.0), axis=1, keepdims=True)
        column = jnp.sum(jnp.where(lane == k, current, 0.0), axis=1, keepdims=True)
        factor = jnp.where(sub[:, :1] > k, column / pivot, 0.0)
        inverse_row = inverse[pl.ds(k, 1), :]
        work[...] = current - factor * row
        inverse[...] = inverse[...] - factor * inverse_row
        return carry

    lax.fori_loop(0, size, step, 0)
    pivots = jnp.sum(jnp.where(lane == sub, work[...], 0.0), axis=1, keepdims=True)
    inverse[...] = inverse[...] * (1.0 / jnp.sqrt(pivots))


def squared(a):
    return jnp.sum(a * a)


def newton(scaled):
    size = scaled.shape[0]
    lane = lax.broadcasted_iota(jnp.int32, (size, size), 1)
    sub = lax.broadcasted_iota(jnp.int32, (size, size), 0)
    eye = jnp.where(lane == sub, 1.0, 0.0)
    half = jnp.where(lane < sub, 1.0, jnp.where(lane == sub, 0.5, 0.0))

    def third_order(error):
        low = error * half
        lowb = low.astype(BF16)
        return (nn(lowb, lowb) + half * nt(lowb, lowb)) - low

    def begin():
        first = (third_order(scaled - eye) + eye) * (RESCALE**0.5)
        fb = first.astype(BF16)
        error = nt(nn(fb, scaled.astype(BF16)).astype(BF16), fb) - eye
        return nn((third_order(error) + eye).astype(BF16), fb)

    def step(t):
        ts = split(t)
        error = dot3(nt, split(dot3(nn, ts, split(scaled))), ts) - eye
        return t + nn(third_order(error).astype(BF16), ts[0]), squared(error)

    return begin, step


def inverse_factor(covariance, work, inverse, use):
    size = covariance.shape[0]
    lane = lax.broadcasted_iota(jnp.int32, (size, size), 1)
    sub = lax.broadcasted_iota(jnp.int32, (size, size), 0)
    on_diagonal = jnp.where(lane == sub, covariance, 0.0)
    scale_row = lax.rsqrt(jnp.sum(on_diagonal, axis=0, keepdims=True) * (1.0 / SCALE))
    scale_column = lax.rsqrt(jnp.sum(on_diagonal, axis=1, keepdims=True) * (1.0 / SCALE))
    scaled = covariance * scale_row * scale_column
    begin, step = newton(scaled)
    t, residual = step(begin())
    use(t * scale_row)

    @pl.when(jnp.logical_not(residual <= TOLERANCE**2))
    def _():
        inverse[...] = t

        def again(carry):
            better, left = step(inverse[...])
            inverse[...] = better
            return carry[0] + 1, left

        def wanted(carry):
            return (carry[0] < 6) & jnp.logical_not(carry[1] <= (0.2 * TOLERANCE) ** 2)

        _, left = lax.while_loop(wanted, again, (0, residual))
        inverse[...] = inverse[...] * scale_row

        @pl.when(jnp.logical_not(left <= (0.2 * TOLERANCE) ** 2))
        def _():
            eliminate(covariance, work, inverse)

        use(inverse[...])


def whiten(observed, tags, values, load, noise_ref, work, inverse, store):
    members = observed.shape[1]
    size = observed.shape[0]
    mean = row_mean(observed)
    lane = lax.broadcasted_iota(jnp.int32, (size, size), 1)
    sub = lax.broadcasted_iota(jnp.int32, (size, size), 0)
    variance_row = jnp.where(tags == 0, 0.5, 2.0)
    mean_row = jnp.sum(jnp.where(lane == sub, mean, 0.0), axis=0, keepdims=True)
    exact = observed.astype(BF16)
    covariance = (nt(exact, exact) - mean * (mean_row * members)) * (1.0 / (members - 1))
    covariance = covariance + jnp.where(lane == sub, variance_row, 0.0)

    def finish(t):
        applied = dot2(nn, split(t), exact)
        noise = dot2(nn, split(t * jnp.sqrt(variance_row)), noise_ref[...])
        mean_part = jnp.sum(t * mean_row, axis=1, keepdims=True)
        value_part = jnp.sum(t * values, axis=1, keepdims=True)
        store((applied - mean_part).astype(BF16), (noise + value_part - applied).astype(BF16))

    load.wait()
    inverse_factor(covariance, work, inverse, finish)


def row_sums(array):
    return nt(jnp.ones((8, array.shape[1]), BF16), array)[:1, :]


def update(state, whitened, white_innov):
    members = state.shape[1]
    projected = dot2(nt, split(state), whitened) - row_mean(state) * row_sums(whitened)
    return state + dot2(nn, split(projected), white_innov) * (1.0 / (members - 1))


def both_halves(place, own, other):
    own, other = own[...].astype(F32), other[...].astype(F32)
    first = place[0] % 2 == 0
    return jnp.concatenate(
        [jnp.where(first, own, other), jnp.where(first, other, own)], axis=1
    )


def first_kernel(
    place, tags, values, noise_ref, own, other, whitened, white_innov, noise, loads, work, inverse
):
    load = pltpu.make_async_copy(noise_ref.at[0], noise, loads.at[0])
    load.start()
    observed = both_halves(place, own, other)

    def store(w, v):
        whitened[...] = w
        white_innov[...] = v

    whiten(observed, tags[:1, :], values[:1, :], load, noise, work, inverse, store)


def second_kernel(
    place,
    tags,
    values,
    noise_ref,
    own,
    other,
    whitened,
    white_innov,
    state_ref,
    analysis,
    noise,
    loads,
    work,
    inverse,
    state,
):
    load = pltpu.make_async_copy(noise_ref.at[1], noise, loads.at[0])
    load_state = pltpu.make_async_copy(state_ref, state, loads.at[1])
    load_state.start()
    load.start()
    w, v = whitened[...], white_innov[...]
    observed = rounded(update(both_halves(place, own, other), w, v) * UNIT)
    load_state.wait()
    first = update(state[...], w, v)

    def store(w, v):
        analysis[...] = update(first, w, v)

    whiten(observed, tags[1:2, :], values[1:2, :], load, noise, work, inverse, store)


def batch_call(kernel, name, outs, place, tags, values, noise, *arrays, state=()):
    rows, members = noise.shape[1:]
    return pl.pallas_call(
        kernel,
        out_shape=outs,
        in_specs=[SMEM, VMEM, VMEM, ANYWHERE] + [VMEM] * len(arrays) + [ANYWHERE] * len(state),
        out_specs=[VMEM] * len(outs),
        scratch_shapes=[
            pltpu.VMEM((rows, members), BF16),
            pltpu.SemaphoreType.DMA((2,)),
            pltpu.VMEM((rows, rows), F32),
            pltpu.VMEM((rows, rows), F32),
        ]
        + [pltpu.VMEM(array.shape, F32) for array in state],
        compiler_params=PARAMS,
        name=name,
    )(place, tags, values, noise, *arrays, *state)


def batches(place, tags, values, noise, state, observed, prior):
    shape = jax.ShapeDtypeStruct(noise.shape[1:], BF16)
    shared = (place, tags, values, noise)
    white = batch_call(first_kernel, "first_batch", [shape, shape], *shared, *observed)
    analysis = jax.ShapeDtypeStruct(state.shape, F32)
    return batch_call(
        second_kernel, "second_batch", [analysis], *shared, *prior, *white, state=(state,)
    )[0]


AXES = ("row", "col")
CORE, Y, X, NEAR_Z, FAR_Z = 1, 2, 4, 8, 16


def swap(value, mask):
    return lax.ppermute(value, AXES, [(i, i ^ mask) for i in range(32)])


def after(value, other):
    return lax.optimization_barrier((value, other))[0]


def joined(first, second):
    return jnp.concatenate([first, second], axis=0)


EARLY = (0, 4, 8, 12, 2, 10, 5, 13, 1, 9, 3, 11, 6, 7)
LATE = (14, 15)


def by_slots(place, ensemble, blocks, weights):
    keep, send = pick(place, blocks, weights, ensemble)
    own = (keep + swap(send, CORE))[None]
    far, near = swap(own, FAR_Z), swap(own, NEAR_Z)
    near_far = swap(far, NEAR_Z)
    both = joined(own, near)
    both_x = swap(both, X)
    far_y = swap(after(far, near), Y)
    near_far_y = swap(near_far, Y)
    both_y = swap(after(joined(both, both_x), near_far), Y)
    far_x = swap(joined(far, far_y), X)
    near_far_x = swap(joined(near_far, near_far_y), X)
    early_places, late_places, fits = order(place, blocks, (len(EARLY), len(LATE)))
    pieces = [own, far, near, near_far, both_x, far_y, near_far_y, both_y, far_x]
    early = early_rows(early_places, pieces)
    return late_rows(late_places, early, [near_far_x]), after(fits, early)


def add_by_swaps(value):
    for mask in (CORE, Y, X, NEAR_Z, FAR_Z):
        value = value + swap(value, mask)
    return value


def half_of(value, core):
    rows, members = value.shape
    return lax.dynamic_slice(value, (0, core * (members // 2)), (rows, members // 2))


def by_sum(add_up, other, place, ensemble, blocks, weights):
    rows = blocks.shape[1]
    codes = add_up(pick_all(place, blocks, weights, ensemble))
    codes = half_of(codes, (place[0] + other) % 2)
    return (codes[:rows] * UNIT).astype(BF16), codes[rows:].astype(jnp.int16)


def body(staged, ensemble, obs_blocks, obs_weights, comp_tags, obs_values, obs_noise):
    held = ensemble.shape[0] // obs_weights.shape[2]
    place = jnp.stack([lax.axis_index(AXES), held]).astype(jnp.int32)
    by_point = jnp.swapaxes(obs_weights, 1, 2)
    operands = (place, ensemble, obs_blocks, by_point)
    if staged:
        slotted, fits = by_slots(*operands)
        own = lax.cond(
            fits[0] == 1,
            lambda slotted, *operands: tuple(slotted),
            lambda slotted, *operands: by_sum(add_by_swaps, 0, *operands),
            slotted,
            *operands,
        )
        pairs = [(half, swap(half, CORE)) for half in own]
    else:
        add_up = lambda value: lax.psum(value, AXES)
        pairs = list(zip(by_sum(add_up, 0, *operands), by_sum(add_up, 1, *operands)))
    return batches(place, comp_tags, obs_values, obs_noise, ensemble, *pairs)


def solution(mesh):
    staged = (mesh.shape["row"], mesh.shape["col"]) == (8, 4)
    in_specs = (P(AXES, None), P(), P(), P(), P(), P())
    out_specs = P(AXES, None)
    return jax.shard_map(
        functools.partial(body, staged),
        mesh=mesh,
        in_specs=in_specs,
        out_specs=out_specs,
        check_vma=False,
    )
```
